32 devices in a mesh: row: 8 (over z, y), col: 4 (over x, core).
Axes of the slice: x: 2, y: 2, z: 4, core: 2. Of those that a mesh axis runs over, the one named last changes fastest.
Arguments:
- embeddings: bfloat16 [65536, 1024], P('row', 'col'), may hold values from -0.1875 to 0.1875
- quality: float32 [65536], P('row'), may hold values from 0.5 to 2
- probes: float32 [32, 65536], P(None, 'row'), may hold values from -6 to 6
- neighbors: int32 [512, 8], P('row'), may hold values from 0 to 511, as said below
Outputs:
- first: float32 [32, 65536], P(None, 'row')
- second: float32 [32, 65536], P(None, 'row')
The draws below stay inside these ranges and needn't reach their ends.
Inputs may be any that keep to these rules, and one draw needn't show every extreme that they name: `neighbors`: block b is held by row index b // 64. Among the 512 entries of one row index's blocks, at most 32 name blocks of any one other row index, and on every row index some other index is named exactly 32 times; the remaining entries name the index's own blocks.
All inputs are finite; a program needn't handle non-finite values.
Results may differ from the reference program's by a relative error of at most 0.02.
Values may be sent and summed in bfloat16 or wider, within the bound.
No kernel may reach another device: no remote copies, remote signals or barrier semaphores. Data moves between devices by JAX's collectives and lax.ppermute only.
A program may use at most 64 MiB of HBM per device.

```python
import math
import jax
import jax.numpy as jnp
from jax import lax

EMB = 1024
BS = 128
PROBES = 32
KN = 8
BLK_DEV = 64
NBLK = 512
NDOC = 65536
CAP = 32
N_ROW = 8
N_COL = 4


def draw_neighbors(key, part):
    entries = BLK_DEV * KN
    key_count, key_force, key_perm, key_local = jax.random.split(jax.random.fold_in(key, 17), 4)
    counts = jax.random.randint(key_count, (N_ROW, N_ROW), CAP // 4, CAP + 1)
    offsets = jnp.arange(N_ROW, dtype=jnp.int32)
    forced = jax.random.randint(key_force, (N_ROW,), 1, N_ROW)
    counts = jnp.where(offsets[None, :] == forced[:, None], CAP, counts)
    counts = jnp.where(offsets[None, :] == 0, 0, counts)
    bounds = jnp.cumsum(counts, axis=1)
    perm_keys = jax.random.split(key_perm, N_ROW)
    ranks = jax.vmap(lambda one_key: jax.random.permutation(one_key, entries))(perm_keys).astype(jnp.int32)
    offset = jnp.sum((ranks[:, :, None] >= bounds[:, None, :]).astype(jnp.int32), axis=2)
    offset = jnp.where(offset >= N_ROW, 0, offset)
    owner = (offsets[:, None] + offset) % N_ROW
    local = jax.random.randint(key_local, (N_ROW, entries), 0, BLK_DEV)
    return (owner * BLK_DEV + local).astype(jnp.int32).reshape(NBLK, KN)


def shard_levels(stream_key, extent, shards, least, top_value):
    def one(dim, parts):
        steps = jax.random.uniform(jax.random.fold_in(jax.random.fold_in(stream_key, 6), dim), (parts,), jnp.float32, least / len(shards), top_value / len(shards))
        return jnp.repeat(jnp.exp(steps), extent[dim] // parts).reshape((-1,) + (1,) * (len(extent) - dim - 1))

    gain = one(*shards[0])
    for cut in shards[1:]:
        gain = gain * one(*cut)
    return gain


def gaussian(stream_key, extent, spread, most, cuts=(), kind=jnp.bfloat16):
    gain = shard_levels(stream_key, extent, cuts, -0.22, 0.18) if cuts else 1.0
    drawn = jax.random.normal(stream_key, extent, jnp.float32) * spread * gain
    return jnp.minimum(jnp.maximum(drawn, -most), most).astype(kind)


def setup_inputs(seed: int = 0) -> dict:
    key_of = jax.random.split(jax.random.key(seed), 5)
    embeddings = gaussian(key_of[0], (NDOC, EMB), EMB ** -0.5, 0.1875, ((0, 8), (1, 4)))
    quality = jnp.clip(jnp.exp(math.log(2.0) - 1.3862944 * jax.random.uniform(key_of[1], (NDOC,), jnp.float32) ** shard_levels(key_of[1], (NDOC,), ((0, 8),), -0.2, 0.2)), 0.5, 2.0)
    probes = gaussian(key_of[2], (PROBES, NDOC), 1.0, 6.0, ((1, 8),), jnp.float32)
    neighbors = draw_neighbors(jax.random.fold_in(key_of[4], 71), 0)
    return dict(embeddings=embeddings, quality=quality, probes=probes, neighbors=neighbors)


def reference(embeddings, quality, probes, neighbors):
    width = EMB // N_COL
    blocks = embeddings.reshape(N_ROW, BLK_DEV, BS, N_COL, width)
    lists = neighbors.reshape(N_ROW, BLK_DEV, KN)

    def block_sums(vec):
        scaled = (vec * quality[None, :]).astype(jnp.bfloat16).reshape(PROBES, N_ROW, BLK_DEV, BS)
        scaled = jnp.moveaxis(scaled, 1, 0)

        def one_shard(pair):
            emb, weights = pair
            return jnp.einsum("bdsc,pbd->bscp", emb.astype(jnp.float32), weights.astype(jnp.float32)).astype(jnp.bfloat16)

        return lax.map(one_shard, (blocks, scaled)).reshape(NBLK, N_COL, width, PROBES)

    def apply(vec):
        sums = block_sums(vec)

        def one_shard(pair):
            emb, ids = pair
            gathered = jnp.sum(sums[ids].astype(jnp.float32), axis=1).astype(jnp.bfloat16)
            partial_value = jnp.einsum("bdsc,bscp->spbd", emb.astype(jnp.float32), gathered.astype(jnp.float32)).astype(jnp.bfloat16)
            return jnp.sum(partial_value.astype(jnp.float32), axis=0).reshape(PROBES, BLK_DEV * BS)

        total = lax.map(one_shard, (blocks, lists))
        total = jnp.moveaxis(total, 0, 1).reshape(PROBES, NDOC)
        return total * quality[None, :] - vec

    first = apply(probes)
    second = 2.0 * apply(first) - probes
    return first, second
```

```python
import functools

import jax
import jax.numpy as jnp
from jax import lax
from jax.experimental import pallas as pl
from jax.experimental.pallas import tpu as pltpu
from jax.sharding import PartitionSpec as P

CHUNKS = 2
TILE_BLOCKS = 8
VMEM_LIMIT = 32 * 1024 * 1024


def params(**kw):
    return pltpu.CompilerParams(vmem_limit_bytes=VMEM_LIMIT, **kw)


def cost(flops, nbytes):
    return pl.CostEstimate(flops=int(flops), bytes_accessed=int(nbytes), transcendentals=0)


def swap(value, axis, size, mask):
    return lax.ppermute(value, axis, [(i, i ^ mask) for i in range(size)])


def project(block_len, scaled, emb_ref, sums_ref):
    for b in range(sums_ref.shape[0]):
        docs = slice(b * block_len, (b + 1) * block_len)
        sums_ref[b] = jnp.dot(
            scaled[:, docs], emb_ref[docs, :], preferred_element_type=jnp.float32
        ).astype(jnp.bfloat16)


def first_sums_kernel(block_len, vec_ref, quality_ref, emb_ref, sums_ref):
    scaled = (vec_ref[...] * quality_ref[...]).astype(jnp.bfloat16)
    project(block_len, scaled, emb_ref, sums_ref)


def next_sums_kernel(block_len, mine_ref, other_ref, vec_ref, quality_ref, emb_ref, out_ref, sums_ref):
    total = mine_ref[...].astype(jnp.float32) + other_ref[...].astype(jnp.float32)
    quality = quality_ref[...]
    out = total * quality - vec_ref[...]
    out_ref[...] = out
    project(block_len, (out * quality).astype(jnp.bfloat16), emb_ref, sums_ref)


def combine_kernel(ids_ref, *refs):
    *shards, out_ref, table, sems = refs
    blocks = shards[0].shape[0]
    copies = [
        pltpu.make_async_copy(ref, table.at[pl.ds(i * blocks, blocks)], sems.at[i])
        for i, ref in enumerate(shards)
    ]
    for copy in copies:
        copy.start()
    table[len(shards) * blocks] = jnp.zeros(table.shape[1:], table.dtype)
    for copy in copies:
        copy.wait()
    entries = ids_ref.shape[0] // out_ref.shape[0]

    def step(b, carry):
        total = table[ids_ref[b * entries]].astype(jnp.float32)
        for k in range(1, entries):
            total = total + table[ids_ref[b * entries + k]].astype(jnp.float32)
        out_ref[b] = total.astype(out_ref.dtype)
        return carry

    lax.fori_loop(0, out_ref.shape[0], step, 0, unroll=4)


def expand_kernel(block_len, own_ref, arrived_ref, emb_ref, out_ref):
    for b in range(own_ref.shape[0]):
        docs = slice(b * block_len, (b + 1) * block_len)
        gathered = (own_ref[b] + arrived_ref[b].astype(jnp.float32)).astype(jnp.bfloat16)
        out_ref[:, docs] = lax.dot_general(
            gathered, emb_ref[docs, :], (((1,), (1,)), ((), ())),
            preferred_element_type=jnp.float32,
        ).astype(jnp.bfloat16)


def body(embeddings, quality, probes, neighbors):
    nrow, ncol = lax.axis_size("row"), lax.axis_size("col")
    me = lax.axis_index("row")
    blk_count, list_len = neighbors.shape
    docs, width = embeddings.shape
    block_len = docs // blk_count
    nprobe = probes.shape[0]
    part = nprobe // CHUNKS
    bits = nrow.bit_length() - 1
    gather_bits = [m for m in (2, 1) if m < nrow]
    near = sum(gather_bits)
    reduce_bits = [1 << i for i in reversed(range(bits)) if not (1 << i) & near]
    far = sum(reduce_bits)

    def table_ids(lists):
        flat = lists.reshape(-1)
        apart = (flat // blk_count) ^ me
        inside = (apart & far) == 0
        place = jnp.where(inside, apart & near, 0) * blk_count + flat % blk_count
        return jnp.where(inside, place, (near + 1) * blk_count)

    dests = [0]
    for m in reduce_bits:
        dests = dests + [d | m for d in dests]
    ids = {d: table_ids(neighbors if d == 0 else swap(neighbors, "row", nrow, d)) for d in dests}

    qrow = quality[None, :]
    tile_docs = TILE_BLOCKS * block_len
    steps = blk_count // TILE_BLOCKS
    shard_shape = (blk_count, part, width)
    shard_size = blk_count * part * width
    mac = 2 * part * docs * width
    emb_spec = pl.BlockSpec((tile_docs, width), lambda j: (j, 0))
    vec_spec = pl.BlockSpec((part, tile_docs), lambda j: (0, j))
    q_spec = pl.BlockSpec((1, tile_docs), lambda j: (0, j))
    shard_spec = pl.BlockSpec((TILE_BLOCKS, part, width), lambda j: (j, 0, 0))

    def chunk_spec(c):
        return pl.BlockSpec((part, tile_docs), lambda j: (c, j))

    def first_sums(c):
        return pl.pallas_call(
            functools.partial(first_sums_kernel, block_len),
            grid=(steps,),
            in_specs=[chunk_spec(c), q_spec, emb_spec],
            out_specs=shard_spec,
            out_shape=jax.ShapeDtypeStruct(shard_shape, jnp.bfloat16),
            compiler_params=params(),
            cost_estimate=cost(mac, 2 * docs * width + 4 * part * docs + 2 * shard_size),
        )(probes, qrow, embeddings)

    def next_sums(c, mine, other):
        return pl.pallas_call(
            functools.partial(next_sums_kernel, block_len),
            grid=(steps,),
            in_specs=[vec_spec, vec_spec, chunk_spec(c), q_spec, emb_spec],
            out_specs=[vec_spec, shard_spec],
            out_shape=[
                jax.ShapeDtypeStruct((part, docs), jnp.float32),
                jax.ShapeDtypeStruct(shard_shape, jnp.bfloat16),
            ],
            compiler_params=params(),
            cost_estimate=cost(mac, 2 * docs * width + 12 * part * docs + 2 * shard_size),
        )(mine, other, probes, qrow, embeddings)

    def combine(dest, shards, dtype):
        count = len(shards)
        return pl.pallas_call(
            combine_kernel,
            in_specs=[pl.BlockSpec(memory_space=pltpu.SMEM)] + [pl.BlockSpec(memory_space=pl.ANY)] * count,
            out_specs=pl.BlockSpec(memory_space=pltpu.VMEM),
            out_shape=jax.ShapeDtypeStruct(shard_shape, dtype),
            scratch_shapes=[
                pltpu.VMEM((count * blk_count + 1, part, width), jnp.bfloat16),
                pltpu.SemaphoreType.DMA((count,)),
            ],
            compiler_params=params(),
            cost_estimate=cost(list_len * shard_size, 2 * count * shard_size + 4 * shard_size),
        )(ids[dest], *shards)

    def expand(own, arrived):
        return pl.pallas_call(
            functools.partial(expand_kernel, block_len),
            grid=(steps,),
            in_specs=[shard_spec, shard_spec, emb_spec],
            out_specs=vec_spec,
            out_shape=jax.ShapeDtypeStruct((part, docs), jnp.bfloat16),
            compiler_params=params(),
            cost_estimate=cost(mac, 2 * docs * width + 2 * part * docs + 6 * shard_size),
        )(own, arrived, embeddings)

    def exchange(sums):
        shards = {0: sums}
        for m in gather_bits:
            shards.update({k | m: swap(v, "row", nrow, m) for k, v in list(shards.items())})
        shards = [shards[k] for k in sorted(shards)]
        outgoing = {d: combine(d, shards, jnp.bfloat16) for d in dests if d}
        own = combine(0, shards, jnp.float32)
        arrived = None
        for m in reduce_bits:
            taken = {d ^ m: swap(outgoing.pop(d), "row", nrow, m) for d in list(outgoing) if d & m}
            for d, value in taken.items():
                if d in outgoing:
                    outgoing[d] = (
                        outgoing[d].astype(jnp.float32) + value.astype(jnp.float32)
                    ).astype(jnp.bfloat16)
                else:
                    arrived = value if arrived is None else (
                        arrived.astype(jnp.float32) + value.astype(jnp.float32)
                    ).astype(jnp.bfloat16)
        return own, arrived

    def col_sum(value):
        masks = [1 << i for i in range(ncol.bit_length() - 1)]
        for m in masks[:-1]:
            other = swap(value, "col", ncol, m)
            value = (value.astype(jnp.float32) + other.astype(jnp.float32)).astype(jnp.bfloat16)
        return value, swap(value, "col", ncol, masks[-1])

    sums = [first_sums(c) for c in range(CHUNKS)]
    halves = [col_sum(expand(*exchange(s))) for s in sums]
    firsts, sums = zip(*[next_sums(c, *h) for c, h in enumerate(halves)])
    halves = [col_sum(expand(*exchange(s))) for s in sums]
    seconds = []
    for c, (mine, other) in enumerate(halves):
        total = mine.astype(jnp.float32) + other.astype(jnp.float32)
        seconds.append(2.0 * (total * qrow - firsts[c]) - probes[c * part:(c + 1) * part])
    return jnp.concatenate(firsts, axis=0), jnp.concatenate(seconds, axis=0)


def solution(mesh):
    placed = (P("row", "col"), P("row"), P(None, "row"), P("row", None))
    return jax.shard_map(
        body,
        mesh=mesh,
        in_specs=placed,
        out_specs=(P(None, "row"), P(None, "row")),
        check_vma=False,
    )
```

```python
import functools

import jax
import jax.numpy as jnp
from jax import lax
from jax.experimental import pallas as pl
from jax.experimental.pallas import tpu as pltpu
from jax.sharding import PartitionSpec as P

TILE_BLOCKS = 8
VMEM_LIMIT = 8 * 1024 * 1024
NEAR = 3


def params():
    return pltpu.CompilerParams(vmem_limit_bytes=VMEM_LIMIT)


def cost(flops, nbytes):
    return pl.CostEstimate(flops=int(flops), bytes_accessed=int(nbytes), transcendentals=0)


def swap(value, axis, size, mask):
    return lax.ppermute(value, axis, [(i, i ^ mask) for i in range(size)])


def add_bf16(a, b):
    return (a.astype(jnp.float32) + b.astype(jnp.float32)).astype(jnp.bfloat16)


def project(block_len, scaled, emb_ref, sums_refs):
    count = len(sums_refs)
    part = emb_ref.shape[1] // count
    for b in range(sums_refs[0].shape[0]):
        docs = slice(b * block_len, (b + 1) * block_len)
        sums = jnp.dot(
            scaled[:, docs], emb_ref[docs, :], preferred_element_type=jnp.float32
        ).astype(jnp.bfloat16)
        for i, ref in enumerate(sums_refs):
            ref[b] = sums[:, i * part:(i + 1) * part]


def first_sums_kernel(block_len, vec_ref, quality_ref, emb_ref, *sums_refs):
    scaled = (vec_ref[...] * quality_ref[...]).astype(jnp.bfloat16)
    project(block_len, scaled, emb_ref, sums_refs)


def next_sums_kernel(block_len, mine_ref, other_ref, vec_ref, quality_ref, emb_ref, out_ref, *sums_refs):
    total = mine_ref[...].astype(jnp.float32) + other_ref[...].astype(jnp.float32)
    quality = quality_ref[...]
    out = total * quality - vec_ref[...]
    out_ref[...] = out
    project(block_len, (out * quality).astype(jnp.bfloat16), emb_ref, sums_refs)


def finish_kernel(mine_ref, other_ref, first_ref, vec_ref, quality_ref, out_ref):
    total = mine_ref[...].astype(jnp.float32) + other_ref[...].astype(jnp.float32)
    out_ref[...] = 2.0 * (total * quality_ref[...] - first_ref[...]) - vec_ref[...]


def combine_kernel(ids_ref, *refs):
    *shards, out_ref, table, sems = refs
    blocks = shards[0].shape[0]
    copies = [
        pltpu.make_async_copy(ref, table.at[pl.ds(i * blocks, blocks)], sems.at[i])
        for i, ref in enumerate(shards)
    ]
    for copy in copies:
        copy.start()
    table[len(shards) * blocks] = jnp.zeros(table.shape[1:], table.dtype)
    for copy in copies:
        copy.wait()
    entries = ids_ref.shape[0] // out_ref.shape[0]

    def step(b, carry):
        total = table[ids_ref[b * entries]].astype(jnp.float32)
        for k in range(1, entries):
            total = total + table[ids_ref[b * entries + k]].astype(jnp.float32)
        out_ref[b] = total.astype(out_ref.dtype)
        return carry

    lax.fori_loop(0, out_ref.shape[0], step, 0, unroll=4)


def expand_kernel(block_len, counts, *refs):
    *refs, emb_ref, out_ref = refs
    for b in range(refs[0].shape[0]):
        docs = slice(b * block_len, (b + 1) * block_len)
        parts, at = [], 0
        for count in counts:
            total = refs[at][b]
            for ref in refs[at + 1:at + count]:
                total = total + ref[b].astype(jnp.float32)
            parts.append(total.astype(jnp.bfloat16))
            at += count
        out_ref[:, docs] = lax.dot_general(
            jnp.concatenate(parts, axis=1), emb_ref[docs, :], (((1,), (1,)), ((), ())),
            preferred_element_type=jnp.float32,
        ).astype(jnp.bfloat16)


def body(embeddings, quality, probes, neighbors):
    nrow, ncol = lax.axis_size("row"), lax.axis_size("col")
    me = lax.axis_index("row")
    blk_count, list_len = neighbors.shape
    docs, width = embeddings.shape
    block_len = docs // blk_count
    nprobe = probes.shape[0]
    bits = [1 << i for i in reversed(range(nrow.bit_length() - 1))]
    near = [m for m in bits if m & NEAR]
    far = [m for m in bits if not m & NEAR]
    plans = [(far, near[::-1]), (near, far)]
    nparts = len(plans)
    part = width // nparts

    dests = []
    for _, reduce_bits in plans:
        found = [0]
        for m in reversed(reduce_bits):
            found = [d | m for d in found] + found
        dests.append(found)
    lists = {d: swap(neighbors, "row", nrow, d) for found in dests for d in found if d}
    lists[0] = neighbors

    def table_ids(dest, gather_bits):
        flat = lists[dest].reshape(-1)
        apart = (flat // blk_count) ^ me
        inside = (apart & ~sum(gather_bits)) == 0
        slot = sum(((apart & m) != 0).astype(jnp.int32) << i for i, m in enumerate(gather_bits))
        return jnp.where(inside, slot * blk_count + flat % blk_count, blk_count << len(gather_bits))

    qrow = quality[None, :]
    tile_docs = TILE_BLOCKS * block_len
    steps = blk_count // TILE_BLOCKS
    shard_shape = (blk_count, nprobe, part)
    shard_size = blk_count * nprobe * part
    mac = 2 * nprobe * docs * width
    emb_spec = pl.BlockSpec((tile_docs, width), lambda j: (j, 0))
    vec_spec = pl.BlockSpec((nprobe, tile_docs), lambda j: (0, j))
    q_spec = pl.BlockSpec((1, tile_docs), lambda j: (0, j))
    shard_spec = pl.BlockSpec((TILE_BLOCKS, nprobe, part), lambda j: (j, 0, 0))
    shard_out = jax.ShapeDtypeStruct(shard_shape, jnp.bfloat16)
    vec_out = jax.ShapeDtypeStruct((nprobe, docs), jnp.float32)

    def first_sums(qrow):
        return pl.pallas_call(
            functools.partial(first_sums_kernel, block_len),
            grid=(steps,),
            in_specs=[vec_spec, q_spec, emb_spec],
            out_specs=[shard_spec] * nparts,
            out_shape=[shard_out] * nparts,
            compiler_params=params(),
            cost_estimate=cost(mac, 2 * docs * width + 4 * nprobe * docs + 4 * shard_size),
        )(probes, qrow, embeddings)

    def next_sums(mine, other):
        first, *sums = pl.pallas_call(
            functools.partial(next_sums_kernel, block_len),
            grid=(steps,),
            in_specs=[vec_spec, vec_spec, vec_spec, q_spec, emb_spec],
            out_specs=[vec_spec] + [shard_spec] * nparts,
            out_shape=[vec_out] + [shard_out] * nparts,
            compiler_params=params(),
            cost_estimate=cost(mac, 2 * docs * width + 12 * nprobe * docs + 4 * shard_size),
        )(mine, other, probes, qrow, embeddings)
        return first, sums

    def finish(mine, other, first):
        return pl.pallas_call(
            finish_kernel,
            grid=(steps // 2,),
            in_specs=[pl.BlockSpec((nprobe, 2 * tile_docs), lambda j: (0, j))] * 4
            + [pl.BlockSpec((1, 2 * tile_docs), lambda j: (0, j))],
            out_specs=pl.BlockSpec((nprobe, 2 * tile_docs), lambda j: (0, j)),
            out_shape=vec_out,
            compiler_params=params(),
            cost_estimate=cost(6 * nprobe * docs, 16 * nprobe * docs),
        )(mine, other, first, probes, qrow)

    def combine(ids, shards, dtype):
        count = len(shards)
        return pl.pallas_call(
            combine_kernel,
            in_specs=[pl.BlockSpec(memory_space=pltpu.SMEM)] + [pl.BlockSpec(memory_space=pl.ANY)] * count,
            out_specs=pl.BlockSpec(memory_space=pltpu.VMEM),
            out_shape=jax.ShapeDtypeStruct(shard_shape, dtype),
            scratch_shapes=[
                pltpu.VMEM((count * blk_count + 1, nprobe, part), jnp.bfloat16),
                pltpu.SemaphoreType.DMA((count,)),
            ],
            compiler_params=params(),
            cost_estimate=cost(list_len * shard_size, 2 * count * shard_size + 4 * shard_size),
        )(ids, *shards)

    def expand(groups):
        values = [v for group in groups for v in group]
        return pl.pallas_call(
            functools.partial(expand_kernel, block_len, [len(group) for group in groups]),
            grid=(steps,),
            in_specs=[shard_spec] * len(values) + [emb_spec],
            out_specs=vec_spec,
            out_shape=jax.ShapeDtypeStruct((nprobe, docs), jnp.bfloat16),
            compiler_params=params(),
            cost_estimate=cost(mac, 2 * docs * width + 2 * nprobe * docs + 6 * len(values) * shard_size // 2),
        )(*values, embeddings)

    ids = [{d: table_ids(d, gather_bits) for d in found} for found, (gather_bits, _) in zip(dests, plans)]

    def gather(sums, gather_bits):
        shards = [sums]
        for m in gather_bits:
            shards = shards + [swap(v, "row", nrow, m) for v in shards]
        return shards

    def reduce(outgoing, reduce_bits):
        arrived = []
        for m in reduce_bits:
            taken = {d ^ m: swap(outgoing.pop(d), "row", nrow, m) for d in list(outgoing) if d & m}
            for d, value in taken.items():
                if d:
                    outgoing[d] = add_bf16(outgoing[d], value)
                else:
                    arrived.append(value)
        return arrived

    def exchange(sums):
        shards = [gather(s, gather_bits) for s, (gather_bits, _) in zip(sums, plans)]
        order = [(i, found[k]) for k in range(nrow) for i, found in enumerate(dests) if k + 1 < len(found)]
        combined, last = [{} for _ in plans], None
        for i, d in order + [(i, 0) for i in range(nparts)]:
            picks = ids[i][d] if last is None else lax.optimization_barrier((ids[i][d], last))[0]
            last = combine(picks, shards[i], jnp.bfloat16 if d else jnp.float32)
            combined[i][d] = last
        own = [found.pop(0) for found in combined]
        return [[o] + reduce(c, reduce_bits) for o, c, (_, reduce_bits) in zip(own, combined, plans)]

    def col_sum(value):
        masks = [1 << i for i in range(ncol.bit_length() - 1)]
        for m in masks[:-1]:
            value = add_bf16(value, swap(value, "col", ncol, m))
        return value, swap(value, "col", ncol, masks[-1])

    halves = col_sum(expand(exchange(first_sums(lax.optimization_barrier((qrow, lists))[0]))))
    first, sums = next_sums(*halves)
    halves = col_sum(expand(exchange(sums)))
    return first, finish(*halves, first)


def solution(mesh):
    placed = (P("row", "col"), P("row"), P(None, "row"), P("row", None))
    return jax.shard_map(
        body,
        mesh=mesh,
        in_specs=placed,
        out_specs=(P(None, "row"), P(None, "row")),
        check_vma=False,
    )
```

```python
import functools

import jax
import jax.numpy as jnp
from jax import lax
from jax.experimental import pallas as pl
from jax.experimental.pallas import tpu as pltpu
from jax.sharding import PartitionSpec as P

GROUPS = 2
PARTS = 2
TILE_BLOCKS = 8
VMEM_LIMIT = 8 * 1024 * 1024
SIDE, NEXT = 1, 2

ORDER = (
    "As Bs Al Af1",
    "Af2 Ao1 Aw1 Ao2",
    "Az1 Aw2 Bf1 Bf2",
    "Ae Bo1 Bw1 Bo2",
    "Bw2 Bz1 As Be",
    "Af1 Af2 Ao1 Aw1",
    "Bs Ao2 Az1 Aw2",
    "Bf1 Bf2 Ae Bo1",
    "Bw1 Bo2 Bw2 Bz1",
    "Ar Be Br",
)


def params():
    return pltpu.CompilerParams(vmem_limit_bytes=VMEM_LIMIT)


def swap(value, axis, size, mask):
    return lax.ppermute(value, axis, [(i, i ^ mask) for i in range(size)])


def add_bf16(a, b):
    return (a.astype(jnp.float32) + b.astype(jnp.float32)).astype(jnp.bfloat16)


def tree_sum(values):
    values = [v.astype(jnp.float32) for v in values]
    while len(values) > 1:
        values = [values[i] + values[i + 1] for i in range(0, len(values), 2)]
    return values[0]


def project(block_len, scaled, emb_ref, sums_refs):
    count = len(sums_refs)
    part = emb_ref.shape[1] // count
    for b in range(sums_refs[0].shape[0]):
        docs = slice(b * block_len, (b + 1) * block_len)
        sums = jnp.dot(
            scaled[:, docs], emb_ref[docs, :], preferred_element_type=jnp.float32
        ).astype(jnp.bfloat16)
        for i, ref in enumerate(sums_refs):
            ref[b] = sums[:, i * part:(i + 1) * part]


def first_sums_kernel(block_len, vec_ref, quality_ref, emb_ref, *sums_refs):
    scaled = (vec_ref[...] * quality_ref[...]).astype(jnp.bfloat16)
    project(block_len, scaled, emb_ref, sums_refs)


def next_sums_kernel(block_len, nsum, *refs):
    vec_ref, quality_ref, emb_ref = refs[nsum:nsum + 3]
    out_ref, *sums_refs = refs[-1 - PARTS:]
    quality = quality_ref[...]
    out = tree_sum([ref[...] for ref in refs[:nsum]]) * quality - vec_ref[...]
    out_ref[...] = out
    project(block_len, (out * quality).astype(jnp.bfloat16), emb_ref, sums_refs)


def finish_kernel(nsum, *refs):
    first_ref, vec_ref, quality_ref = refs[nsum:nsum + 3]
    total = tree_sum([ref[...] for ref in refs[:nsum]])
    refs[-1][...] = 2.0 * (total * quality_ref[...] - first_ref[...]) - vec_ref[...]


def combine_kernel(ids_ref, *refs):
    *shards, out_ref, table, sems = refs
    blocks = shards[0].shape[0]
    copies = [
        pltpu.make_async_copy(ref, table.at[pl.ds(i * blocks, blocks)], sems.at[i])
        for i, ref in enumerate(shards)
    ]
    for copy in copies:
        copy.start()
    table[len(shards) * blocks] = jnp.zeros(table.shape[1:], table.dtype)
    for copy in copies:
        copy.wait()
    entries = ids_ref.shape[0] // out_ref.shape[0]

    def step(b, carry):
        total = table[ids_ref[b * entries]].astype(jnp.float32)
        for k in range(1, entries):
            total = total + table[ids_ref[b * entries + k]].astype(jnp.float32)
        out_ref[b] = total.astype(out_ref.dtype)
        return carry

    lax.fori_loop(0, out_ref.shape[0], step, 0, unroll=4)


def expand_kernel(block_len, counts, *refs):
    *refs, emb_ref, out_ref = refs
    for b in range(refs[0].shape[0]):
        docs = slice(b * block_len, (b + 1) * block_len)
        parts, at = [], 0
        for count in counts:
            total = refs[at][b]
            for ref in refs[at + 1:at + count]:
                total = total + ref[b].astype(jnp.float32)
            parts.append(total.astype(jnp.bfloat16))
            at += count
        out_ref[:, docs] = lax.dot_general(
            jnp.concatenate(parts, axis=1), emb_ref[docs, :], (((1,), (1,)), ((), ())),
            preferred_element_type=jnp.float32,
        ).astype(jnp.bfloat16)


def body(embeddings, quality, probes, neighbors):
    nrow, ncol = lax.axis_size("row"), lax.axis_size("col")
    me = lax.axis_index("row")
    blk_count, list_len = neighbors.shape
    docs, width = embeddings.shape
    block_len = docs // blk_count
    nprobe = probes.shape[0]
    group, part = nprobe // GROUPS, width // PARTS
    reduce_bits = [1 << i for i in reversed(range(nrow.bit_length() - 1)) if 1 << i not in (SIDE, NEXT)]
    dests = [0]
    for m in reversed(reduce_bits):
        dests = [d | m for d in dests] + dests
    shards = (0, NEXT, SIDE, NEXT | SIDE)

    def table_ids(lists):
        flat = lists.reshape(-1)
        apart = (flat // blk_count) ^ me
        place = flat % blk_count
        for i, shard in enumerate(shards):
            place = jnp.where(apart == shard, i * blk_count + flat % blk_count, place)
        return jnp.where((apart & ~(NEXT | SIDE)) == 0, place, len(shards) * blk_count)

    qrow = quality[None, :]
    tile_docs = TILE_BLOCKS * block_len
    steps = blk_count // TILE_BLOCKS
    shard_shape = (blk_count, group, part)
    nsum = ncol
    emb_spec = pl.BlockSpec((tile_docs, width), lambda j: (j, 0))
    vec_spec = pl.BlockSpec((group, tile_docs), lambda j: (0, j))
    q_spec = pl.BlockSpec((1, tile_docs), lambda j: (0, j))
    shard_spec = pl.BlockSpec((TILE_BLOCKS, group, part), lambda j: (j, 0, 0))
    any_spec = pl.BlockSpec(memory_space=pl.ANY)
    shard_out = jax.ShapeDtypeStruct(shard_shape, jnp.bfloat16)
    vec_out = jax.ShapeDtypeStruct((nprobe, docs), jnp.float32)

    def group_spec(c):
        return pl.BlockSpec((group, tile_docs), lambda j: (c, j))

    def first_sums(c, qrow):
        return pl.pallas_call(
            functools.partial(first_sums_kernel, block_len),
            grid=(steps,),
            in_specs=[group_spec(c), q_spec, emb_spec],
            out_specs=[shard_spec] * PARTS,
            out_shape=[shard_out] * PARTS,
            compiler_params=params(),
        )(probes, qrow, embeddings)

    def next_sums(c, first, values):
        held = [] if first is None else [first]
        first, *sums = pl.pallas_call(
            functools.partial(next_sums_kernel, block_len, nsum),
            grid=(steps,),
            in_specs=[vec_spec] * nsum + [group_spec(c), q_spec, emb_spec] + [any_spec] * len(held),
            out_specs=[group_spec(c)] + [shard_spec] * PARTS,
            out_shape=[vec_out] + [shard_out] * PARTS,
            input_output_aliases={nsum + 3: 0} if held else {},
            compiler_params=params(),
        )(*values, probes, qrow, embeddings, *held)
        return first, sums

    def finish(c, first, second, values):
        held = [] if second is None else [second]
        wide = pl.BlockSpec((group, 2 * tile_docs), lambda j: (0, j))
        here = pl.BlockSpec((group, 2 * tile_docs), lambda j: (c, j))
        wide_q = pl.BlockSpec((1, 2 * tile_docs), lambda j: (0, j))
        return pl.pallas_call(
            functools.partial(finish_kernel, nsum),
            grid=(steps // 2,),
            in_specs=[wide] * nsum + [here, here, wide_q] + [any_spec] * len(held),
            out_specs=here,
            out_shape=vec_out,
            input_output_aliases={nsum + 3: 0} if held else {},
            compiler_params=params(),
        )(*values, first, probes, qrow, *held)

    def combine(ids, shards, dtype):
        count = len(shards)
        return pl.pallas_call(
            combine_kernel,
            in_specs=[pl.BlockSpec(memory_space=pltpu.SMEM)] + [any_spec] * count,
            out_specs=pl.BlockSpec(memory_space=pltpu.VMEM),
            out_shape=jax.ShapeDtypeStruct(shard_shape, dtype),
            scratch_shapes=[
                pltpu.VMEM((count * blk_count + 1, group, part), jnp.bfloat16),
                pltpu.SemaphoreType.DMA((count,)),
            ],
            compiler_params=params(),
        )(ids, *shards)

    def expand(parts):
        values = [v for values in parts for v in values]
        return pl.pallas_call(
            functools.partial(expand_kernel, block_len, [len(values) for values in parts]),
            grid=(steps,),
            in_specs=[shard_spec] * len(values) + [emb_spec],
            out_specs=vec_spec,
            out_shape=jax.ShapeDtypeStruct((group, docs), jnp.bfloat16),
            compiler_params=params(),
        )(*values, embeddings)

    def reduce(outgoing):
        arrived = []
        for m in reduce_bits:
            taken = {d ^ m: swap(outgoing.pop(d), "row", nrow, m) for d in list(outgoing) if d & m}
            for d, value in taken.items():
                if d:
                    outgoing[d] = add_bf16(outgoing[d], value)
                else:
                    arrived.append(value)
        return arrived

    token = []

    def take(*values):
        if token:
            values = lax.optimization_barrier(values + (token.pop(),))[:-1]
        return values

    lists = {d: swap(neighbors, "row", nrow, d) if d else neighbors for d in dests}
    first = second = None
    tables = [[None] * PARTS for _ in range(GROUPS)]
    own = [[None] * PARTS for _ in range(GROUPS)]
    arrived = [[None] * PARTS for _ in range(GROUPS)]
    products = [None] * GROUPS
    for word in (word for line in ORDER for word in line.split()):
        c, step, p = ord(word[0]) - ord("A"), word[1], int(word[2:] or 0) - 1
        if step == "l":
            taken = take(*(lists[d] for d in dests))
            ids = dict(zip(dests, lax.optimization_barrier(tuple(table_ids(v) for v in taken))))
            token.append(ids[0])
        elif step == "s":
            if products[c] is None:
                sums = first_sums(c, *take(qrow))
            else:
                first, sums = next_sums(c, first, take(*products[c]))
            token.append(sums[0])
            for i, value in enumerate(sums):
                tables[c][i] = {0: value}
                for m in (NEXT, SIDE):
                    tables[c][i][m] = swap(value, "row", nrow, m)
        elif step == "f":
            table = tables[c][p]
            table[NEXT], table[SIDE] = take(table[NEXT], table[SIDE])
            table[NEXT | SIDE] = swap(table[NEXT], "row", nrow, SIDE)
            token.append(table[NEXT])
        elif step == "o":
            tables[c][p] = take(*(tables[c][p][m] for m in shards))
            outgoing = {d: combine(ids[d], tables[c][p], jnp.bfloat16) for d in dests if d}
            token.append(outgoing[reduce_bits[-1]])
            arrived[c][p] = reduce(outgoing)
        elif step == "w":
            own[c][p] = combine(ids[0], take(*tables[c][p]), jnp.float32)
            token.append(own[c][p])
        elif step == "z":
            arrived[c][p] = take(*arrived[c][p])
            token.append(arrived[c][p][-1])
        elif step == "e":
            flat = take(*own[c], *(v for values in arrived[c] for v in values))
            later = [flat[PARTS + i * len(reduce_bits):PARTS + (i + 1) * len(reduce_bits)] for i in range(PARTS)]
            value = expand([(flat[i], *later[i]) for i in range(PARTS)])
            products[c] = [value] + [swap(value, "col", ncol, m) for m in range(1, ncol)]
            token.append(value)
        else:
            second = finish(c, first, second, take(*products[c]))
            token.append(second)
    return first, second


def solution(mesh):
    placed = (P("row", "col"), P("row"), P(None, "row"), P("row", None))
    return jax.shard_map(
        body,
        mesh=mesh,
        in_specs=placed,
        out_specs=(P(None, "row"), P(None, "row")),
        check_vma=False,
    )
```

```python
import functools

import jax
import jax.numpy as jnp
from jax import lax
from jax.experimental import pallas as pl
from jax.experimental.pallas import tpu as pltpu
from jax.sharding import PartitionSpec as P

GROUPS = 2
PARTS = 2
TILE_BLOCKS = 8
VMEM_LIMIT = 8 * 1024 * 1024
SIDE, NEXT = 1, 2

ORDER = (
    "As Al Af1 Af2",
    "Ao1 Bs Ao2 Az1",
    "Aw Bg1 Ae Bo1",
    "Bg2 Ac Bo2 Bw",
    "Bz1 As Be Ag1",
    "Ag2 Bc Ao1 Bs",
    "Ao2 Az1 Bf1 Aw",
    "Ae Bo1 Bg2 Ac",
    "Ap Bo2 Bp Bw",
    "Bz1 Ar Be Bc",
    "Br",
)

VMEM = pl.BlockSpec(memory_space=pltpu.VMEM)
SMEM = pl.BlockSpec(memory_space=pltpu.SMEM)
ANY = pl.BlockSpec(memory_space=pl.ANY)
HBM = pl.BlockSpec(memory_space=pltpu.HBM)


def params():
    return pltpu.CompilerParams(vmem_limit_bytes=VMEM_LIMIT)


def swap(value, axis, size, mask):
    return lax.ppermute(value, axis, [(i, i ^ mask) for i in range(size)])


def add_bf16(a, b):
    return (a.astype(jnp.float32) + b.astype(jnp.float32)).astype(jnp.bfloat16)


def add_f32(a, b):
    return a.astype(jnp.float32) + b.astype(jnp.float32)


def store_sums(b, scaled, emb, sums_refs):
    sums = jnp.dot(scaled, emb, preferred_element_type=jnp.float32).astype(jnp.bfloat16)
    part = sums.shape[1] // len(sums_refs)
    for i, ref in enumerate(sums_refs):
        ref[b] = sums[:, i * part:(i + 1) * part]


def first_sums_kernel(rows, vec_ref, quality_ref, emb_ref, *refs):
    *sums_refs, vec, quality, emb, sems = refs
    tiles, tile_docs = emb.shape[:2]
    blocks = sums_refs[0].shape[0]
    block_len = tiles * tile_docs // blocks
    here = [
        pltpu.make_async_copy(quality_ref, quality, sems.at[tiles]),
        pltpu.make_async_copy(vec_ref.at[rows], vec, sems.at[tiles + 1]),
    ]

    def tile_copy(j):
        docs = pl.ds(pl.multiple_of(j * tile_docs, tile_docs), tile_docs)
        return pltpu.make_async_copy(emb_ref.at[docs], emb.at[j], sems.at[j])

    for copy in here:
        copy.start()
    for j in range(tiles):
        tile_copy(j).start()
    for copy in here:
        copy.wait()

    def step(j, carry):
        tile_copy(j).wait()
        for b in range(blocks // tiles):
            docs = pl.ds(pl.multiple_of(j * tile_docs + b * block_len, block_len), block_len)
            scaled = (vec[:, docs] * quality[:, docs]).astype(jnp.bfloat16)
            store_sums(j * (blocks // tiles) + b, scaled, emb[j, b * block_len:(b + 1) * block_len], sums_refs)
        return carry

    lax.fori_loop(0, tiles, step, 0)


def next_sums_kernel(rows, pair, vec_ref, quality_ref, emb_ref, *sums_refs):
    blocks = sums_refs[0].shape[0]
    block_len = emb_ref.shape[0] // blocks

    def step(b, carry):
        docs = pl.ds(pl.multiple_of(b * block_len, block_len), block_len)
        quality = quality_ref[:, docs]
        value = vec_ref[rows, docs]
        if pair:
            value = add_f32(pair[0][:, docs], pair[1][:, docs]) * quality - value
        store_sums(b, (value * quality).astype(jnp.bfloat16), emb_ref[docs], sums_refs)
        return carry

    lax.fori_loop(0, blocks, step, 0, unroll=TILE_BLOCKS)


def later_sums_kernel(rows, mine_ref, other_ref, *refs):
    next_sums_kernel(rows, (mine_ref, other_ref), *refs)


def fill_kernel(rows, second, mine_ref, other_ref, vec_ref, quality_ref, *refs):
    out_ref, out, sems = refs[-3:]
    tiles = sems.shape[0]
    tile_docs = out.shape[1] // tiles
    copies = []
    for j in range(tiles):
        docs = pl.ds(j * tile_docs, tile_docs)
        vec, quality = vec_ref[rows, docs], quality_ref[:, docs]
        total = add_f32(mine_ref[:, docs], other_ref[:, docs])
        if second:
            first = add_f32(refs[0][:, docs], refs[1][:, docs]) * quality - vec
            value = 2.0 * (total * quality - first) - vec
        else:
            value = total * quality - vec
        out[:, docs] = value
        copies.append(pltpu.make_async_copy(out.at[:, docs], out_ref.at[rows, docs], sems.at[j]))
        copies[-1].start()
    for copy in copies:
        copy.wait()


def lookup(ids_ref, tables, outs, entries):
    def step(b, carry):
        places = [ids_ref[b * entries + k] for k in range(entries)]
        for table, ref in zip(tables, outs):
            total = table[places[0]].astype(jnp.float32)
            for place in places[1:]:
                total = total + table[place].astype(jnp.float32)
            ref[b] = total.astype(ref.dtype)
        return carry

    lax.fori_loop(0, outs[0].shape[0], step, 0, unroll=4)


def table_kernel(ids_ref, *refs):
    *shards, out_ref, table, sems = refs
    blocks = shards[0].shape[0]
    copies = [
        pltpu.make_async_copy(ref, table.at[pl.ds(i * blocks, blocks)], sems.at[i])
        for i, ref in enumerate(shards)
    ]
    for copy in copies:
        copy.start()
    table[len(shards) * blocks] = jnp.zeros(table.shape[1:], table.dtype)
    for copy in copies:
        copy.wait()
    lookup(ids_ref, [table], [out_ref], ids_ref.shape[0] // blocks)


def lookup_kernel(ids_ref, *refs):
    count = len(refs) // 2
    lookup(ids_ref, refs[:count], refs[count:], ids_ref.shape[0] // refs[count].shape[0])


def expand_kernel(count, *refs):
    *refs, emb_ref, out_ref = refs
    blocks = refs[0].shape[0]
    block_len = emb_ref.shape[0] // blocks

    def step(b, carry):
        docs = pl.ds(pl.multiple_of(b * block_len, block_len), block_len)
        parts = []
        for at in range(0, len(refs), count):
            total = refs[at][b]
            for ref in refs[at + 1:at + count]:
                total = total + ref[b].astype(jnp.float32)
            parts.append(total.astype(jnp.bfloat16))
        out_ref[:, docs] = lax.dot_general(
            jnp.concatenate(parts, axis=1), emb_ref[docs], (((1,), (1,)), ((), ())),
            preferred_element_type=jnp.float32,
        ).astype(jnp.bfloat16)
        return carry

    lax.fori_loop(0, blocks, step, 0, unroll=TILE_BLOCKS)


def body(embeddings, quality, probes, neighbors):
    nrow, ncol = lax.axis_size("row"), lax.axis_size("col")
    me = lax.axis_index("row")
    blk_count, list_len = neighbors.shape
    docs, width = embeddings.shape
    nprobe = probes.shape[0]
    group, part = nprobe // GROUPS, width // PARTS
    tiles = blk_count // TILE_BLOCKS
    reduce_bits = [1 << i for i in reversed(range(nrow.bit_length() - 1)) if 1 << i not in (SIDE, NEXT)]
    dests = [0]
    for m in reversed(reduce_bits):
        dests = [d | m for d in dests] + dests
    shards = (0, NEXT, SIDE, NEXT | SIDE)

    def table_ids(lists):
        flat = lists.reshape(-1)
        apart = (flat // blk_count) ^ me
        place = flat % blk_count
        for i, shard in enumerate(shards):
            place = jnp.where(apart == shard, i * blk_count + flat % blk_count, place)
        return jnp.where((apart & ~(NEXT | SIDE)) == 0, place, len(shards) * blk_count)

    qrow = quality[None, :]
    shard_shape = (blk_count, group, part)
    shard_out = jax.ShapeDtypeStruct(shard_shape, jnp.bfloat16)
    vec_out = jax.ShapeDtypeStruct((nprobe, docs), jnp.float32)

    def rows(c):
        return pl.ds(c * group, group)

    def first_sums(c, qrow):
        if c:
            return pl.pallas_call(
                functools.partial(next_sums_kernel, rows(c), ()),
                in_specs=[VMEM] * 3,
                out_specs=[VMEM] * PARTS,
                out_shape=[shard_out] * PARTS,
                compiler_params=params(),
            )(probes, qrow, embeddings)
        return pl.pallas_call(
            functools.partial(first_sums_kernel, rows(c)),
            in_specs=[HBM] * 3,
            out_specs=[VMEM] * PARTS,
            out_shape=[shard_out] * PARTS,
            scratch_shapes=[
                pltpu.VMEM((group, docs), jnp.float32),
                pltpu.VMEM((1, docs), jnp.float32),
                pltpu.VMEM((tiles, docs // tiles, width), jnp.bfloat16),
                pltpu.SemaphoreType.DMA((tiles + 2,)),
            ],
            compiler_params=params(),
        )(*(pltpu.with_memory_space_constraint(v, pltpu.HBM) for v in (probes, qrow, embeddings)))

    def next_sums(c, pair):
        return pl.pallas_call(
            functools.partial(later_sums_kernel, rows(c)),
            in_specs=[VMEM] * 5,
            out_specs=[VMEM] * PARTS,
            out_shape=[shard_out] * PARTS,
            compiler_params=params(),
        )(*pair, probes, qrow, embeddings)

    def fill(c, held, pair, *others):
        held = [] if held is None else [held]
        return pl.pallas_call(
            functools.partial(fill_kernel, rows(c), bool(others)),
            in_specs=[VMEM] * (4 + len(others)) + [ANY] * len(held),
            out_specs=HBM,
            out_shape=vec_out,
            input_output_aliases={4 + len(others): 0} if held else {},
            scratch_shapes=[pltpu.VMEM((group, docs), jnp.float32), pltpu.SemaphoreType.DMA((4,))],
            compiler_params=params(),
        )(*pair, probes, qrow, *others, *held)

    def combine_far(ids, shards):
        rows_held = len(shards) * blk_count + 1
        return pl.pallas_call(
            table_kernel,
            in_specs=[SMEM] + [VMEM] * len(shards),
            out_specs=[VMEM] * 2,
            out_shape=[shard_out, jax.ShapeDtypeStruct((rows_held, group, part), jnp.bfloat16)],
            scratch_shapes=[pltpu.SemaphoreType.DMA((len(shards),))],
            compiler_params=params(),
        )(ids, *shards)

    def combine(ids, tables, dtype):
        return pl.pallas_call(
            lookup_kernel,
            in_specs=[SMEM] + [VMEM] * len(tables),
            out_specs=[VMEM] * len(tables),
            out_shape=[jax.ShapeDtypeStruct(shard_shape, dtype)] * len(tables),
            compiler_params=params(),
        )(ids, *tables)

    def expand(parts):
        values = [v for values in parts for v in values]
        return pl.pallas_call(
            functools.partial(expand_kernel, len(parts[0])),
            in_specs=[VMEM] * (len(values) + 1),
            out_specs=VMEM,
            out_shape=jax.ShapeDtypeStruct((group, docs), jnp.bfloat16),
            compiler_params=params(),
        )(*values, embeddings)

    def reduce(outgoing):
        arrived = []
        for m in reduce_bits:
            taken = {d ^ m: swap(outgoing.pop(d), "row", nrow, m) for d in list(outgoing) if d & m}
            for d, value in taken.items():
                if d:
                    outgoing[d] = add_bf16(outgoing[d], value)
                else:
                    arrived.append(value)
        return arrived

    token = []

    def take(*values):
        if token:
            values = lax.optimization_barrier(values + (token.pop(),))[:-1]
        return values

    lists = {d: swap(neighbors, "row", nrow, d) if d else neighbors for d in dests}
    first = second = None
    gathered = [[None] * PARTS for _ in range(GROUPS)]
    tables = [[None] * PARTS for _ in range(GROUPS)]
    own = [[None] * PARTS for _ in range(GROUPS)]
    arrived = [[None] * PARTS for _ in range(GROUPS)]
    products = [None] * GROUPS
    halves = [None] * GROUPS
    for word in (word for line in ORDER for word in line.split()):
        c, step, p = ord(word[0]) - ord("A"), word[1], int(word[2:] or 0) - 1
        if step == "l":
            taken = take(*(lists[d] for d in dests))
            ids = dict(zip(dests, lax.optimization_barrier(tuple(table_ids(v) for v in taken))))
            token.append(ids[0])
        elif step == "s":
            if products[c] is None:
                sums = first_sums(c, *take(qrow))
            else:
                sums = next_sums(c, take(*products[c]))
                halves[c] = products[c]
            token.append(sums[0])
            for i, value in enumerate(sums):
                gathered[c][i] = {0: value}
                for m in (NEXT, SIDE):
                    gathered[c][i][m] = swap(value, "row", nrow, m)
        elif step in "fg":
            held = gathered[c][p]
            if step == "g":
                held[NEXT], held[SIDE] = take(held[NEXT], held[SIDE])
            else:
                (held[NEXT],) = take(held[NEXT])
            held[NEXT | SIDE] = swap(held[NEXT], "row", nrow, SIDE)
            token.append(held[NEXT])
        elif step == "o":
            held = take(*(gathered[c][p][m] for m in shards))
            outgoing = {}
            for d in dests[:-1]:
                if outgoing:
                    outgoing[d] = combine(ids[d], [tables[c][p]], jnp.bfloat16)[0]
                else:
                    outgoing[d], tables[c][p] = combine_far(ids[d], held)
            token.append(outgoing[dests[-2]])
            arrived[c][p] = reduce(outgoing)
        elif step == "w":
            tables[c] = list(take(*tables[c]))
            own[c] = combine(ids[0], tables[c], jnp.float32)
            token.append(own[c][0])
        elif step == "z":
            arrived[c][p] = take(*arrived[c][p])
            token.append(arrived[c][p][-1])
        elif step == "e":
            flat = take(*own[c], *(v for values in arrived[c] for v in values))
            later = [flat[PARTS + i * len(reduce_bits):PARTS + (i + 1) * len(reduce_bits)] for i in range(PARTS)]
            value = expand([(flat[i], *later[i]) for i in range(PARTS)])
            products[c] = [value, swap(value, "col", ncol, 1)]
            token.append(value)
        elif step == "c":
            pair = take(*products[c])
            for i in range(1, ncol.bit_length() - 1):
                value = add_bf16(*pair)
                pair = [value, swap(value, "col", ncol, 1 << i)]
            products[c] = pair
            token.append(value)
        elif step == "p":
            first = fill(c, first, take(*halves[c]))
            token.append(first)
        else:
            second = fill(c, second, take(*products[c]), *halves[c])
            token.append(second)
    return first, second


def solution(mesh):
    placed = (P("row", "col"), P("row"), P(None, "row"), P("row", None))
    return jax.shard_map(
        body,
        mesh=mesh,
        in_specs=placed,
        out_specs=(P(None, "row"), P(None, "row")),
        check_vma=False,
    )
```

```python
import functools

import jax
import jax.numpy as jnp
from jax import lax
from jax.experimental import pallas as pl
from jax.experimental.pallas import tpu as pltpu
from jax.sharding import PartitionSpec as P

GROUPS = 2
TILE_BLOCKS = 8
VMEM_LIMIT = 8 * 1024 * 1024
SIDE, NEXT = 1, 2

ORDER = (
    "As Bs Ag Al",
    "Bh Ao Bi Bj",
    "Aw Bn Bw Ae",
    "Be Ac Bc As",
    "Bs Ag Bh Ao",
    "Bi Ap Aw Bj",
    "Bn Bw Bp Ae",
    "Be Ac Bc Ar",
    "Br",
)

VMEM = pl.BlockSpec(memory_space=pltpu.VMEM)
SMEM = pl.BlockSpec(memory_space=pltpu.SMEM)
ANY = pl.BlockSpec(memory_space=pl.ANY)
HBM = pl.BlockSpec(memory_space=pltpu.HBM)


def params():
    return pltpu.CompilerParams(vmem_limit_bytes=VMEM_LIMIT)


def swap(value, axis, size, mask):
    return lax.ppermute(value, axis, [(i, i ^ mask) for i in range(size)])


def add_bf16(a, b):
    return (a.astype(jnp.float32) + b.astype(jnp.float32)).astype(jnp.bfloat16)


def add_f32(a, b):
    return a.astype(jnp.float32) + b.astype(jnp.float32)


def block_sum(scaled, emb):
    return jnp.dot(scaled, emb, preferred_element_type=jnp.float32).astype(jnp.bfloat16)


def first_sums_kernel(rows, vec_ref, quality_ref, emb_ref, *refs):
    sums_ref, vec, quality, emb, sems = refs
    tiles, tile_docs = emb.shape[:2]
    blocks = sums_ref.shape[0]
    block_len = tiles * tile_docs // blocks
    here = [
        pltpu.make_async_copy(quality_ref, quality, sems.at[tiles]),
        pltpu.make_async_copy(vec_ref.at[rows], vec, sems.at[tiles + 1]),
    ]

    def tile_copy(j):
        docs = pl.ds(pl.multiple_of(j * tile_docs, tile_docs), tile_docs)
        return pltpu.make_async_copy(emb_ref.at[docs], emb.at[j], sems.at[j])

    for copy in here:
        copy.start()
    for j in range(tiles):
        tile_copy(j).start()
    for copy in here:
        copy.wait()

    def step(j, carry):
        tile_copy(j).wait()
        for b in range(blocks // tiles):
            docs = pl.ds(pl.multiple_of(j * tile_docs + b * block_len, block_len), block_len)
            scaled = (vec[:, docs] * quality[:, docs]).astype(jnp.bfloat16)
            sums_ref[j * (blocks // tiles) + b] = block_sum(scaled, emb[j, b * block_len:(b + 1) * block_len])
        return carry

    lax.fori_loop(0, tiles, step, 0)


def next_sums_kernel(rows, pair, vec_ref, quality_ref, emb_ref, sums_ref):
    blocks = sums_ref.shape[0]
    block_len = emb_ref.shape[0] // blocks

    def step(b, carry):
        docs = pl.ds(pl.multiple_of(b * block_len, block_len), block_len)
        quality = quality_ref[:, docs]
        value = vec_ref[rows, docs]
        if pair:
            value = add_f32(pair[0][:, docs], pair[1][:, docs]) * quality - value
        sums_ref[b] = block_sum((value * quality).astype(jnp.bfloat16), emb_ref[docs])
        return carry

    lax.fori_loop(0, blocks, step, 0, unroll=TILE_BLOCKS)


def later_sums_kernel(rows, mine_ref, other_ref, *refs):
    next_sums_kernel(rows, (mine_ref, other_ref), *refs)


def fill_kernel(rows, second, mine_ref, other_ref, vec_ref, quality_ref, *refs):
    out_ref, out, sems = refs[-3:]
    tiles = sems.shape[0]
    tile_docs = out.shape[1] // tiles
    copies = []
    for j in range(tiles):
        docs = pl.ds(j * tile_docs, tile_docs)
        vec, quality = vec_ref[rows, docs], quality_ref[:, docs]
        total = add_f32(mine_ref[:, docs], other_ref[:, docs])
        if second:
            first = add_f32(refs[0][:, docs], refs[1][:, docs]) * quality - vec
            value = 2.0 * (total * quality - first) - vec
        else:
            value = total * quality - vec
        out[:, docs] = value
        copies.append(pltpu.make_async_copy(out.at[:, docs], out_ref.at[rows, docs], sems.at[j]))
        copies[-1].start()
    for copy in copies:
        copy.wait()


def lookup_kernel(ids_ref, table, out_ref):
    entries = ids_ref.shape[0] // out_ref.shape[0]

    def step(b, carry):
        total = table[ids_ref[b * entries]].astype(jnp.float32)
        for k in range(1, entries):
            total = total + table[ids_ref[b * entries + k]].astype(jnp.float32)
        out_ref[b] = total.astype(out_ref.dtype)
        return carry

    lax.fori_loop(0, out_ref.shape[0], step, 0, unroll=4)


def table_kernel(ids_ref, *refs):
    *shards, out_ref, table, sems = refs
    blocks = shards[0].shape[0]
    copies = [
        pltpu.make_async_copy(ref, table.at[pl.ds(i * blocks, blocks)], sems.at[i])
        for i, ref in enumerate(shards)
    ]
    for copy in copies:
        copy.start()
    table[len(shards) * blocks] = jnp.zeros(table.shape[1:], table.dtype)
    for copy in copies:
        copy.wait()
    lookup_kernel(ids_ref, table, out_ref)


def expand_kernel(own_ref, *refs):
    *arrived_refs, emb_ref, out_ref = refs
    blocks = own_ref.shape[0]
    block_len = emb_ref.shape[0] // blocks

    def step(b, carry):
        docs = pl.ds(pl.multiple_of(b * block_len, block_len), block_len)
        total = own_ref[b]
        for ref in arrived_refs:
            total = total + ref[b].astype(jnp.float32)
        out_ref[:, docs] = lax.dot_general(
            total.astype(jnp.bfloat16), emb_ref[docs], (((1,), (1,)), ((), ())),
            preferred_element_type=jnp.float32,
        ).astype(jnp.bfloat16)
        return carry

    lax.fori_loop(0, blocks, step, 0, unroll=TILE_BLOCKS)


def body(embeddings, quality, probes, neighbors):
    nrow, ncol = lax.axis_size("row"), lax.axis_size("col")
    me = lax.axis_index("row")
    blk_count, list_len = neighbors.shape
    docs, width = embeddings.shape
    nprobe = probes.shape[0]
    group = nprobe // GROUPS
    tiles = blk_count // TILE_BLOCKS
    near = [NEXT, SIDE]
    far = [1 << i for i in reversed(range(nrow.bit_length() - 1)) if 1 << i not in near]
    far_dests = [0]
    for m in reversed(far):
        far_dests = [d | m for d in far_dests] + far_dests

    def table_ids(lists, dest, bits):
        flat = lax.dynamic_slice_in_dim(lists, (me ^ dest) * blk_count, blk_count).reshape(-1)
        apart = (flat // blk_count) ^ me
        place = flat % blk_count
        for i, m in enumerate(bits):
            place = place + jnp.where((apart & m) != 0, blk_count << i, 0)
        return jnp.where((apart & ~sum(bits)) == 0, place, blk_count << len(bits))

    qrow = quality[None, :]

    def blocks_out(count, dtype):
        return jax.ShapeDtypeStruct((count, group, width), dtype)

    shard_out = blocks_out(blk_count, jnp.bfloat16)
    vec_out = jax.ShapeDtypeStruct((nprobe, docs), jnp.float32)

    def rows(c):
        return pl.ds(c * group, group)

    def first_sums(c, qrow):
        if c:
            return pl.pallas_call(
                functools.partial(next_sums_kernel, rows(c), ()),
                in_specs=[VMEM] * 3,
                out_specs=VMEM,
                out_shape=shard_out,
                compiler_params=params(),
            )(probes, qrow, embeddings)
        return pl.pallas_call(
            functools.partial(first_sums_kernel, rows(c)),
            in_specs=[HBM] * 3,
            out_specs=VMEM,
            out_shape=shard_out,
            scratch_shapes=[
                pltpu.VMEM((group, docs), jnp.float32),
                pltpu.VMEM((1, docs), jnp.float32),
                pltpu.VMEM((tiles, docs // tiles, width), jnp.bfloat16),
                pltpu.SemaphoreType.DMA((tiles + 2,)),
            ],
            compiler_params=params(),
        )(*(pltpu.with_memory_space_constraint(v, pltpu.HBM) for v in (probes, qrow, embeddings)))

    def next_sums(c, pair):
        return pl.pallas_call(
            functools.partial(later_sums_kernel, rows(c)),
            in_specs=[VMEM] * 5,
            out_specs=VMEM,
            out_shape=shard_out,
            compiler_params=params(),
        )(*pair, probes, qrow, embeddings)

    def fill(c, held, pair, *others):
        held = [] if held is None else [held]
        return pl.pallas_call(
            functools.partial(fill_kernel, rows(c), bool(others)),
            in_specs=[VMEM] * (4 + len(others)) + [ANY] * len(held),
            out_specs=HBM,
            out_shape=vec_out,
            input_output_aliases={4 + len(others): 0} if held else {},
            scratch_shapes=[pltpu.VMEM((group, docs), jnp.float32), pltpu.SemaphoreType.DMA((4,))],
            compiler_params=params(),
        )(*pair, probes, qrow, *others, *held)

    def combine_first(ids, shards):
        return pl.pallas_call(
            table_kernel,
            in_specs=[SMEM] + [VMEM] * len(shards),
            out_specs=[VMEM] * 2,
            out_shape=[shard_out, blocks_out(len(shards) * blk_count + 1, jnp.bfloat16)],
            scratch_shapes=[pltpu.SemaphoreType.DMA((len(shards),))],
            compiler_params=params(),
        )(ids, *shards)

    def combine(ids, table, dtype):
        return pl.pallas_call(
            lookup_kernel,
            in_specs=[SMEM, VMEM],
            out_specs=VMEM,
            out_shape=blocks_out(blk_count, dtype),
            compiler_params=params(),
        )(ids, table)

    def expand(own, arrived):
        return pl.pallas_call(
            expand_kernel,
            in_specs=[VMEM] * (len(arrived) + 2),
            out_specs=VMEM,
            out_shape=jax.ShapeDtypeStruct((group, docs), jnp.bfloat16),
            compiler_params=params(),
        )(own, *arrived, embeddings)

    def reduce(outgoing, bits):
        arrived = []
        for m in bits:
            taken = {d ^ m: swap(outgoing.pop(d), "row", nrow, m) for d in list(outgoing) if d & m}
            for d, value in taken.items():
                if d:
                    outgoing[d] = add_bf16(outgoing[d], value)
                else:
                    arrived.append(value)
        return arrived

    token = []

    def take(*values):
        if token:
            values = lax.optimization_barrier(values + (token.pop(),))[:-1]
        return values

    lists = lax.all_gather(neighbors, "row", axis=0, tiled=True)
    first = second = None
    gathered, tables, own, arrived, products, halves = ([None] * GROUPS for _ in range(6))
    for word in (word for line in ORDER for word in line.split()):
        c, step = ord(word[0]) - ord("A"), word[1]
        if step == "l":
            (lists,) = take(lists)
            ids = {(0, d): table_ids(lists, d, near) for d in far_dests}
            ids.update({(1, d): table_ids(lists, d, far) for d in (NEXT | SIDE, SIDE, NEXT, 0)})
            ids = lax.optimization_barrier(ids)
            token.append(ids[0, 0])
        elif step == "s":
            if products[c] is None:
                sums = first_sums(c, *take(qrow))
            else:
                sums = next_sums(c, take(*products[c]))
                halves[c] = products[c]
            token.append(sums)
            gathered[c] = [sums] + [swap(sums, "row", nrow, m) for m in (far[:1] if c else near)]
        elif step == "g":
            gathered[c] = list(take(*gathered[c]))
            gathered[c].append(swap(gathered[c][1], "row", nrow, SIDE))
            token.append(gathered[c][1])
        elif step == "o":
            held, table, outgoing = take(*gathered[c]), None, {}
            for d in far_dests[:-1]:
                if table is None:
                    outgoing[d], table = combine_first(ids[c, d], held)
                else:
                    outgoing[d] = combine(ids[c, d], table, jnp.bfloat16)
            tables[c] = table
            token.append(outgoing[far_dests[-2]])
            arrived[c] = reduce(outgoing, far)
        elif step == "h":
            for m in far[1:]:
                gathered[c] += [swap(v, "row", nrow, m) for v in gathered[c]]
            value, tables[c] = combine_first(ids[c, NEXT | SIDE], take(*gathered[c]))
            arrived[c] = [swap(value, "row", nrow, SIDE)]
            token.append(value)
        elif step == "i":
            (table,) = take(tables[c])
            value = combine(ids[c, SIDE], table, jnp.bfloat16)
            arrived[c].append(swap(value, "row", nrow, SIDE))
            token.append(value)
        elif step == "j":
            (table,) = take(tables[c])
            own[c] = combine(ids[c, NEXT], table, jnp.bfloat16)
            token.append(own[c])
        elif step == "n":
            value = add_bf16(*take(own[c], arrived[c].pop(0)))
            arrived[c].append(swap(value, "row", nrow, NEXT))
            token.append(value)
        elif step == "w":
            (table,) = take(tables[c])
            own[c] = combine(ids[c, 0], table, jnp.float32)
            token.append(own[c])
        elif step == "e":
            here, *later = take(own[c], *arrived[c])
            value = expand(here, later)
            products[c] = [value, swap(value, "col", ncol, 1)]
            token.append(value)
        elif step == "c":
            pair = take(*products[c])
            for i in range(1, ncol.bit_length() - 1):
                value = add_bf16(*pair)
                pair = [value, swap(value, "col", ncol, 1 << i)]
            products[c] = pair
            token.append(value)
        elif step == "p":
            first = fill(c, first, take(*halves[c]))
            token.append(first)
        else:
            second = fill(c, second, take(*products[c]), *halves[c])
            token.append(second)
    return first, second


def solution(mesh):
    placed = (P("row", "col"), P("row"), P(None, "row"), P("row", None))
    return jax.shard_map(
        body,
        mesh=mesh,
        in_specs=placed,
        out_specs=(P(None, "row"), P(None, "row")),
        check_vma=False,
    )
```

```python
import functools

import jax
import jax.numpy as jnp
from jax import lax
from jax.experimental import pallas as pl
from jax.experimental.pallas import tpu as pltpu
from jax.sharding import PartitionSpec as P

GROUPS = 2
PARTS = 2
TILE_BLOCKS = 8
VMEM_LIMIT = 8 * 1024 * 1024
SIDE, NEXT = 1, 2

ORDER = (
    "As Al Af1 Af2",
    "Bs Ao1 Ao2 Aw",
    "Ae1 Bf1 Bg2 Ae2",
    "Bo1 Ac As Bo2",
    "Bw Be1 Ag1 Be2",
    "Ag2 Ao1 Bc Bs",
    "Ao2 Aw Ae1 Ap",
    "Bg1 Ae2 Bg2 Bo1",
    "Bo2 Bp Ac Bw",
    "Be1 Ar Be2 Bc",
    "Br",
)

VMEM = pl.BlockSpec(memory_space=pltpu.VMEM)
SMEM = pl.BlockSpec(memory_space=pltpu.SMEM)
ANY = pl.BlockSpec(memory_space=pl.ANY)
HBM = pl.BlockSpec(memory_space=pltpu.HBM)


def params():
    return pltpu.CompilerParams(vmem_limit_bytes=VMEM_LIMIT)


def swap(value, axis, size, mask):
    return lax.ppermute(value, axis, [(i, i ^ mask) for i in range(size)])


def add_bf16(a, b):
    return (a.astype(jnp.float32) + b.astype(jnp.float32)).astype(jnp.bfloat16)


def add_f32(a, b):
    return a.astype(jnp.float32) + b.astype(jnp.float32)


def store_sums(b, scaled, emb, sums_refs):
    sums = jnp.dot(scaled, emb, preferred_element_type=jnp.float32).astype(jnp.bfloat16)
    part = sums.shape[1] // len(sums_refs)
    for i, ref in enumerate(sums_refs):
        ref[b] = sums[:, i * part:(i + 1) * part]


def first_sums_kernel(rows, vec_ref, quality_ref, emb_ref, *refs):
    *sums_refs, vec, quality, emb, sems = refs
    tiles, tile_docs = emb.shape[:2]
    blocks = sums_refs[0].shape[0]
    block_len = tiles * tile_docs // blocks
    here = [
        pltpu.make_async_copy(quality_ref, quality, sems.at[tiles]),
        pltpu.make_async_copy(vec_ref.at[rows], vec, sems.at[tiles + 1]),
    ]

    def tile_copy(j):
        docs = pl.ds(pl.multiple_of(j * tile_docs, tile_docs), tile_docs)
        return pltpu.make_async_copy(emb_ref.at[docs], emb.at[j], sems.at[j])

    for copy in here:
        copy.start()
    for j in range(tiles):
        tile_copy(j).start()
    for copy in here:
        copy.wait()

    def step(j, carry):
        tile_copy(j).wait()
        for b in range(blocks // tiles):
            docs = pl.ds(pl.multiple_of(j * tile_docs + b * block_len, block_len), block_len)
            scaled = (vec[:, docs] * quality[:, docs]).astype(jnp.bfloat16)
            store_sums(j * (blocks // tiles) + b, scaled, emb[j, b * block_len:(b + 1) * block_len], sums_refs)
        return carry

    lax.fori_loop(0, tiles, step, 0)


def next_sums_kernel(rows, pair, vec_ref, quality_ref, emb_ref, *sums_refs):
    blocks = sums_refs[0].shape[0]
    block_len = emb_ref.shape[0] // blocks

    def step(b, carry):
        docs = pl.ds(pl.multiple_of(b * block_len, block_len), block_len)
        quality = quality_ref[:, docs]
        value = vec_ref[rows, docs]
        if pair:
            value = add_f32(pair[0][:, docs], pair[1][:, docs]) * quality - value
        store_sums(b, (value * quality).astype(jnp.bfloat16), emb_ref[docs], sums_refs)
        return carry

    lax.fori_loop(0, blocks, step, 0, unroll=TILE_BLOCKS)


def later_sums_kernel(rows, mine_ref, other_ref, *refs):
    next_sums_kernel(rows, (mine_ref, other_ref), *refs)


def fill_kernel(rows, second, mine_ref, other_ref, vec_ref, quality_ref, *refs):
    out_ref, out, sems = refs[-3:]
    tiles = sems.shape[0]
    tile_docs = out.shape[1] // tiles
    copies = []
    for j in range(tiles):
        docs = pl.ds(j * tile_docs, tile_docs)
        vec, quality = vec_ref[rows, docs], quality_ref[:, docs]
        total = add_f32(mine_ref[:, docs], other_ref[:, docs])
        if second:
            first = add_f32(refs[0][:, docs], refs[1][:, docs]) * quality - vec
            value = 2.0 * (total * quality - first) - vec
        else:
            value = total * quality - vec
        out[:, docs] = value
        copies.append(pltpu.make_async_copy(out.at[:, docs], out_ref.at[rows, docs], sems.at[j]))
        copies[-1].start()
    for copy in copies:
        copy.wait()


def lookup(ids_ref, tables, outs, entries):
    def step(b, carry):
        places = [ids_ref[b * entries + k] for k in range(entries)]
        for table, ref in zip(tables, outs):
            total = table[places[0]].astype(jnp.float32)
            for place in places[1:]:
                total = total + table[place].astype(jnp.float32)
            ref[b] = total.astype(ref.dtype)
        return carry

    lax.fori_loop(0, outs[0].shape[0], step, 0, unroll=4)


def table_kernel(ids_ref, *refs):
    *shards, out_ref, table, sems = refs
    blocks = shards[0].shape[0]
    copies = [
        pltpu.make_async_copy(ref, table.at[pl.ds(i * blocks, blocks)], sems.at[i])
        for i, ref in enumerate(shards)
    ]
    for copy in copies:
        copy.start()
    table[len(shards) * blocks] = jnp.zeros(table.shape[1:], table.dtype)
    for copy in copies:
        copy.wait()
    lookup(ids_ref, [table], [out_ref], ids_ref.shape[0] // blocks)


def lookup_kernel(ids_ref, *refs):
    count = len(refs) // 2
    lookup(ids_ref, refs[:count], refs[count:], ids_ref.shape[0] // refs[count].shape[0])


def expand_kernel(part, own_ref, *refs):
    *refs, emb_ref, out_ref = refs
    blocks, _, width = own_ref.shape
    block_len = emb_ref.shape[0] // blocks
    held = refs.pop() if part else None
    features = pl.ds(part * width, width)

    def step(b, carry):
        docs = pl.ds(pl.multiple_of(b * block_len, block_len), block_len)
        total = own_ref[b]
        for ref in refs:
            total = total + ref[b].astype(jnp.float32)
        products = lax.dot_general(
            total.astype(jnp.bfloat16), emb_ref[docs, features], (((1,), (1,)), ((), ())),
            preferred_element_type=jnp.float32,
        )
        if part:
            products = products + held[:, docs]
        out_ref[:, docs] = products.astype(out_ref.dtype)
        return carry

    lax.fori_loop(0, blocks, step, 0, unroll=TILE_BLOCKS)


def body(embeddings, quality, probes, neighbors):
    nrow, ncol = lax.axis_size("row"), lax.axis_size("col")
    me = lax.axis_index("row")
    blk_count, list_len = neighbors.shape
    docs, width = embeddings.shape
    nprobe = probes.shape[0]
    group, part = nprobe // GROUPS, width // PARTS
    tiles = blk_count // TILE_BLOCKS
    reduce_bits = [1 << i for i in reversed(range(nrow.bit_length() - 1)) if 1 << i not in (SIDE, NEXT)]
    dests = [0]
    for m in reversed(reduce_bits):
        dests = [d | m for d in dests] + dests
    shards = (0, NEXT, SIDE, NEXT | SIDE)

    def table_ids(lists):
        flat = lists.reshape(-1)
        apart = (flat // blk_count) ^ me
        place = flat % blk_count
        for i, shard in enumerate(shards):
            place = jnp.where(apart == shard, i * blk_count + flat % blk_count, place)
        return jnp.where((apart & ~(NEXT | SIDE)) == 0, place, len(shards) * blk_count)

    qrow = quality[None, :]
    shard_shape = (blk_count, group, part)
    shard_out = jax.ShapeDtypeStruct(shard_shape, jnp.bfloat16)
    vec_out = jax.ShapeDtypeStruct((nprobe, docs), jnp.float32)

    def rows(c):
        return pl.ds(c * group, group)

    def first_sums(c, qrow):
        if c:
            return pl.pallas_call(
                functools.partial(next_sums_kernel, rows(c), ()),
                in_specs=[VMEM] * 3,
                out_specs=[VMEM] * PARTS,
                out_shape=[shard_out] * PARTS,
                compiler_params=params(),
            )(probes, qrow, embeddings)
        return pl.pallas_call(
            functools.partial(first_sums_kernel, rows(c)),
            in_specs=[HBM] * 3,
            out_specs=[VMEM] * PARTS,
            out_shape=[shard_out] * PARTS,
            scratch_shapes=[
                pltpu.VMEM((group, docs), jnp.float32),
                pltpu.VMEM((1, docs), jnp.float32),
                pltpu.VMEM((tiles, docs // tiles, width), jnp.bfloat16),
                pltpu.SemaphoreType.DMA((tiles + 2,)),
            ],
            compiler_params=params(),
        )(*(pltpu.with_memory_space_constraint(v, pltpu.HBM) for v in (probes, qrow, embeddings)))

    def next_sums(c, pair):
        return pl.pallas_call(
            functools.partial(later_sums_kernel, rows(c)),
            in_specs=[VMEM] * 5,
            out_specs=[VMEM] * PARTS,
            out_shape=[shard_out] * PARTS,
            compiler_params=params(),
        )(*pair, probes, qrow, embeddings)

    def fill(c, held, pair, *others):
        held = [] if held is None else [held]
        return pl.pallas_call(
            functools.partial(fill_kernel, rows(c), bool(others)),
            in_specs=[VMEM] * (4 + len(others)) + [ANY] * len(held),
            out_specs=HBM,
            out_shape=vec_out,
            input_output_aliases={4 + len(others): 0} if held else {},
            scratch_shapes=[pltpu.VMEM((group, docs), jnp.float32), pltpu.SemaphoreType.DMA((4,))],
            compiler_params=params(),
        )(*pair, probes, qrow, *others, *held)

    def combine_far(ids, shards):
        rows_held = len(shards) * blk_count + 1
        return pl.pallas_call(
            table_kernel,
            in_specs=[SMEM] + [VMEM] * len(shards),
            out_specs=[VMEM] * 2,
            out_shape=[shard_out, jax.ShapeDtypeStruct((rows_held, group, part), jnp.bfloat16)],
            scratch_shapes=[pltpu.SemaphoreType.DMA((len(shards),))],
            compiler_params=params(),
        )(ids, *shards)

    def combine(ids, tables, dtype):
        return pl.pallas_call(
            lookup_kernel,
            in_specs=[SMEM] + [VMEM] * len(tables),
            out_specs=[VMEM] * len(tables),
            out_shape=[jax.ShapeDtypeStruct(shard_shape, dtype)] * len(tables),
            compiler_params=params(),
        )(ids, *tables)

    def expand(p, own, arrived, held):
        values = [own, *arrived] + ([held] if p else [])
        return pl.pallas_call(
            functools.partial(expand_kernel, p),
            in_specs=[VMEM] * (len(values) + 1),
            out_specs=VMEM,
            out_shape=jax.ShapeDtypeStruct((group, docs), jnp.bfloat16 if p + 1 == PARTS else jnp.float32),
            compiler_params=params(),
        )(*values, embeddings)

    def reduce(outgoing):
        arrived = []
        for m in reduce_bits:
            taken = {d ^ m: swap(outgoing.pop(d), "row", nrow, m) for d in list(outgoing) if d & m}
            for d, value in taken.items():
                if d:
                    outgoing[d] = add_bf16(outgoing[d], value)
                else:
                    arrived.append(value)
        return arrived

    token = []

    def take(*values):
        if token:
            values = lax.optimization_barrier(values + (token.pop(),))[:-1]
        return values

    lists = {d: swap(neighbors, "row", nrow, d) if d else neighbors for d in dests}
    first = second = None
    gathered = [[None] * PARTS for _ in range(GROUPS)]
    tables = [[None] * PARTS for _ in range(GROUPS)]
    own = [[None] * PARTS for _ in range(GROUPS)]
    arrived = [[None] * PARTS for _ in range(GROUPS)]
    products = [None] * GROUPS
    halves = [None] * GROUPS
    for word in (word for line in ORDER for word in line.split()):
        c, step, p = ord(word[0]) - ord("A"), word[1], int(word[2:] or 0) - 1
        if step == "l":
            taken = take(*(lists[d] for d in dests))
            ids = dict(zip(dests, lax.optimization_barrier(tuple(table_ids(v) for v in taken))))
            token.append(ids[0])
        elif step == "s":
            if products[c] is None:
                sums = first_sums(c, *take(qrow))
                if c == 0:
                    *sums, tied = lax.optimization_barrier((*sums, tuple(lists.values())))
                    lists = dict(zip(lists, tied))
            else:
                sums = next_sums(c, take(*products[c]))
                halves[c] = products[c]
            token.append(sums[0])
            for i, value in enumerate(sums):
                gathered[c][i] = {0: value}
                for m in (NEXT, SIDE):
                    gathered[c][i][m] = swap(value, "row", nrow, m)
        elif step in "fg":
            held = gathered[c][p]
            if step == "g":
                held[NEXT], held[SIDE] = take(held[NEXT], held[SIDE])
            else:
                (held[NEXT],) = take(held[NEXT])
            held[NEXT | SIDE] = swap(held[NEXT], "row", nrow, SIDE)
            token.append(held[NEXT])
        elif step == "o":
            held = take(*(gathered[c][p][m] for m in shards))
            outgoing = {}
            for d in dests[:-1]:
                if outgoing:
                    outgoing[d] = combine(ids[d], [tables[c][p]], jnp.bfloat16)[0]
                else:
                    outgoing[d], tables[c][p] = combine_far(ids[d], held)
            token.append(outgoing[dests[-2]])
            arrived[c][p] = reduce(outgoing)
        elif step == "w":
            tables[c] = list(take(*tables[c]))
            own[c] = combine(ids[0], tables[c], jnp.float32)
            token.append(own[c][0])
        elif step == "z":
            arrived[c][p] = take(*arrived[c][p])
            token.append(arrived[c][p][-1])
        elif step == "e":
            here, *later = take(own[c][p], *arrived[c][p])
            value = expand(p, here, later, products[c])
            products[c] = value
            token.append(value)
            if p + 1 == PARTS:
                products[c] = [value, swap(value, "col", ncol, 1)]
        elif step == "c":
            pair = take(*products[c])
            for i in range(1, ncol.bit_length() - 1):
                value = add_bf16(*pair)
                pair = [value, swap(value, "col", ncol, 1 << i)]
            products[c] = pair
            token.append(value)
        elif step == "p":
            first = fill(c, first, take(*halves[c]))
            token.append(first)
        else:
            second = fill(c, second, take(*products[c]), *halves[c])
            token.append(second)
    return first, second


def solution(mesh):
    placed = (P("row", "col"), P("row"), P(None, "row"), P("row", None))
    return jax.shard_map(
        body,
        mesh=mesh,
        in_specs=placed,
        out_specs=(P(None, "row"), P(None, "row")),
        check_vma=False,
    )
```

```python
import functools

import jax
import jax.numpy as jnp
from jax import lax
from jax.experimental import pallas as pl
from jax.experimental.pallas import tpu as pltpu
from jax.sharding import PartitionSpec as P

GROUPS = 2
PARTS = 2
TILE_BLOCKS = 8
UNROLL = 16
VMEM_LIMIT = 8 * 1024 * 1024
SIDE, NEXT = 1, 2

ORDER = (
    "As Al Af1 Af2",
    "Ao1 Ao2 Aw Az1",
    "Bg1 Az2 Bg2 Ae",
    "Bo1 Ac As Bo2",
    "Bw Bz1 Ag1 Be",
    "Ag2 Ao1 Bc Ao2",
    "Bs Aw Az1 Ap",
    "Bg1 Ae Bf2 Bo1",
    "Bo2 Bp Ac Bw",
    "Bz1 Ar Be Bc",
    "Br",
)

VMEM = pl.BlockSpec(memory_space=pltpu.VMEM)
SMEM = pl.BlockSpec(memory_space=pltpu.SMEM)
ANY = pl.BlockSpec(memory_space=pl.ANY)
HBM = pl.BlockSpec(memory_space=pltpu.HBM)


def params():
    return pltpu.CompilerParams(vmem_limit_bytes=VMEM_LIMIT)


def swap(value, axis, size, mask):
    return lax.ppermute(value, axis, [(i, i ^ mask) for i in range(size)])


def add_bf16(a, b):
    return (a.astype(jnp.float32) + b.astype(jnp.float32)).astype(jnp.bfloat16)


def add_f32(a, b):
    return a.astype(jnp.float32) + b.astype(jnp.float32)


def store_sums(b, scaled, emb, sums_refs):
    sums = jnp.dot(scaled, emb, preferred_element_type=jnp.float32).astype(jnp.bfloat16)
    _, group, part = sums_refs[0].shape
    for i, ref in enumerate(sums_refs):
        c, p = divmod(i, sums.shape[1] // part)
        ref[b] = sums[c * group:(c + 1) * group, p * part:(p + 1) * part]


def first_sums_kernel(vec_ref, quality_ref, emb_ref, *refs):
    *sums_refs, vec, quality, emb, sems = refs
    tiles, tile_docs = emb.shape[:2]
    blocks = sums_refs[0].shape[0]
    block_len = tiles * tile_docs // blocks
    here = [
        pltpu.make_async_copy(quality_ref, quality, sems.at[tiles]),
        pltpu.make_async_copy(vec_ref, vec, sems.at[tiles + 1]),
    ]

    def tile_copy(j):
        docs = pl.ds(pl.multiple_of(j * tile_docs, tile_docs), tile_docs)
        return pltpu.make_async_copy(emb_ref.at[docs], emb.at[j], sems.at[j])

    for copy in here:
        copy.start()
    for j in range(tiles):
        tile_copy(j).start()
    for copy in here:
        copy.wait()

    def step(j, carry):
        tile_copy(j).wait()
        for b in range(blocks // tiles):
            docs = pl.ds(pl.multiple_of(j * tile_docs + b * block_len, block_len), block_len)
            scaled = (vec[:, docs] * quality[:, docs]).astype(jnp.bfloat16)
            store_sums(j * (blocks // tiles) + b, scaled, emb[j, b * block_len:(b + 1) * block_len], sums_refs)
        return carry

    lax.fori_loop(0, tiles, step, 0)


def next_sums_kernel(rows, mine_ref, other_ref, vec_ref, quality_ref, emb_ref, *sums_refs):
    blocks = sums_refs[0].shape[0]
    block_len = emb_ref.shape[0] // blocks

    def step(b, carry):
        docs = pl.ds(pl.multiple_of(b * block_len, block_len), block_len)
        quality = quality_ref[:, docs]
        value = add_f32(mine_ref[:, docs], other_ref[:, docs]) * quality - vec_ref[rows, docs]
        store_sums(b, (value * quality).astype(jnp.bfloat16), emb_ref[docs], sums_refs)
        return carry

    lax.fori_loop(0, blocks, step, 0, unroll=UNROLL)


def fill_kernel(rows, second, mine_ref, other_ref, vec_ref, quality_ref, *refs):
    out_ref, out, sems = refs[-3:]
    tiles = sems.shape[0]
    tile_docs = out.shape[1] // tiles
    copies = []
    for j in range(tiles):
        docs = pl.ds(j * tile_docs, tile_docs)
        vec, quality = vec_ref[rows, docs], quality_ref[:, docs]
        total = add_f32(mine_ref[:, docs], other_ref[:, docs])
        if second:
            first = add_f32(refs[0][:, docs], refs[1][:, docs]) * quality - vec
            value = 2.0 * (total * quality - first) - vec
        else:
            value = total * quality - vec
        out[:, docs] = value
        copies.append(pltpu.make_async_copy(out.at[:, docs], out_ref.at[rows, docs], sems.at[j]))
        copies[-1].start()
    for copy in copies:
        copy.wait()


def lookup(ids_ref, tables, outs, entries):
    def step(b, carry):
        places = [ids_ref[b * entries + k] for k in range(entries)]
        for table, ref in zip(tables, outs):
            total = table[places[0]].astype(jnp.float32)
            for place in places[1:]:
                total = total + table[place].astype(jnp.float32)
            ref[b] = total.astype(ref.dtype)
        return carry

    lax.fori_loop(0, outs[0].shape[0], step, 0, unroll=UNROLL)


def table_kernel(ids_ref, *refs):
    *shards, out_ref, table, sems = refs
    blocks = shards[0].shape[0]
    copies = [
        pltpu.make_async_copy(ref, table.at[pl.ds(i * blocks, blocks)], sems.at[i])
        for i, ref in enumerate(shards)
    ]
    for copy in copies:
        copy.start()
    table[len(shards) * blocks] = jnp.zeros(table.shape[1:], table.dtype)
    for copy in copies:
        copy.wait()
    lookup(ids_ref, [table], [out_ref], ids_ref.shape[0] // blocks)


def lookup_kernel(ids_ref, *refs):
    count = len(refs) // 2
    lookup(ids_ref, refs[:count], refs[count:], ids_ref.shape[0] // refs[count].shape[0])


def expand_kernel(count, *refs):
    *refs, emb_ref, out_ref = refs
    blocks = refs[0].shape[0]
    block_len = emb_ref.shape[0] // blocks

    def step(b, carry):
        docs = pl.ds(pl.multiple_of(b * block_len, block_len), block_len)
        parts = []
        for at in range(0, len(refs), count):
            total = refs[at][b]
            for ref in refs[at + 1:at + count]:
                total = total + ref[b].astype(jnp.float32)
            parts.append(total.astype(jnp.bfloat16))
        out_ref[:, docs] = lax.dot_general(
            jnp.concatenate(parts, axis=1), emb_ref[docs], (((1,), (1,)), ((), ())),
            preferred_element_type=jnp.float32,
        ).astype(jnp.bfloat16)
        return carry

    lax.fori_loop(0, blocks, step, 0, unroll=UNROLL)


def body(embeddings, quality, probes, neighbors):
    nrow, ncol = lax.axis_size("row"), lax.axis_size("col")
    me = lax.axis_index("row")
    blk_count, list_len = neighbors.shape
    docs, width = embeddings.shape
    nprobe = probes.shape[0]
    group, part = nprobe // GROUPS, width // PARTS
    tiles = blk_count // TILE_BLOCKS
    reduce_bits = [1 << i for i in reversed(range(nrow.bit_length() - 1)) if 1 << i not in (SIDE, NEXT)]
    dests = [0]
    for m in reversed(reduce_bits):
        dests = [d | m for d in dests] + dests
    shards = (0, NEXT, SIDE, NEXT | SIDE)

    def table_ids(lists):
        flat = lists.reshape(-1)
        apart = (flat // blk_count) ^ me
        place = flat % blk_count
        for i, shard in enumerate(shards):
            place = jnp.where(apart == shard, i * blk_count + flat % blk_count, place)
        return jnp.where((apart & ~(NEXT | SIDE)) == 0, place, len(shards) * blk_count)

    qrow = quality[None, :]
    shard_shape = (blk_count, group, part)
    shard_out = jax.ShapeDtypeStruct(shard_shape, jnp.bfloat16)
    vec_out = jax.ShapeDtypeStruct((nprobe, docs), jnp.float32)

    def rows(c):
        return pl.ds(c * group, group)

    def first_sums():
        return pl.pallas_call(
            first_sums_kernel,
            in_specs=[HBM] * 3,
            out_specs=[VMEM] * (GROUPS * PARTS),
            out_shape=[shard_out] * (GROUPS * PARTS),
            scratch_shapes=[
                pltpu.VMEM((nprobe, docs), jnp.float32),
                pltpu.VMEM((1, docs), jnp.float32),
                pltpu.VMEM((tiles, docs // tiles, width), jnp.bfloat16),
                pltpu.SemaphoreType.DMA((tiles + 2,)),
            ],
            compiler_params=params(),
        )(*(pltpu.with_memory_space_constraint(v, pltpu.HBM) for v in (probes, qrow, embeddings)))

    def next_sums(c, pair):
        return pl.pallas_call(
            functools.partial(next_sums_kernel, rows(c)),
            in_specs=[VMEM] * 5,
            out_specs=[VMEM] * PARTS,
            out_shape=[shard_out] * PARTS,
            compiler_params=params(),
        )(*pair, probes, qrow, embeddings)

    def fill(c, held, pair, *others):
        held = [] if held is None else [held]
        return pl.pallas_call(
            functools.partial(fill_kernel, rows(c), bool(others)),
            in_specs=[VMEM] * (4 + len(others)) + [ANY] * len(held),
            out_specs=HBM,
            out_shape=vec_out,
            input_output_aliases={4 + len(others): 0} if held else {},
            scratch_shapes=[pltpu.VMEM((group, docs), jnp.float32), pltpu.SemaphoreType.DMA((4,))],
            compiler_params=params(),
        )(*pair, probes, qrow, *others, *held)

    def combine_far(ids, shards):
        rows_held = len(shards) * blk_count + 1
        return pl.pallas_call(
            table_kernel,
            in_specs=[SMEM] + [VMEM] * len(shards),
            out_specs=[VMEM] * 2,
            out_shape=[shard_out, jax.ShapeDtypeStruct((rows_held, group, part), jnp.bfloat16)],
            scratch_shapes=[pltpu.SemaphoreType.DMA((len(shards),))],
            compiler_params=params(),
        )(ids, *shards)

    def combine(ids, tables, dtype):
        return pl.pallas_call(
            lookup_kernel,
            in_specs=[SMEM] + [VMEM] * len(tables),
            out_specs=[VMEM] * len(tables),
            out_shape=[jax.ShapeDtypeStruct(shard_shape, dtype)] * len(tables),
            compiler_params=params(),
        )(ids, *tables)

    def expand(parts):
        values = [v for values in parts for v in values]
        return pl.pallas_call(
            functools.partial(expand_kernel, len(parts[0])),
            in_specs=[VMEM] * (len(values) + 1),
            out_specs=VMEM,
            out_shape=jax.ShapeDtypeStruct((group, docs), jnp.bfloat16),
            compiler_params=params(),
        )(*values, embeddings)

    def reduce(outgoing):
        arrived = []
        for m in reduce_bits:
            taken = {d ^ m: swap(outgoing.pop(d), "row", nrow, m) for d in list(outgoing) if d & m}
            for d, value in taken.items():
                if d:
                    outgoing[d] = add_bf16(outgoing[d], value)
                else:
                    arrived.append(value)
        return arrived

    token = []

    def take(*values):
        if token:
            values = lax.optimization_barrier(values + (token.pop(),))[:-1]
        return values

    lists = {d: swap(neighbors, "row", nrow, d) if d else neighbors for d in dests}
    first = second = None
    gathered = [[None] * PARTS for _ in range(GROUPS)]
    tables = [[None] * PARTS for _ in range(GROUPS)]
    own = [[None] * PARTS for _ in range(GROUPS)]
    arrived = [[None] * PARTS for _ in range(GROUPS)]
    products = [None] * GROUPS
    halves = [None] * GROUPS
    for word in (word for line in ORDER for word in line.split()):
        c, step, p = ord(word[0]) - ord("A"), word[1], int(word[2:] or 0) - 1
        if step == "l":
            taken = take(*(lists[d] for d in dests))
            ids = dict(zip(dests, lax.optimization_barrier(tuple(table_ids(v) for v in taken))))
            token.append(ids[0])
        elif step == "s":
            if products[c] is None:
                *sums, tied = lax.optimization_barrier((*first_sums(), tuple(lists.values())))
                lists = dict(zip(lists, tied))
                new = [(i // PARTS, i % PARTS, value) for i, value in enumerate(sums)]
            else:
                sums = next_sums(c, take(*products[c]))
                halves[c] = products[c]
                new = [(c, i, value) for i, value in enumerate(sums)]
            token.append(sums[0])
            for c, i, value in new:
                gathered[c][i] = {0: value}
                for m in (NEXT, SIDE):
                    gathered[c][i][m] = swap(value, "row", nrow, m)
        elif step in "fg":
            held = gathered[c][p]
            if step == "g":
                held[NEXT], held[SIDE] = take(held[NEXT], held[SIDE])
            else:
                (held[NEXT],) = take(held[NEXT])
            held[NEXT | SIDE] = swap(held[NEXT], "row", nrow, SIDE)
            token.append(held[NEXT])
        elif step == "o":
            held = take(*(gathered[c][p][m] for m in shards))
            outgoing = {}
            for d in dests[:-1]:
                if outgoing:
                    outgoing[d] = combine(ids[d], [tables[c][p]], jnp.bfloat16)[0]
                else:
                    outgoing[d], tables[c][p] = combine_far(ids[d], held)
            token.append(outgoing[dests[-2]])
            arrived[c][p] = reduce(outgoing)
        elif step == "w":
            tables[c] = list(take(*tables[c]))
            own[c] = combine(ids[0], tables[c], jnp.float32)
            token.append(own[c][0])
        elif step == "z":
            arrived[c][p] = take(*arrived[c][p])
            token.append(arrived[c][p][-1])
        elif step == "e":
            flat = take(*own[c], *(v for values in arrived[c] for v in values))
            later = [flat[PARTS + i * len(reduce_bits):PARTS + (i + 1) * len(reduce_bits)] for i in range(PARTS)]
            value = expand([(flat[i], *later[i]) for i in range(PARTS)])
            products[c] = [value, swap(value, "col", ncol, 1)]
            token.append(value)
        elif step == "c":
            pair = take(*products[c])
            for i in range(1, ncol.bit_length() - 1):
                value = add_bf16(*pair)
                pair = [value, swap(value, "col", ncol, 1 << i)]
            products[c] = pair
            token.append(value)
        elif step == "p":
            first = fill(c, first, take(*halves[c]))
            token.append(first)
        else:
            second = fill(c, second, take(*products[c]), *halves[c])
            token.append(second)
    return first, second


def solution(mesh):
    placed = (P("row", "col"), P("row"), P(None, "row"), P("row", None))
    return jax.shard_map(
        body,
        mesh=mesh,
        in_specs=placed,
        out_specs=(P(None, "row"), P(None, "row")),
        check_vma=False,
    )
```

```python
import functools

import jax
import jax.numpy as jnp
from jax import lax
from jax.experimental import pallas as pl
from jax.experimental.pallas import tpu as pltpu
from jax.sharding import PartitionSpec as P

CORES = 2
GROUPS = 2
PARTS = CORES
TILE_BLOCKS = 8
UNROLL = 32
VMEM_LIMIT = 8 * 1024 * 1024
SIDE, NEXT = 1, 2

ORDER = (
    "As Al Am Bm",
    "Af1 Af2 Ao1 Ao2",
    "Aw Az1 Bg1 Az2",
    "Bg2 Ae Bo1 As",
    "Bo2 Bw Bz1 Ag1",
    "Be Ag2 Ao1 Ao2",
    "Bs Aw Az1 Ap",
    "Bg1 Ae Bf2 Bo1",
    "Bo2 Bp Bw Bz1",
    "Ar Be Au Br",
    "Bu",
)

VMEM = pl.BlockSpec(memory_space=pltpu.VMEM)
SMEM = pl.BlockSpec(memory_space=pltpu.SMEM)
ANY = pl.BlockSpec(memory_space=pl.ANY)
HBM = pl.BlockSpec(memory_space=pltpu.HBM)


def params():
    return pltpu.CompilerParams(vmem_limit_bytes=VMEM_LIMIT)


def swap(value, axis, size, mask):
    return lax.ppermute(value, axis, [(i, i ^ mask) for i in range(size)])


def add_bf16(a, b):
    return (a.astype(jnp.float32) + b.astype(jnp.float32)).astype(jnp.bfloat16)


def add_f32(a, b):
    return a.astype(jnp.float32) + b.astype(jnp.float32)


def block_sum(scaled, emb):
    return jnp.dot(scaled, emb, preferred_element_type=jnp.float32).astype(jnp.bfloat16)


def probe_rows(core, group, size):
    return pl.ds(pl.multiple_of((core * GROUPS + group) * size, size), size)


def first_sums_kernel(core_ref, vec_ref, quality_ref, emb_ref, *refs):
    *sums_refs, vec, quality, emb, sems = refs
    tiles, tile_docs = emb.shape[:2]
    blocks, group, _ = sums_refs[0].shape
    block_len = tiles * tile_docs // blocks
    core = core_ref[0]
    here = [pltpu.make_async_copy(quality_ref, quality, sems.at[tiles])]
    for i in range(CORES * GROUPS):
        rows = probe_rows(core if i < GROUPS else 1 - core, i % GROUPS, group)
        here.append(pltpu.make_async_copy(vec_ref.at[rows], vec.at[pl.ds(i * group, group)], sems.at[tiles + 1 + i]))

    def tile_copy(j):
        docs = pl.ds(pl.multiple_of(j * tile_docs, tile_docs), tile_docs)
        return pltpu.make_async_copy(emb_ref.at[docs], emb.at[j], sems.at[j])

    for copy in here:
        copy.start()
    for j in range(tiles):
        tile_copy(j).start()
    for copy in here:
        copy.wait()

    def step(j, carry):
        tile_copy(j).wait()
        for b in range(blocks // tiles):
            docs = pl.ds(pl.multiple_of(j * tile_docs + b * block_len, block_len), block_len)
            scaled = (vec[:, docs] * quality[:, docs]).astype(jnp.bfloat16)
            sums = block_sum(scaled, emb[j, b * block_len:(b + 1) * block_len])
            for i, ref in enumerate(sums_refs):
                ref[j * (blocks // tiles) + b] = sums[i * group:(i + 1) * group]
        return carry

    lax.fori_loop(0, tiles, step, 0)


def next_sums_kernel(c, core_ref, mine_ref, other_ref, vec_ref, quality_ref, *refs):
    emb_refs, sums_refs = refs[:PARTS], refs[PARTS:]
    blocks, group, _ = sums_refs[0].shape
    block_len = emb_refs[0].shape[0] // blocks
    rows = probe_rows(core_ref[0], c, group)

    def step(b, carry):
        docs = pl.ds(pl.multiple_of(b * block_len, block_len), block_len)
        quality = quality_ref[:, docs]
        value = add_f32(mine_ref[:, docs], other_ref[:, docs]) * quality - vec_ref[rows, docs]
        scaled = (value * quality).astype(jnp.bfloat16)
        for emb_ref, ref in zip(emb_refs, sums_refs):
            ref[b] = block_sum(scaled, emb_ref[docs])
        return carry

    lax.fori_loop(0, blocks, step, 0, unroll=UNROLL)


def fill_kernel(c, second, core_ref, vec_ref, quality_ref, *refs):
    out_ref, out, sems = refs[-3:]
    tiles = sems.shape[1]
    _, group, docs_all = out.shape
    tile_docs = docs_all // tiles
    copies = []
    for i in range(CORES):
        rows = probe_rows(core_ref[0] if i == 0 else 1 - core_ref[0], c, group)
        pair, before = refs[2 * i:2 * i + 2], refs[2 * (CORES + i):2 * (CORES + i) + 2]
        for j in range(tiles):
            docs = pl.ds(j * tile_docs, tile_docs)
            vec, quality = vec_ref[rows, docs], quality_ref[:, docs]
            value = add_f32(pair[0][:, docs], pair[1][:, docs]) * quality
            if second:
                first = add_f32(before[0][:, docs], before[1][:, docs]) * quality - vec
                value = 2.0 * (value - first) - vec
            else:
                value = value - vec
            out[i, :, docs] = value
            copies.append(pltpu.make_async_copy(out.at[i, :, docs], out_ref.at[rows, docs], sems.at[i, j]))
            copies[-1].start()
    for copy in copies:
        copy.wait()


def lookup(ids_ref, tables, outs, entries):
    def step(b, carry):
        places = [ids_ref[b * entries + k] for k in range(entries)]
        for table, ref in zip(tables, outs):
            total = table[places[0]].astype(jnp.float32)
            for place in places[1:]:
                total = total + table[place].astype(jnp.float32)
            ref[b] = total.astype(ref.dtype)
        return carry

    lax.fori_loop(0, outs[0].shape[0], step, 0, unroll=UNROLL)


def table_kernel(ids_ref, *refs):
    *shards, out_ref, table, sems = refs
    blocks = shards[0].shape[0]
    copies = [
        pltpu.make_async_copy(ref, table.at[pl.ds(i * blocks, blocks)], sems.at[i])
        for i, ref in enumerate(shards)
    ]
    for copy in copies:
        copy.start()
    table[len(shards) * blocks] = jnp.zeros(table.shape[1:], table.dtype)
    for copy in copies:
        copy.wait()
    lookup(ids_ref, [table], [out_ref], ids_ref.shape[0] // blocks)


def lookup_kernel(ids_ref, *refs):
    count = len(refs) // 2
    lookup(ids_ref, refs[:count], refs[count:], ids_ref.shape[0] // refs[count].shape[0])


def expand_kernel(count, *refs):
    *refs, out_ref = refs
    values, embs = refs[:-PARTS], refs[-PARTS:]
    blocks = values[0].shape[0]
    block_len = embs[0].shape[0] // blocks

    def step(b, carry):
        docs = pl.ds(pl.multiple_of(b * block_len, block_len), block_len)
        products = None
        for p, emb_ref in enumerate(embs):
            here = values[p * count:(p + 1) * count]
            total = here[0][b]
            for ref in here[1:]:
                total = total + ref[b].astype(jnp.float32)
            product = lax.dot_general(
                total.astype(jnp.bfloat16), emb_ref[docs], (((1,), (1,)), ((), ())),
                preferred_element_type=jnp.float32,
            )
            products = product if products is None else products + product
        out_ref[:, docs] = products.astype(jnp.bfloat16)
        return carry

    lax.fori_loop(0, blocks, step, 0, unroll=UNROLL)


def body(embeddings, quality, probes, neighbors):
    nrow, ncol = lax.axis_size("row"), lax.axis_size("col")
    me = lax.axis_index("row")
    blk_count, list_len = neighbors.shape
    docs, width = embeddings.shape
    nprobe = probes.shape[0]
    group = nprobe // (CORES * GROUPS)
    core = (lax.axis_index("col") % CORES).astype(jnp.int32).reshape(1)
    tiles = blk_count // TILE_BLOCKS
    reduce_bits = [1 << i for i in reversed(range(nrow.bit_length() - 1)) if 1 << i not in (SIDE, NEXT)]
    dests = [0]
    for m in reversed(reduce_bits):
        dests = [d | m for d in dests] + dests
    shards = (0, NEXT, SIDE, NEXT | SIDE)

    def table_ids(lists):
        flat = lists.reshape(-1)
        apart = (flat // blk_count) ^ me
        place = flat % blk_count
        for i, shard in enumerate(shards):
            place = jnp.where(apart == shard, i * blk_count + flat % blk_count, place)
        return jnp.where((apart & ~(NEXT | SIDE)) == 0, place, len(shards) * blk_count)

    qrow = quality[None, :]
    shard_shape = (blk_count, group, width)
    shard_out = jax.ShapeDtypeStruct(shard_shape, jnp.bfloat16)
    vec_out = jax.ShapeDtypeStruct((nprobe, docs), jnp.float32)

    def first_sums():
        return pl.pallas_call(
            first_sums_kernel,
            in_specs=[SMEM] + [HBM] * 3,
            out_specs=[VMEM] * (CORES * GROUPS),
            out_shape=[shard_out] * (CORES * GROUPS),
            scratch_shapes=[
                pltpu.VMEM((nprobe, docs), jnp.float32),
                pltpu.VMEM((1, docs), jnp.float32),
                pltpu.VMEM((tiles, docs // tiles, width), jnp.bfloat16),
                pltpu.SemaphoreType.DMA((tiles + 1 + CORES * GROUPS,)),
            ],
            compiler_params=params(),
        )(core, *(pltpu.with_memory_space_constraint(v, pltpu.HBM) for v in (probes, qrow, embeddings)))

    def next_sums(c, pair):
        return pl.pallas_call(
            functools.partial(next_sums_kernel, c),
            in_specs=[SMEM] + [VMEM] * (4 + PARTS),
            out_specs=[VMEM] * PARTS,
            out_shape=[shard_out] * PARTS,
            compiler_params=params(),
        )(core, *pair, probes, qrow, *embs)

    def fill(c, held, pairs, before=()):
        held = [] if held is None else [held]
        values = [v for pair in (*pairs, *before) for v in pair]
        return pl.pallas_call(
            functools.partial(fill_kernel, c, bool(before)),
            in_specs=[SMEM] + [VMEM] * (2 + len(values)) + [ANY] * len(held),
            out_specs=HBM,
            out_shape=vec_out,
            input_output_aliases={3 + len(values): 0} if held else {},
            scratch_shapes=[pltpu.VMEM((CORES, group, docs), jnp.float32), pltpu.SemaphoreType.DMA((CORES, 4))],
            compiler_params=params(),
        )(core, probes, qrow, *values, *held)

    def combine_far(ids, shards):
        rows_held = len(shards) * blk_count + 1
        return pl.pallas_call(
            table_kernel,
            in_specs=[SMEM] + [VMEM] * len(shards),
            out_specs=[VMEM] * 2,
            out_shape=[shard_out, jax.ShapeDtypeStruct((rows_held, group, width), jnp.bfloat16)],
            scratch_shapes=[pltpu.SemaphoreType.DMA((len(shards),))],
            compiler_params=params(),
        )(ids, *shards)

    def combine(ids, tables, dtype):
        return pl.pallas_call(
            lookup_kernel,
            in_specs=[SMEM] + [VMEM] * len(tables),
            out_specs=[VMEM] * len(tables),
            out_shape=[jax.ShapeDtypeStruct(shard_shape, dtype)] * len(tables),
            compiler_params=params(),
        )(ids, *tables)

    def expand(parts):
        values = [v for values in parts for v in values]
        return pl.pallas_call(
            functools.partial(expand_kernel, len(parts[0])),
            in_specs=[VMEM] * (len(values) + PARTS),
            out_specs=VMEM,
            out_shape=jax.ShapeDtypeStruct((group, docs), jnp.bfloat16),
            compiler_params=params(),
        )(*values, *embs)

    def reduce(outgoing):
        arrived = []
        for m in reduce_bits:
            taken = {d ^ m: swap(outgoing.pop(d), "row", nrow, m) for d in list(outgoing) if d & m}
            for d, value in taken.items():
                if d:
                    outgoing[d] = add_bf16(outgoing[d], value)
                else:
                    arrived.append(value)
        return arrived

    token = []

    def take(*values):
        if token:
            values = lax.optimization_barrier(values + (token.pop(),))[:-1]
        return values

    lists = {d: swap(neighbors, "row", nrow, d) if d else neighbors for d in dests}
    first = second = None
    embs = [embeddings, swap(embeddings, "col", ncol, 1)]
    gathered = [[None] * PARTS for _ in range(GROUPS)]
    tables = [[None] * PARTS for _ in range(GROUPS)]
    own = [[None] * PARTS for _ in range(GROUPS)]
    arrived = [[None] * PARTS for _ in range(GROUPS)]
    pairs = [None] * GROUPS
    before = [None] * GROUPS

    def start_swaps(c, p, value):
        gathered[c][p] = {0: value}
        for m in (NEXT, SIDE):
            gathered[c][p][m] = swap(value, "row", nrow, m)

    def share(c):
        (mine, other), theirs = pairs[c]
        pairs[c] = (take(mine, other), (theirs[0], swap(other, "col", ncol, 1)))

    for word in (word for line in ORDER for word in line.split()):
        c, step, p = ord(word[0]) - ord("A"), word[1], int(word[2:] or 0) - 1
        if step == "l":
            taken = take(*(lists[d] for d in dests))
            ids = dict(zip(dests, lax.optimization_barrier(tuple(table_ids(v) for v in taken))))
            token.append(ids[0])
        elif step == "s":
            if pairs[c] is None:
                *sums, tied = lax.optimization_barrier((*first_sums(), tuple(lists.values())))
                lists = dict(zip(lists, tied))
                token.append(sums[0])
                for i in range(GROUPS):
                    start_swaps(i, 0, sums[i])
                late = [swap(v, "col", ncol, 1) for v in sums[GROUPS:]]
            else:
                share(c)
                before[c] = pairs[c]
                sums = next_sums(c, pairs[c][0])
                token.append(sums[0])
                for i, value in enumerate(sums):
                    start_swaps(c, i, value)
        elif step == "m":
            (value,) = take(late[c])
            token.append(value)
            start_swaps(c, 1, value)
        elif step in "fg":
            held = gathered[c][p]
            if step == "g":
                held[NEXT], held[SIDE] = take(held[NEXT], held[SIDE])
            else:
                (held[NEXT],) = take(held[NEXT])
            held[NEXT | SIDE] = swap(held[NEXT], "row", nrow, SIDE)
            token.append(held[NEXT])
        elif step == "o":
            held = take(*(gathered[c][p][m] for m in shards))
            outgoing = {}
            for d in dests[:-1]:
                if outgoing:
                    outgoing[d] = combine(ids[d], [tables[c][p]], jnp.bfloat16)[0]
                else:
                    outgoing[d], tables[c][p] = combine_far(ids[d], held)
            token.append(outgoing[dests[-2]])
            arrived[c][p] = reduce(outgoing)
        elif step == "w":
            tables[c] = list(take(*tables[c]))
            own[c] = combine(ids[0], tables[c], jnp.float32)
            token.append(own[c][0])
        elif step == "z":
            arrived[c][p] = take(*arrived[c][p])
            token.append(arrived[c][p][-1])
        elif step == "e":
            flat = take(*own[c], *(v for values in arrived[c] for v in values))
            later = [flat[PARTS + i * len(reduce_bits):PARTS + (i + 1) * len(reduce_bits)] for i in range(PARTS)]
            value = expand([(flat[i], *later[i]) for i in range(PARTS)])
            token.append(value)
            other = swap(value, "col", ncol, CORES)
            for i in range(2, ncol.bit_length() - 1):
                value = add_bf16(value, other)
                other = swap(value, "col", ncol, 1 << i)
            pairs[c] = ((value, other), (swap(value, "col", ncol, 1),))
        elif step == "p":
            theirs = take(*before[c][1])
            before[c] = (before[c][0], theirs)
            first = fill(c, first, before[c])
            token.append(first)
        elif step == "r":
            share(c)
            token.append(pairs[c][0][0])
        else:
            theirs = take(*pairs[c][1])
            second = fill(c, second, (pairs[c][0], theirs), before[c])
            token.append(second)
    return first, second


def solution(mesh):
    placed = (P("row", "col"), P("row"), P(None, "row"), P("row", None))
    return jax.shard_map(
        body,
        mesh=mesh,
        in_specs=placed,
        out_specs=(P(None, "row"), P(None, "row")),
        check_vma=False,
    )
```

```python
import functools

import jax
import jax.numpy as jnp
from jax import lax
from jax.experimental import pallas as pl
from jax.experimental.pallas import tpu as pltpu
from jax.sharding import PartitionSpec as P

CORES = 2
GROUPS = 2
PARTS = CORES
TILE_BLOCKS = 8
UNROLL = 16
VMEM_LIMIT = 8 * 1024 * 1024
SIDE, NEXT = 1, 2

ORDER = (
    "As Al Am Bm",
    "Af1 Af2 Ao1 Ao2",
    "Aw Az1 Bg1 Az2",
    "Bg2 Ae Bo1 As",
    "Bo2 Bw Bz1 Ag1",
    "Be Ag2 Ao1 Ao2",
    "Bs Aw Az1 Ap",
    "Bg1 Ae Bf2 Bo1",
    "Bo2 Bp Bw Bz1",
    "Ar Au Be Br",
    "Bu",
)

VMEM = pl.BlockSpec(memory_space=pltpu.VMEM)
SMEM = pl.BlockSpec(memory_space=pltpu.SMEM)
ANY = pl.BlockSpec(memory_space=pl.ANY)
HBM = pl.BlockSpec(memory_space=pltpu.HBM)


def params():
    return pltpu.CompilerParams(vmem_limit_bytes=VMEM_LIMIT)


def swap(value, axis, size, mask):
    return lax.ppermute(value, axis, [(i, i ^ mask) for i in range(size)])


def add_bf16(a, b):
    return (a.astype(jnp.float32) + b.astype(jnp.float32)).astype(jnp.bfloat16)


def add_f32(a, b):
    return a.astype(jnp.float32) + b.astype(jnp.float32)


def block_sum(scaled, emb):
    return jnp.dot(scaled, emb, preferred_element_type=jnp.float32).astype(jnp.bfloat16)


def probe_rows(core, group, size):
    return pl.ds(pl.multiple_of((core * GROUPS + group) * size, size), size)


def first_sums_kernel(core_ref, vec_ref, quality_ref, emb_ref, *refs):
    *sums_refs, vec, quality, emb, sems = refs
    tiles, tile_docs = emb.shape[:2]
    blocks, group, _ = sums_refs[0].shape
    block_len = tiles * tile_docs // blocks
    core = core_ref[0]
    here = [pltpu.make_async_copy(quality_ref, quality, sems.at[tiles])]
    for i in range(CORES * GROUPS):
        rows = probe_rows(core if i < GROUPS else 1 - core, i % GROUPS, group)
        here.append(pltpu.make_async_copy(vec_ref.at[rows], vec.at[pl.ds(i * group, group)], sems.at[tiles + 1 + i]))

    def tile_copy(j):
        docs = pl.ds(pl.multiple_of(j * tile_docs, tile_docs), tile_docs)
        return pltpu.make_async_copy(emb_ref.at[docs], emb.at[j], sems.at[j])

    for copy in here:
        copy.start()
    for j in range(tiles):
        tile_copy(j).start()
    for copy in here:
        copy.wait()

    def step(j, carry):
        tile_copy(j).wait()
        for b in range(blocks // tiles):
            docs = pl.ds(pl.multiple_of(j * tile_docs + b * block_len, block_len), block_len)
            scaled = (vec[:, docs] * quality[:, docs]).astype(jnp.bfloat16)
            sums = block_sum(scaled, emb[j, b * block_len:(b + 1) * block_len])
            for i, ref in enumerate(sums_refs):
                ref[j * (blocks // tiles) + b] = sums[i * group:(i + 1) * group]
        return carry

    lax.fori_loop(0, tiles, step, 0)


def next_sums_kernel(c, core_ref, mine_ref, other_ref, vec_ref, quality_ref, *refs):
    emb_refs, sums_refs = refs[:PARTS], refs[PARTS:]
    blocks, group, _ = sums_refs[0].shape
    block_len = emb_refs[0].shape[0] // blocks
    rows = probe_rows(core_ref[0], c, group)

    def step(b, carry):
        docs = pl.ds(pl.multiple_of(b * block_len, block_len), block_len)
        quality = quality_ref[:, docs]
        value = add_f32(mine_ref[:, docs], other_ref[:, docs]) * quality - vec_ref[rows, docs]
        scaled = (value * quality).astype(jnp.bfloat16)
        for emb_ref, ref in zip(emb_refs, sums_refs):
            ref[b] = block_sum(scaled, emb_ref[docs])
        return carry

    lax.fori_loop(0, blocks, step, 0, unroll=UNROLL)


def fill_kernel(c, second, core_ref, vec_ref, quality_ref, *refs):
    out_ref, out, sems = refs[-3:]
    tiles = sems.shape[1]
    _, group, docs_all = out.shape
    tile_docs = docs_all // tiles
    copies = []
    for i in range(CORES):
        rows = probe_rows(core_ref[0] if i == 0 else 1 - core_ref[0], c, group)
        pair, before = refs[2 * i:2 * i + 2], refs[2 * (CORES + i):2 * (CORES + i) + 2]
        for j in range(tiles):
            docs = pl.ds(j * tile_docs, tile_docs)
            vec, quality = vec_ref[rows, docs], quality_ref[:, docs]
            value = add_f32(pair[0][:, docs], pair[1][:, docs]) * quality
            if second:
                first = add_f32(before[0][:, docs], before[1][:, docs]) * quality - vec
                value = 2.0 * (value - first) - vec
            else:
                value = value - vec
            out[i, :, docs] = value
            copies.append(pltpu.make_async_copy(out.at[i, :, docs], out_ref.at[rows, docs], sems.at[i, j]))
            copies[-1].start()
    for copy in copies:
        copy.wait()


def lookup(ids_ref, tables, outs, entries):
    def step(b, carry):
        places = [ids_ref[b * entries + k] for k in range(entries)]
        for table, ref in zip(tables, outs):
            total = table[places[0]].astype(jnp.float32)
            for place in places[1:]:
                total = total + table[place].astype(jnp.float32)
            ref[b] = total.astype(ref.dtype)
        return carry

    lax.fori_loop(0, outs[0].shape[0], step, 0, unroll=UNROLL)


def table_kernel(ids_ref, *refs):
    *shards, out_ref, table, sems = refs
    blocks = shards[0].shape[0]
    copies = [
        pltpu.make_async_copy(ref, table.at[pl.ds(i * blocks, blocks)], sems.at[i])
        for i, ref in enumerate(shards)
    ]
    for copy in copies:
        copy.start()
    table[len(shards) * blocks] = jnp.zeros(table.shape[1:], table.dtype)
    for copy in copies:
        copy.wait()
    lookup(ids_ref, [table], [out_ref], ids_ref.shape[0] // blocks)


def lookup_kernel(ids_ref, *refs):
    count = len(refs) // 2
    lookup(ids_ref, refs[:count], refs[count:], ids_ref.shape[0] // refs[count].shape[0])


def expand_kernel(count, *refs):
    *refs, out_ref = refs
    values, embs = refs[:-PARTS], refs[-PARTS:]
    blocks = values[0].shape[0]
    block_len = embs[0].shape[0] // blocks

    def step(b, carry):
        docs = pl.ds(pl.multiple_of(b * block_len, block_len), block_len)
        products = None
        for p, emb_ref in enumerate(embs):
            here = values[p * count:(p + 1) * count]
            total = here[0][b]
            for ref in here[1:]:
                total = total + ref[b].astype(jnp.float32)
            product = lax.dot_general(
                total.astype(jnp.bfloat16), emb_ref[docs], (((1,), (1,)), ((), ())),
                preferred_element_type=jnp.float32,
            )
            products = product if products is None else products + product
        out_ref[:, docs] = products.astype(jnp.bfloat16)
        return carry

    lax.fori_loop(0, blocks, step, 0, unroll=UNROLL)


def body(embeddings, quality, probes, neighbors):
    nrow, ncol = lax.axis_size("row"), lax.axis_size("col")
    me = lax.axis_index("row")
    blk_count, list_len = neighbors.shape
    docs, width = embeddings.shape
    nprobe = probes.shape[0]
    group = nprobe // (CORES * GROUPS)
    core = (lax.axis_index("col") % CORES).astype(jnp.int32).reshape(1)
    tiles = blk_count // TILE_BLOCKS
    reduce_bits = [1 << i for i in reversed(range(nrow.bit_length() - 1)) if 1 << i not in (SIDE, NEXT)]
    dests = [0]
    for m in reversed(reduce_bits):
        dests = [d | m for d in dests] + dests
    shards = (0, NEXT, SIDE, NEXT | SIDE)

    def table_ids(lists):
        flat = lists.reshape(-1)
        apart = (flat // blk_count) ^ me
        place = flat % blk_count
        for i, shard in enumerate(shards):
            place = jnp.where(apart == shard, i * blk_count + flat % blk_count, place)
        return jnp.where((apart & ~(NEXT | SIDE)) == 0, place, len(shards) * blk_count)

    qrow = quality[None, :]
    shard_shape = (blk_count, group, width)
    shard_out = jax.ShapeDtypeStruct(shard_shape, jnp.bfloat16)
    vec_out = jax.ShapeDtypeStruct((nprobe, docs), jnp.float32)

    def first_sums():
        return pl.pallas_call(
            first_sums_kernel,
            in_specs=[SMEM] + [HBM] * 3,
            out_specs=[VMEM] * (CORES * GROUPS),
            out_shape=[shard_out] * (CORES * GROUPS),
            scratch_shapes=[
                pltpu.VMEM((nprobe, docs), jnp.float32),
                pltpu.VMEM((1, docs), jnp.float32),
                pltpu.VMEM((tiles, docs // tiles, width), jnp.bfloat16),
                pltpu.SemaphoreType.DMA((tiles + 1 + CORES * GROUPS,)),
            ],
            compiler_params=params(),
        )(core, *(pltpu.with_memory_space_constraint(v, pltpu.HBM) for v in (probes, qrow, embeddings)))

    def next_sums(c, pair):
        return pl.pallas_call(
            functools.partial(next_sums_kernel, c),
            in_specs=[SMEM] + [VMEM] * (4 + PARTS),
            out_specs=[VMEM] * PARTS,
            out_shape=[shard_out] * PARTS,
            compiler_params=params(),
        )(core, *pair, probes, qrow, *embs)

    def fill(c, held, pairs, before=()):
        held = [] if held is None else [held]
        values = [v for pair in (*pairs, *before) for v in pair]
        return pl.pallas_call(
            functools.partial(fill_kernel, c, bool(before)),
            in_specs=[SMEM] + [VMEM] * (2 + len(values)) + [ANY] * len(held),
            out_specs=HBM,
            out_shape=vec_out,
            input_output_aliases={3 + len(values): 0} if held else {},
            scratch_shapes=[pltpu.VMEM((CORES, group, docs), jnp.float32), pltpu.SemaphoreType.DMA((CORES, 4))],
            compiler_params=params(),
        )(core, probes, qrow, *values, *held)

    def combine_far(ids, shards):
        rows_held = len(shards) * blk_count + 1
        return pl.pallas_call(
            table_kernel,
            in_specs=[SMEM] + [VMEM] * len(shards),
            out_specs=[VMEM] * 2,
            out_shape=[shard_out, jax.ShapeDtypeStruct((rows_held, group, width), jnp.bfloat16)],
            scratch_shapes=[pltpu.SemaphoreType.DMA((len(shards),))],
            compiler_params=params(),
        )(ids, *shards)

    def combine(ids, tables, dtype):
        return pl.pallas_call(
            lookup_kernel,
            in_specs=[SMEM] + [VMEM] * len(tables),
            out_specs=[VMEM] * len(tables),
            out_shape=[jax.ShapeDtypeStruct(shard_shape, dtype)] * len(tables),
            compiler_params=params(),
        )(ids, *tables)

    def expand(parts):
        values = [v for values in parts for v in values]
        return pl.pallas_call(
            functools.partial(expand_kernel, len(parts[0])),
            in_specs=[VMEM] * (len(values) + PARTS),
            out_specs=VMEM,
            out_shape=jax.ShapeDtypeStruct((group, docs), jnp.bfloat16),
            compiler_params=params(),
        )(*values, *embs)

    def reduce(outgoing):
        arrived = []
        for m in reduce_bits:
            taken = {d ^ m: swap(outgoing.pop(d), "row", nrow, m) for d in list(outgoing) if d & m}
            for d, value in taken.items():
                if d:
                    outgoing[d] = add_bf16(outgoing[d], value)
                else:
                    arrived.append(value)
        return arrived

    token = []

    def take(*values):
        if token:
            values = lax.optimization_barrier(values + (token.pop(),))[:-1]
        return values

    lists = {d: swap(neighbors, "row", nrow, d) if d else neighbors for d in dests}
    first = second = None
    embs = [embeddings, swap(embeddings, "col", ncol, 1)]
    gathered = [[None] * PARTS for _ in range(GROUPS)]
    tables = [[None] * PARTS for _ in range(GROUPS)]
    own = [[None] * PARTS for _ in range(GROUPS)]
    arrived = [[None] * PARTS for _ in range(GROUPS)]
    pairs = [None] * GROUPS
    before = [None] * GROUPS

    def start_swaps(c, p, value):
        gathered[c][p] = {0: value}
        for m in (NEXT, SIDE):
            gathered[c][p][m] = swap(value, "row", nrow, m)

    def share(c):
        (mine, other), theirs = pairs[c]
        pairs[c] = (take(mine, other), (theirs[0], swap(other, "col", ncol, 1)))

    for word in (word for line in ORDER for word in line.split()):
        c, step, p = ord(word[0]) - ord("A"), word[1], int(word[2:] or 0) - 1
        if step == "l":
            taken = take(*(lists[d] for d in dests))
            ids = dict(zip(dests, lax.optimization_barrier(tuple(table_ids(v) for v in taken))))
            token.append(ids[0])
        elif step == "s":
            if pairs[c] is None:
                *sums, tied = lax.optimization_barrier((*first_sums(), tuple(lists.values())))
                lists = dict(zip(lists, tied))
                token.append(sums[0])
                for i in range(GROUPS):
                    start_swaps(i, 0, sums[i])
                late = [swap(v, "col", ncol, 1) for v in sums[GROUPS:]]
            else:
                share(c)
                before[c] = pairs[c]
                sums = next_sums(c, pairs[c][0])
                token.append(sums[0])
                for i, value in enumerate(sums):
                    start_swaps(c, i, value)
        elif step == "m":
            (value,) = take(late[c])
            token.append(value)
            start_swaps(c, 1, value)
        elif step in "fg":
            held = gathered[c][p]
            if step == "g":
                held[NEXT], held[SIDE] = take(held[NEXT], held[SIDE])
            else:
                (held[NEXT],) = take(held[NEXT])
            held[NEXT | SIDE] = swap(held[NEXT], "row", nrow, SIDE)
            token.append(held[NEXT])
        elif step == "o":
            held = take(*(gathered[c][p][m] for m in shards))
            outgoing = {}
            for d in dests[:-1]:
                if outgoing:
                    outgoing[d] = combine(ids[d], [tables[c][p]], jnp.bfloat16)[0]
                else:
                    outgoing[d], tables[c][p] = combine_far(ids[d], held)
            token.append(outgoing[dests[-2]])
            arrived[c][p] = reduce(outgoing)
        elif step == "w":
            tables[c] = list(take(*tables[c]))
            own[c] = combine(ids[0], tables[c], jnp.float32)
            token.append(own[c][0])
        elif step == "z":
            arrived[c][p] = take(*arrived[c][p])
            token.append(arrived[c][p][-1])
        elif step == "e":
            flat = take(*own[c], *(v for values in arrived[c] for v in values))
            later = [flat[PARTS + i * len(reduce_bits):PARTS + (i + 1) * len(reduce_bits)] for i in range(PARTS)]
            value = expand([(flat[i], *later[i]) for i in range(PARTS)])
            token.append(value)
            other = swap(value, "col", ncol, CORES)
            for i in range(2, ncol.bit_length() - 1):
                value = add_bf16(value, other)
                other = swap(value, "col", ncol, 1 << i)
            pairs[c] = ((value, other), (swap(value, "col", ncol, 1),))
        elif step == "p":
            theirs = take(*before[c][1])
            before[c] = (before[c][0], theirs)
            first = fill(c, first, before[c])
            token.append(first)
        elif step == "r":
            share(c)
            token.append(pairs[c][0][0])
        else:
            theirs = take(*pairs[c][1])
            second = fill(c, second, (pairs[c][0], theirs), before[c])
            token.append(second)
    return first, second


def solution(mesh):
    placed = (P("row", "col"), P("row"), P(None, "row"), P("row", None))
    return jax.shard_map(
        body,
        mesh=mesh,
        in_specs=placed,
        out_specs=(P(None, "row"), P(None, "row")),
        check_vma=False,
    )
```

```python
import functools

import jax
import jax.numpy as jnp
from jax import lax
from jax.experimental import pallas as pl
from jax.experimental.pallas import tpu as pltpu
from jax.sharding import PartitionSpec as P

CORES = 2
GROUPS = 2
PARTS = CORES
TILE_BLOCKS = 8
UNROLL = 32
VMEM_LIMIT = 8 * 1024 * 1024
SIDE, NEXT = 1, 2

ORDER = (
    "As Al Am Bm",
    "Af1 Af2 Ao1 Ao2",
    "Aw Ak Az1 Bg1",
    "Az2 Bg2 Ae Bo1",
    "As Bo2 Bw Bz1",
    "Ag1 Be Ag2 Ao1",
    "Ao2 Bs Aw Az1",
    "Ap Bg1 Ae Bf2",
    "Bo1 Bo2 Bp Bw",
    "Bz1 Ar Au Be",
    "Br Bu",
)

VMEM = pl.BlockSpec(memory_space=pltpu.VMEM)
SMEM = pl.BlockSpec(memory_space=pltpu.SMEM)
ANY = pl.BlockSpec(memory_space=pl.ANY)
HBM = pl.BlockSpec(memory_space=pltpu.HBM)


def params():
    return pltpu.CompilerParams(vmem_limit_bytes=VMEM_LIMIT)


def swap(value, axis, size, mask):
    return lax.ppermute(value, axis, [(i, i ^ mask) for i in range(size)])


def add_bf16(a, b):
    return (a.astype(jnp.float32) + b.astype(jnp.float32)).astype(jnp.bfloat16)


def add_f32(a, b):
    return a.astype(jnp.float32) + b.astype(jnp.float32)


def block_sum(scaled, emb):
    return jnp.dot(scaled, emb, preferred_element_type=jnp.float32).astype(jnp.bfloat16)


def probe_rows(core, group, size):
    return pl.ds(pl.multiple_of((core * GROUPS + group) * size, size), size)


def first_sums_kernel(core_ref, vec_ref, quality_ref, emb_ref, *refs):
    *sums_refs, vec, quality, emb, sems = refs
    tiles, tile_docs = emb.shape[:2]
    blocks, group, _ = sums_refs[0].shape
    block_len = tiles * tile_docs // blocks
    core = core_ref[0]
    here = [pltpu.make_async_copy(quality_ref, quality, sems.at[tiles])]
    for i in range(CORES * GROUPS):
        rows = probe_rows(core if i < GROUPS else 1 - core, i % GROUPS, group)
        here.append(pltpu.make_async_copy(vec_ref.at[rows], vec.at[pl.ds(i * group, group)], sems.at[tiles + 1 + i]))

    def tile_copy(j):
        docs = pl.ds(pl.multiple_of(j * tile_docs, tile_docs), tile_docs)
        return pltpu.make_async_copy(emb_ref.at[docs], emb.at[j], sems.at[j])

    for copy in here:
        copy.start()
    for j in range(tiles):
        tile_copy(j).start()
    for copy in here:
        copy.wait()

    def step(j, carry):
        tile_copy(j).wait()
        for b in range(blocks // tiles):
            docs = pl.ds(pl.multiple_of(j * tile_docs + b * block_len, block_len), block_len)
            scaled = (vec[:, docs] * quality[:, docs]).astype(jnp.bfloat16)
            sums = block_sum(scaled, emb[j, b * block_len:(b + 1) * block_len])
            for i, ref in enumerate(sums_refs):
                ref[j * (blocks // tiles) + b] = sums[i * group:(i + 1) * group]
        return carry

    lax.fori_loop(0, tiles, step, 0)


def hold_kernel(src_ref, out_ref, sem):
    copy = pltpu.make_async_copy(src_ref, out_ref, sem)
    copy.start()
    copy.wait()


def next_sums_kernel(c, core_ref, mine_ref, other_ref, vec_ref, quality_ref, *refs):
    emb_refs, sums_refs = refs[:PARTS], refs[PARTS:]
    blocks, group, _ = sums_refs[0].shape
    block_len = emb_refs[0].shape[0] // blocks
    rows = probe_rows(core_ref[0], c, group)

    def step(b, carry):
        docs = pl.ds(pl.multiple_of(b * block_len, block_len), block_len)
        quality = quality_ref[:, docs]
        value = add_f32(mine_ref[:, docs], other_ref[:, docs]) * quality - vec_ref[rows, docs]
        scaled = (value * quality).astype(jnp.bfloat16)
        for emb_ref, ref in zip(emb_refs, sums_refs):
            ref[b] = block_sum(scaled, emb_ref[docs])
        return carry

    lax.fori_loop(0, blocks, step, 0, unroll=UNROLL)


def fill_kernel(c, second, core_ref, vec_ref, quality_ref, *refs):
    out_ref, out, sems = refs[-3:]
    tiles = sems.shape[1]
    _, group, docs_all = out.shape
    tile_docs = docs_all // tiles
    copies = []
    for i in range(CORES):
        rows = probe_rows(core_ref[0] if i == 0 else 1 - core_ref[0], c, group)
        pair, before = refs[2 * i:2 * i + 2], refs[2 * (CORES + i):2 * (CORES + i) + 2]
        for j in range(tiles):
            docs = pl.ds(j * tile_docs, tile_docs)
            vec, quality = vec_ref[rows, docs], quality_ref[:, docs]
            value = add_f32(pair[0][:, docs], pair[1][:, docs]) * quality
            if second:
                first = add_f32(before[0][:, docs], before[1][:, docs]) * quality - vec
                value = 2.0 * (value - first) - vec
            else:
                value = value - vec
            out[i, :, docs] = value
            copies.append(pltpu.make_async_copy(out.at[i, :, docs], out_ref.at[rows, docs], sems.at[i, j]))
            copies[-1].start()
    for copy in copies:
        copy.wait()


def lookup(ids_ref, tables, outs, entries):
    def step(b, carry):
        places = [ids_ref[b * entries + k] for k in range(entries)]
        for table, ref in zip(tables, outs):
            total = table[places[0]].astype(jnp.float32)
            for place in places[1:]:
                total = total + table[place].astype(jnp.float32)
            ref[b] = total.astype(ref.dtype)
        return carry

    lax.fori_loop(0, outs[0].shape[0], step, 0, unroll=UNROLL)


def table_kernel(ids_ref, *refs):
    *shards, out_ref, table, sems = refs
    blocks = shards[0].shape[0]
    copies = [
        pltpu.make_async_copy(ref, table.at[pl.ds(i * blocks, blocks)], sems.at[i])
        for i, ref in enumerate(shards)
    ]
    for copy in copies:
        copy.start()
    table[len(shards) * blocks] = jnp.zeros(table.shape[1:], table.dtype)
    for copy in copies:
        copy.wait()
    lookup(ids_ref, [table], [out_ref], ids_ref.shape[0] // blocks)


def lookup_kernel(ids_ref, *refs):
    count = len(refs) // 2
    lookup(ids_ref, refs[:count], refs[count:], ids_ref.shape[0] // refs[count].shape[0])


def expand_kernel(count, *refs):
    *refs, out_ref = refs
    values, embs = refs[:-PARTS], refs[-PARTS:]
    blocks = values[0].shape[0]
    block_len = embs[0].shape[0] // blocks

    def step(b, carry):
        docs = pl.ds(pl.multiple_of(b * block_len, block_len), block_len)
        products = None
        for p, emb_ref in enumerate(embs):
            here = values[p * count:(p + 1) * count]
            total = here[0][b]
            for ref in here[1:]:
                total = total + ref[b].astype(jnp.float32)
            product = lax.dot_general(
                total.astype(jnp.bfloat16), emb_ref[docs], (((1,), (1,)), ((), ())),
                preferred_element_type=jnp.float32,
            )
            products = product if products is None else products + product
        out_ref[:, docs] = products.astype(jnp.bfloat16)
        return carry

    lax.fori_loop(0, blocks, step, 0, unroll=UNROLL)


def body(embeddings, quality, probes, neighbors):
    nrow, ncol = lax.axis_size("row"), lax.axis_size("col")
    me = lax.axis_index("row")
    blk_count, list_len = neighbors.shape
    docs, width = embeddings.shape
    nprobe = probes.shape[0]
    group = nprobe // (CORES * GROUPS)
    core = (lax.axis_index("col") % CORES).astype(jnp.int32).reshape(1)
    tiles = blk_count // TILE_BLOCKS
    reduce_bits = [1 << i for i in reversed(range(nrow.bit_length() - 1)) if 1 << i not in (SIDE, NEXT)]
    dests = [0]
    for m in reversed(reduce_bits):
        dests = [d | m for d in dests] + dests
    shards = (0, NEXT, SIDE, NEXT | SIDE)

    def table_ids(lists):
        flat = lists.reshape(-1)
        apart = (flat // blk_count) ^ me
        place = flat % blk_count
        for i, shard in enumerate(shards):
            place = jnp.where(apart == shard, i * blk_count + flat % blk_count, place)
        return jnp.where((apart & ~(NEXT | SIDE)) == 0, place, len(shards) * blk_count)

    qrow = quality[None, :]
    shard_shape = (blk_count, group, width)
    shard_out = jax.ShapeDtypeStruct(shard_shape, jnp.bfloat16)
    vec_out = jax.ShapeDtypeStruct((nprobe, docs), jnp.float32)

    def first_sums():
        return pl.pallas_call(
            first_sums_kernel,
            in_specs=[SMEM] + [HBM] * 3,
            out_specs=[VMEM] * (CORES * GROUPS),
            out_shape=[shard_out] * (CORES * GROUPS),
            scratch_shapes=[
                pltpu.VMEM((nprobe, docs), jnp.float32),
                pltpu.VMEM((1, docs), jnp.float32),
                pltpu.VMEM((tiles, docs // tiles, width), jnp.bfloat16),
                pltpu.SemaphoreType.DMA((tiles + 1 + CORES * GROUPS,)),
            ],
            compiler_params=params(),
        )(core, *(pltpu.with_memory_space_constraint(v, pltpu.HBM) for v in (probes, qrow, embeddings)))

    def hold(value):
        return pl.pallas_call(
            hold_kernel,
            in_specs=[ANY],
            out_specs=VMEM,
            out_shape=jax.ShapeDtypeStruct(value.shape, value.dtype),
            scratch_shapes=[pltpu.SemaphoreType.DMA],
            compiler_params=params(),
        )(value)

    def next_sums(c, pair):
        return pl.pallas_call(
            functools.partial(next_sums_kernel, c),
            in_specs=[SMEM] + [VMEM] * (4 + PARTS),
            out_specs=[VMEM] * PARTS,
            out_shape=[shard_out] * PARTS,
            compiler_params=params(),
        )(core, *pair, probes, qrow, *embs)

    def fill(c, held, pairs, before=()):
        held = [] if held is None else [held]
        values = [v for pair in (*pairs, *before) for v in pair]
        return pl.pallas_call(
            functools.partial(fill_kernel, c, bool(before)),
            in_specs=[SMEM] + [VMEM] * (2 + len(values)) + [ANY] * len(held),
            out_specs=HBM,
            out_shape=vec_out,
            input_output_aliases={3 + len(values): 0} if held else {},
            scratch_shapes=[pltpu.VMEM((CORES, group, docs), jnp.float32), pltpu.SemaphoreType.DMA((CORES, 4))],
            compiler_params=params(),
        )(core, probes, qrow, *values, *held)

    def combine_far(ids, shards):
        rows_held = len(shards) * blk_count + 1
        return pl.pallas_call(
            table_kernel,
            in_specs=[SMEM] + [VMEM] * len(shards),
            out_specs=[VMEM] * 2,
            out_shape=[shard_out, jax.ShapeDtypeStruct((rows_held, group, width), jnp.bfloat16)],
            scratch_shapes=[pltpu.SemaphoreType.DMA((len(shards),))],
            compiler_params=params(),
        )(ids, *shards)

    def combine(ids, tables, dtype):
        return pl.pallas_call(
            lookup_kernel,
            in_specs=[SMEM] + [VMEM] * len(tables),
            out_specs=[VMEM] * len(tables),
            out_shape=[jax.ShapeDtypeStruct(shard_shape, dtype)] * len(tables),
            compiler_params=params(),
        )(ids, *tables)

    def expand(parts):
        values = [v for values in parts for v in values]
        return pl.pallas_call(
            functools.partial(expand_kernel, len(parts[0])),
            in_specs=[VMEM] * (len(values) + PARTS),
            out_specs=VMEM,
            out_shape=jax.ShapeDtypeStruct((group, docs), jnp.bfloat16),
            compiler_params=params(),
        )(*values, *embs)

    def reduce(outgoing):
        arrived = []
        for m in reduce_bits:
            taken = {d ^ m: swap(outgoing.pop(d), "row", nrow, m) for d in list(outgoing) if d & m}
            for d, value in taken.items():
                if d:
                    outgoing[d] = add_bf16(outgoing[d], value)
                else:
                    arrived.append(value)
        return arrived

    token = []

    def take(*values):
        if token:
            values = lax.optimization_barrier(values + (token.pop(),))[:-1]
        return values

    lists = {d: swap(neighbors, "row", nrow, d) if d else neighbors for d in dests}
    first = second = None
    embs = [embeddings, swap(embeddings, "col", ncol, 1)]
    gathered = [[None] * PARTS for _ in range(GROUPS)]
    tables = [[None] * PARTS for _ in range(GROUPS)]
    own = [[None] * PARTS for _ in range(GROUPS)]
    arrived = [[None] * PARTS for _ in range(GROUPS)]
    pairs = [None] * GROUPS
    before = [None] * GROUPS

    def start_swaps(c, p, value):
        gathered[c][p] = {0: value}
        for m in (NEXT, SIDE):
            gathered[c][p][m] = swap(value, "row", nrow, m)

    def share(c):
        (mine, other), theirs = pairs[c]
        pairs[c] = (take(mine, other), (theirs[0], swap(other, "col", ncol, 1)))

    for word in (word for line in ORDER for word in line.split()):
        c, step, p = ord(word[0]) - ord("A"), word[1], int(word[2:] or 0) - 1
        if step == "l":
            taken = take(*(lists[d] for d in dests))
            ids = dict(zip(dests, lax.optimization_barrier(tuple(table_ids(v) for v in taken))))
            token.append(ids[0])
        elif step == "s":
            if pairs[c] is None:
                *sums, tied = lax.optimization_barrier((*first_sums(), tuple(lists.values())))
                lists = dict(zip(lists, tied))
                token.append(sums[0])
                for i in range(GROUPS):
                    start_swaps(i, 0, sums[i])
                late = [swap(v, "col", ncol, 1) for v in sums[GROUPS:]]
            else:
                share(c)
                before[c] = pairs[c]
                sums = next_sums(c, pairs[c][0])
                token.append(sums[0])
                for i, value in enumerate(sums):
                    start_swaps(c, i, value)
        elif step == "m":
            (value,) = take(late[c])
            token.append(value)
            start_swaps(c, 1, value)
        elif step == "k":
            embs[1] = hold(*take(embs[1]))
            token.append(embs[1])
        elif step in "fg":
            held = gathered[c][p]
            if step == "g":
                held[NEXT], held[SIDE] = take(held[NEXT], held[SIDE])
            else:
                (held[NEXT],) = take(held[NEXT])
            held[NEXT | SIDE] = swap(held[NEXT], "row", nrow, SIDE)
            token.append(held[NEXT])
        elif step == "o":
            held = take(*(gathered[c][p][m] for m in shards))
            outgoing = {}
            for d in dests[:-1]:
                if outgoing:
                    outgoing[d] = combine(ids[d], [tables[c][p]], jnp.bfloat16)[0]
                else:
                    outgoing[d], tables[c][p] = combine_far(ids[d], held)
            token.append(outgoing[dests[-2]])
            arrived[c][p] = reduce(outgoing)
        elif step == "w":
            tables[c] = list(take(*tables[c]))
            own[c] = combine(ids[0], tables[c], jnp.float32)
            token.append(own[c][0])
        elif step == "z":
            arrived[c][p] = take(*arrived[c][p])
            token.append(arrived[c][p][-1])
        elif step == "e":
            flat = take(*own[c], *(v for values in arrived[c] for v in values))
            later = [flat[PARTS + i * len(reduce_bits):PARTS + (i + 1) * len(reduce_bits)] for i in range(PARTS)]
            value = expand([(flat[i], *later[i]) for i in range(PARTS)])
            token.append(value)
            other = swap(value, "col", ncol, CORES)
            for i in range(2, ncol.bit_length() - 1):
                value = add_bf16(value, other)
                other = swap(value, "col", ncol, 1 << i)
            pairs[c] = ((value, other), (swap(value, "col", ncol, 1),))
        elif step == "p":
            theirs = take(*before[c][1])
            before[c] = (before[c][0], theirs)
            first = fill(c, first, before[c])
            token.append(first)
        elif step == "r":
            share(c)
            token.append(pairs[c][0][0])
        else:
            theirs = take(*pairs[c][1])
            second = fill(c, second, (pairs[c][0], theirs), before[c])
            token.append(second)
    return first, second


def solution(mesh):
    placed = (P("row", "col"), P("row"), P(None, "row"), P("row", None))
    return jax.shard_map(
        body,
        mesh=mesh,
        in_specs=placed,
        out_specs=(P(None, "row"), P(None, "row")),
        check_vma=False,
    )
```

```python
import functools

import jax
import jax.numpy as jnp
from jax import lax
from jax.experimental import pallas as pl
from jax.experimental.pallas import tpu as pltpu
from jax.sharding import PartitionSpec as P

CORES = 2
GROUPS = 2
PARTS = CORES
TILE_BLOCKS = 8
UNROLL = 32
VMEM_LIMIT = 8 * 1024 * 1024
SIDE, NEXT = 1, 2

ORDER = (
    "As Al Am Bm",
    "Af1 Af2 Ao1 Ak",
    "Ao2 Aw Ae1 Bg1",
    "Az2 Bg2 Ae2 Bo1",
    "As1 As2 Bo2 Bw",
    "Be1 Ag1 Bz2 Be2",
    "Ag2 Ao1 Bs1 Ap",
    "Ao2 Bs2 Aw Ae1",
    "Bg1 Bf2 Bo1 Ae2",
    "Bo2 Bp Bw Be1",
    "Ar Au Be2 Br",
    "Bu",
)

VMEM = pl.BlockSpec(memory_space=pltpu.VMEM)
SMEM = pl.BlockSpec(memory_space=pltpu.SMEM)
ANY = pl.BlockSpec(memory_space=pl.ANY)
HBM = pl.BlockSpec(memory_space=pltpu.HBM)


def params():
    return pltpu.CompilerParams(vmem_limit_bytes=VMEM_LIMIT)


def swap(value, axis, size, mask):
    return lax.ppermute(value, axis, [(i, i ^ mask) for i in range(size)])


def add_bf16(a, b):
    return (a.astype(jnp.float32) + b.astype(jnp.float32)).astype(jnp.bfloat16)


def add_f32(a, b):
    return a.astype(jnp.float32) + b.astype(jnp.float32)


def block_sum(scaled, emb):
    return jnp.dot(scaled, emb, preferred_element_type=jnp.float32).astype(jnp.bfloat16)


def probe_rows(core, group, size):
    return pl.ds(pl.multiple_of((core * GROUPS + group) * size, size), size)


def first_sums_kernel(core_ref, vec_ref, quality_ref, emb_ref, *refs):
    *sums_refs, vec, quality, emb, sems = refs
    tiles, tile_docs = emb.shape[:2]
    blocks, group, _ = sums_refs[0].shape
    block_len = tiles * tile_docs // blocks
    core = core_ref[0]
    here = [pltpu.make_async_copy(quality_ref, quality, sems.at[tiles])]
    for i in range(CORES * GROUPS):
        rows = probe_rows(core if i < GROUPS else 1 - core, i % GROUPS, group)
        here.append(pltpu.make_async_copy(vec_ref.at[rows], vec.at[pl.ds(i * group, group)], sems.at[tiles + 1 + i]))

    def tile_copy(j):
        docs = pl.ds(pl.multiple_of(j * tile_docs, tile_docs), tile_docs)
        return pltpu.make_async_copy(emb_ref.at[docs], emb.at[j], sems.at[j])

    for copy in here:
        copy.start()
    for j in range(tiles):
        tile_copy(j).start()
    for copy in here:
        copy.wait()

    def step(j, carry):
        tile_copy(j).wait()
        for b in range(blocks // tiles):
            docs = pl.ds(pl.multiple_of(j * tile_docs + b * block_len, block_len), block_len)
            scaled = (vec[:, docs] * quality[:, docs]).astype(jnp.bfloat16)
            sums = block_sum(scaled, emb[j, b * block_len:(b + 1) * block_len])
            for i, ref in enumerate(sums_refs):
                ref[j * (blocks // tiles) + b] = sums[i * group:(i + 1) * group]
        return carry

    lax.fori_loop(0, tiles, step, 0)


def hold_kernel(src_ref, out_ref, sem):
    copy = pltpu.make_async_copy(src_ref, out_ref, sem)
    copy.start()
    copy.wait()


def next_sums_kernel(c, core_ref, mine_ref, other_ref, vec_ref, quality_ref, emb_ref, sums_ref):
    blocks, group, _ = sums_ref.shape
    block_len = emb_ref.shape[0] // blocks
    rows = probe_rows(core_ref[0], c, group)

    def step(b, carry):
        docs = pl.ds(pl.multiple_of(b * block_len, block_len), block_len)
        quality = quality_ref[:, docs]
        value = add_f32(mine_ref[:, docs], other_ref[:, docs]) * quality - vec_ref[rows, docs]
        sums_ref[b] = block_sum((value * quality).astype(jnp.bfloat16), emb_ref[docs])
        return carry

    lax.fori_loop(0, blocks, step, 0, unroll=UNROLL)


def fill_kernel(c, second, core_ref, vec_ref, quality_ref, *refs):
    out_ref, out, sems = refs[-3:]
    tiles = sems.shape[1]
    _, group, docs_all = out.shape
    tile_docs = docs_all // tiles
    copies = []
    for i in range(CORES):
        rows = probe_rows(core_ref[0] if i == 0 else 1 - core_ref[0], c, group)
        pair, before = refs[2 * i:2 * i + 2], refs[2 * (CORES + i):2 * (CORES + i) + 2]
        for j in range(tiles):
            docs = pl.ds(j * tile_docs, tile_docs)
            vec, quality = vec_ref[rows, docs], quality_ref[:, docs]
            value = add_f32(pair[0][:, docs], pair[1][:, docs]) * quality
            if second:
                first = add_f32(before[0][:, docs], before[1][:, docs]) * quality - vec
                value = 2.0 * (value - first) - vec
            else:
                value = value - vec
            out[i, :, docs] = value
            copies.append(pltpu.make_async_copy(out.at[i, :, docs], out_ref.at[rows, docs], sems.at[i, j]))
            copies[-1].start()
    for copy in copies:
        copy.wait()


def lookup(ids_ref, tables, outs, entries):
    def step(b, carry):
        places = [ids_ref[b * entries + k] for k in range(entries)]
        for table, ref in zip(tables, outs):
            total = table[places[0]].astype(jnp.float32)
            for place in places[1:]:
                total = total + table[place].astype(jnp.float32)
            ref[b] = total.astype(ref.dtype)
        return carry

    lax.fori_loop(0, outs[0].shape[0], step, 0, unroll=UNROLL)


def table_kernel(ids_ref, *refs):
    *shards, out_ref, table, sems = refs
    blocks = shards[0].shape[0]
    copies = [
        pltpu.make_async_copy(ref, table.at[pl.ds(i * blocks, blocks)], sems.at[i])
        for i, ref in enumerate(shards)
    ]
    for copy in copies:
        copy.start()
    table[len(shards) * blocks] = jnp.zeros(table.shape[1:], table.dtype)
    for copy in copies:
        copy.wait()
    lookup(ids_ref, [table], [out_ref], ids_ref.shape[0] // blocks)


def lookup_kernel(ids_ref, *refs):
    count = len(refs) // 2
    lookup(ids_ref, refs[:count], refs[count:], ids_ref.shape[0] // refs[count].shape[0])


def expand_kernel(*refs):
    own_ref, *arrived_refs, emb_ref, out_ref = refs
    held = arrived_refs.pop() if len(arrived_refs[-1].shape) == 2 else None
    blocks = own_ref.shape[0]
    block_len = emb_ref.shape[0] // blocks

    def step(b, carry):
        docs = pl.ds(pl.multiple_of(b * block_len, block_len), block_len)
        total = own_ref[b]
        for ref in arrived_refs:
            total = total + ref[b].astype(jnp.float32)
        products = lax.dot_general(
            total.astype(jnp.bfloat16), emb_ref[docs], (((1,), (1,)), ((), ())),
            preferred_element_type=jnp.float32,
        )
        if held is not None:
            products = products + held[:, docs]
        out_ref[:, docs] = products.astype(out_ref.dtype)
        return carry

    lax.fori_loop(0, blocks, step, 0, unroll=UNROLL)


def body(embeddings, quality, probes, neighbors):
    nrow, ncol = lax.axis_size("row"), lax.axis_size("col")
    me = lax.axis_index("row")
    blk_count, list_len = neighbors.shape
    docs, width = embeddings.shape
    nprobe = probes.shape[0]
    group = nprobe // (CORES * GROUPS)
    core = (lax.axis_index("col") % CORES).astype(jnp.int32).reshape(1)
    tiles = blk_count // TILE_BLOCKS
    reduce_bits = [1 << i for i in reversed(range(nrow.bit_length() - 1)) if 1 << i not in (SIDE, NEXT)]
    dests = [0]
    for m in reversed(reduce_bits):
        dests = [d | m for d in dests] + dests
    shards = (0, NEXT, SIDE, NEXT | SIDE)

    def table_ids(lists):
        flat = lists.reshape(-1)
        apart = (flat // blk_count) ^ me
        place = flat % blk_count
        for i, shard in enumerate(shards):
            place = jnp.where(apart == shard, i * blk_count + flat % blk_count, place)
        return jnp.where((apart & ~(NEXT | SIDE)) == 0, place, len(shards) * blk_count)

    qrow = quality[None, :]
    shard_shape = (blk_count, group, width)
    shard_out = jax.ShapeDtypeStruct(shard_shape, jnp.bfloat16)
    vec_out = jax.ShapeDtypeStruct((nprobe, docs), jnp.float32)

    def first_sums():
        return pl.pallas_call(
            first_sums_kernel,
            in_specs=[SMEM] + [HBM] * 3,
            out_specs=[VMEM] * (CORES * GROUPS),
            out_shape=[shard_out] * (CORES * GROUPS),
            scratch_shapes=[
                pltpu.VMEM((nprobe, docs), jnp.float32),
                pltpu.VMEM((1, docs), jnp.float32),
                pltpu.VMEM((tiles, docs // tiles, width), jnp.bfloat16),
                pltpu.SemaphoreType.DMA((tiles + 1 + CORES * GROUPS,)),
            ],
            compiler_params=params(),
        )(core, *(pltpu.with_memory_space_constraint(v, pltpu.HBM) for v in (probes, qrow, embeddings)))

    def hold(value):
        return pl.pallas_call(
            hold_kernel,
            in_specs=[ANY],
            out_specs=VMEM,
            out_shape=jax.ShapeDtypeStruct(value.shape, value.dtype),
            scratch_shapes=[pltpu.SemaphoreType.DMA],
            compiler_params=params(),
        )(value)

    def next_sums(c, p, pair):
        return pl.pallas_call(
            functools.partial(next_sums_kernel, c),
            in_specs=[SMEM] + [VMEM] * 5,
            out_specs=VMEM,
            out_shape=shard_out,
            compiler_params=params(),
        )(core, *pair, probes, qrow, embs[p])

    def fill(c, held, pairs, before=()):
        held = [] if held is None else [held]
        values = [v for pair in (*pairs, *before) for v in pair]
        return pl.pallas_call(
            functools.partial(fill_kernel, c, bool(before)),
            in_specs=[SMEM] + [VMEM] * (2 + len(values)) + [ANY] * len(held),
            out_specs=HBM,
            out_shape=vec_out,
            input_output_aliases={3 + len(values): 0} if held else {},
            scratch_shapes=[pltpu.VMEM((CORES, group, docs), jnp.float32), pltpu.SemaphoreType.DMA((CORES, 4))],
            compiler_params=params(),
        )(core, probes, qrow, *values, *held)

    def combine_far(ids, shards):
        rows_held = len(shards) * blk_count + 1
        return pl.pallas_call(
            table_kernel,
            in_specs=[SMEM] + [VMEM] * len(shards),
            out_specs=[VMEM] * 2,
            out_shape=[shard_out, jax.ShapeDtypeStruct((rows_held, group, width), jnp.bfloat16)],
            scratch_shapes=[pltpu.SemaphoreType.DMA((len(shards),))],
            compiler_params=params(),
        )(ids, *shards)

    def combine(ids, tables, dtype):
        return pl.pallas_call(
            lookup_kernel,
            in_specs=[SMEM] + [VMEM] * len(tables),
            out_specs=[VMEM] * len(tables),
            out_shape=[jax.ShapeDtypeStruct(shard_shape, dtype)] * len(tables),
            compiler_params=params(),
        )(ids, *tables)

    def expand(p, own, arrived, held):
        values = [own, *arrived] + ([held] if p else [])
        return pl.pallas_call(
            expand_kernel,
            in_specs=[VMEM] * (len(values) + 1),
            out_specs=VMEM,
            out_shape=jax.ShapeDtypeStruct((group, docs), jnp.bfloat16 if p + 1 == PARTS else jnp.float32),
            compiler_params=params(),
        )(*values, embs[p])

    def reduce(outgoing):
        arrived = []
        for m in reduce_bits:
            taken = {d ^ m: swap(outgoing.pop(d), "row", nrow, m) for d in list(outgoing) if d & m}
            for d, value in taken.items():
                if d:
                    outgoing[d] = add_bf16(outgoing[d], value)
                else:
                    arrived.append(value)
        return arrived

    token = []

    def take(*values):
        if token:
            values = lax.optimization_barrier(values + (token.pop(),))[:-1]
        return values

    lists = {d: swap(neighbors, "row", nrow, d) if d else neighbors for d in dests}
    first = second = None
    embs = [embeddings, swap(embeddings, "col", ncol, 1)]
    gathered = [[None] * PARTS for _ in range(GROUPS)]
    tables = [[None] * PARTS for _ in range(GROUPS)]
    own = [[None] * PARTS for _ in range(GROUPS)]
    arrived = [[None] * PARTS for _ in range(GROUPS)]
    products = [None] * GROUPS
    pairs = [None] * GROUPS
    before = [None] * GROUPS

    def start_swaps(c, p, value):
        gathered[c][p] = {0: value}
        for m in (NEXT, SIDE):
            gathered[c][p][m] = swap(value, "row", nrow, m)

    def share(c):
        (mine, other), theirs = pairs[c]
        pairs[c] = (take(mine, other), (theirs[0], swap(other, "col", ncol, 1)))

    for word in (word for line in ORDER for word in line.split()):
        c, step, p = ord(word[0]) - ord("A"), word[1], int(word[2:] or 0) - 1
        if step == "l":
            taken = take(*(lists[d] for d in dests))
            ids = dict(zip(dests, lax.optimization_barrier(tuple(table_ids(v) for v in taken))))
            token.append(ids[0])
        elif step == "s":
            if pairs[c] is None:
                *sums, tied = lax.optimization_barrier((*first_sums(), tuple(lists.values())))
                lists = dict(zip(lists, tied))
                token.append(sums[0])
                for i in range(GROUPS):
                    start_swaps(i, 0, sums[i])
                late = [swap(v, "col", ncol, 1) for v in sums[GROUPS:]]
            else:
                if p == 0:
                    share(c)
                    before[c] = pairs[c]
                    pair = pairs[c][0]
                else:
                    pair = take(*pairs[c][0])
                value = next_sums(c, p, pair)
                token.append(value)
                start_swaps(c, p, value)
        elif step == "m":
            (value,) = take(late[c])
            token.append(value)
            start_swaps(c, 1, value)
        elif step == "k":
            embs[1] = hold(*take(embs[1]))
            token.append(embs[1])
        elif step in "fg":
            held = gathered[c][p]
            if step == "g":
                held[NEXT], held[SIDE] = take(held[NEXT], held[SIDE])
            else:
                (held[NEXT],) = take(held[NEXT])
            held[NEXT | SIDE] = swap(held[NEXT], "row", nrow, SIDE)
            token.append(held[NEXT])
        elif step == "o":
            held = take(*(gathered[c][p][m] for m in shards))
            outgoing = {}
            for d in dests[:-1]:
                if outgoing:
                    outgoing[d] = combine(ids[d], [tables[c][p]], jnp.bfloat16)[0]
                else:
                    outgoing[d], tables[c][p] = combine_far(ids[d], held)
            token.append(outgoing[dests[-2]])
            arrived[c][p] = reduce(outgoing)
        elif step == "w":
            tables[c] = list(take(*tables[c]))
            own[c] = combine(ids[0], tables[c], jnp.float32)
            token.append(own[c][0])
        elif step == "z":
            arrived[c][p] = take(*arrived[c][p])
            token.append(arrived[c][p][-1])
        elif step == "e":
            here, *later = take(own[c][p], *arrived[c][p])
            value = expand(p, here, later, products[c])
            products[c] = value
            token.append(value)
            if p + 1 == PARTS:
                other = swap(value, "col", ncol, CORES)
                for i in range(2, ncol.bit_length() - 1):
                    value = add_bf16(value, other)
                    other = swap(value, "col", ncol, 1 << i)
                pairs[c] = ((value, other), (swap(value, "col", ncol, 1),))
        elif step == "p":
            theirs = take(*before[c][1])
            before[c] = (before[c][0], theirs)
            first = fill(c, first, before[c])
            token.append(first)
        elif step == "r":
            share(c)
            token.append(pairs[c][0][0])
        else:
            theirs = take(*pairs[c][1])
            second = fill(c, second, (pairs[c][0], theirs), before[c])
            token.append(second)
    return first, second


def solution(mesh):
    placed = (P("row", "col"), P("row"), P(None, "row"), P("row", None))
    return jax.shard_map(
        body,
        mesh=mesh,
        in_specs=placed,
        out_specs=(P(None, "row"), P(None, "row")),
        check_vma=False,
    )
```

```python
import functools

import jax
import jax.numpy as jnp
from jax import lax
from jax.experimental import pallas as pl
from jax.experimental.pallas import tpu as pltpu
from jax.sharding import PartitionSpec as P

CORES = 2
GROUPS = 2
PARTS = CORES
TILE_BLOCKS = 8
UNROLL = 32
VMEM_LIMIT = 8 * 1024 * 1024
SIDE, NEXT = 1, 2

ORDER = (
    "As Al Am Bm",
    "Af1 Af2 Ao1 Ak",
    "Ao2 Aw Ae1 Bg1",
    "Az2 Bg2 Ae2 Bo1",
    "As1 As2 Bo2 Bw",
    "Be1 Af1 Be2 Ag2",
    "Ao1 Bs1 Ap Bs2",
    "Ao2 Aw Ae1 Bf1",
    "Ae2 Bf2 Bo1 Bo2",
    "Bw Ar Bp Be1",
    "Au Be2 Br Bu",
)

VMEM = pl.BlockSpec(memory_space=pltpu.VMEM)
SMEM = pl.BlockSpec(memory_space=pltpu.SMEM)
ANY = pl.BlockSpec(memory_space=pl.ANY)
HBM = pl.BlockSpec(memory_space=pltpu.HBM)


def params():
    return pltpu.CompilerParams(vmem_limit_bytes=VMEM_LIMIT)


def swap(value, axis, size, mask):
    return lax.ppermute(value, axis, [(i, i ^ mask) for i in range(size)])


def add_bf16(a, b):
    return (a.astype(jnp.float32) + b.astype(jnp.float32)).astype(jnp.bfloat16)


def add_f32(a, b):
    return a.astype(jnp.float32) + b.astype(jnp.float32)


def block_sum(scaled, emb):
    return jnp.dot(scaled, emb, preferred_element_type=jnp.float32).astype(jnp.bfloat16)


def probe_rows(core, group, size):
    return pl.ds(pl.multiple_of((core * GROUPS + group) * size, size), size)


def first_sums_kernel(core_ref, vec_ref, quality_ref, emb_ref, *refs):
    *sums_refs, vec, quality, emb, sems = refs
    tiles, tile_docs = emb.shape[:2]
    blocks, group, _ = sums_refs[0].shape
    block_len = tiles * tile_docs // blocks
    core = core_ref[0]
    here = [pltpu.make_async_copy(quality_ref, quality, sems.at[tiles])]
    for i in range(CORES * GROUPS):
        rows = probe_rows(core if i < GROUPS else 1 - core, i % GROUPS, group)
        here.append(pltpu.make_async_copy(vec_ref.at[rows], vec.at[pl.ds(i * group, group)], sems.at[tiles + 1 + i]))

    def tile_copy(j):
        docs = pl.ds(pl.multiple_of(j * tile_docs, tile_docs), tile_docs)
        return pltpu.make_async_copy(emb_ref.at[docs], emb.at[j], sems.at[j])

    for copy in here:
        copy.start()
    for j in range(tiles):
        tile_copy(j).start()
    for copy in here:
        copy.wait()

    def step(j, carry):
        tile_copy(j).wait()
        for b in range(blocks // tiles):
            docs = pl.ds(pl.multiple_of(j * tile_docs + b * block_len, block_len), block_len)
            scaled = (vec[:, docs] * quality[:, docs]).astype(jnp.bfloat16)
            sums = block_sum(scaled, emb[j, b * block_len:(b + 1) * block_len])
            for i, ref in enumerate(sums_refs):
                ref[j * (blocks // tiles) + b] = sums[i * group:(i + 1) * group]
        return carry

    lax.fori_loop(0, tiles, step, 0)


def hold_kernel(src_ref, out_ref, sem):
    copy = pltpu.make_async_copy(src_ref, out_ref, sem)
    copy.start()
    copy.wait()


def next_sums_kernel(c, core_ref, mine_ref, other_ref, vec_ref, quality_ref, emb_ref, sums_ref):
    blocks, group, _ = sums_ref.shape
    block_len = emb_ref.shape[0] // blocks
    rows = probe_rows(core_ref[0], c, group)

    def step(b, carry):
        docs = pl.ds(pl.multiple_of(b * block_len, block_len), block_len)
        quality = quality_ref[:, docs]
        value = add_f32(mine_ref[:, docs], other_ref[:, docs]) * quality - vec_ref[rows, docs]
        sums_ref[b] = block_sum((value * quality).astype(jnp.bfloat16), emb_ref[docs])
        return carry

    lax.fori_loop(0, blocks, step, 0, unroll=UNROLL)


def fill_kernel(c, second, core_ref, vec_ref, quality_ref, *refs):
    out_ref, out, sems = refs[-3:]
    tiles = sems.shape[1]
    _, group, docs_all = out.shape
    tile_docs = docs_all // tiles
    copies = []
    for i in range(CORES):
        rows = probe_rows(core_ref[0] if i == 0 else 1 - core_ref[0], c, group)
        pair, before = refs[2 * i:2 * i + 2], refs[2 * (CORES + i):2 * (CORES + i) + 2]
        for j in range(tiles):
            docs = pl.ds(j * tile_docs, tile_docs)
            vec, quality = vec_ref[rows, docs], quality_ref[:, docs]
            value = add_f32(pair[0][:, docs], pair[1][:, docs]) * quality
            if second:
                first = add_f32(before[0][:, docs], before[1][:, docs]) * quality - vec
                value = 2.0 * (value - first) - vec
            else:
                value = value - vec
            out[i, :, docs] = value
            copies.append(pltpu.make_async_copy(out.at[i, :, docs], out_ref.at[rows, docs], sems.at[i, j]))
            copies[-1].start()
    for copy in copies:
        copy.wait()


def lookup(ids_ref, tables, outs, entries):
    def step(b, carry):
        places = [ids_ref[b * entries + k] for k in range(entries)]
        for table, ref in zip(tables, outs):
            total = table[places[0]].astype(jnp.float32)
            for place in places[1:]:
                total = total + table[place].astype(jnp.float32)
            ref[b] = total.astype(ref.dtype)
        return carry

    lax.fori_loop(0, outs[0].shape[0], step, 0, unroll=UNROLL)


def table_kernel(ids_ref, *refs):
    *shards, out_ref, table, sems = refs
    blocks = shards[0].shape[0]
    copies = [
        pltpu.make_async_copy(ref, table.at[pl.ds(i * blocks, blocks)], sems.at[i])
        for i, ref in enumerate(shards)
    ]
    for copy in copies:
        copy.start()
    table[len(shards) * blocks] = jnp.zeros(table.shape[1:], table.dtype)
    for copy in copies:
        copy.wait()
    lookup(ids_ref, [table], [out_ref], ids_ref.shape[0] // blocks)


def lookup_kernel(ids_ref, *refs):
    count = len(refs) // 2
    lookup(ids_ref, refs[:count], refs[count:], ids_ref.shape[0] // refs[count].shape[0])


def expand_kernel(*refs):
    own_ref, *arrived_refs, emb_ref, out_ref = refs
    held = arrived_refs.pop() if len(arrived_refs[-1].shape) == 2 else None
    blocks = own_ref.shape[0]
    block_len = emb_ref.shape[0] // blocks

    def step(b, carry):
        docs = pl.ds(pl.multiple_of(b * block_len, block_len), block_len)
        total = own_ref[b]
        for ref in arrived_refs:
            total = total + ref[b].astype(jnp.float32)
        products = lax.dot_general(
            total.astype(jnp.bfloat16), emb_ref[docs], (((1,), (1,)), ((), ())),
            preferred_element_type=jnp.float32,
        )
        if held is not None:
            products = products + held[:, docs]
        out_ref[:, docs] = products.astype(out_ref.dtype)
        return carry

    lax.fori_loop(0, blocks, step, 0, unroll=UNROLL)


def body(embeddings, quality, probes, neighbors):
    nrow, ncol = lax.axis_size("row"), lax.axis_size("col")
    me = lax.axis_index("row")
    blk_count, list_len = neighbors.shape
    docs, width = embeddings.shape
    nprobe = probes.shape[0]
    group = nprobe // (CORES * GROUPS)
    core = (lax.axis_index("col") % CORES).astype(jnp.int32).reshape(1)
    tiles = blk_count // TILE_BLOCKS
    reduce_bits = [1 << i for i in reversed(range(nrow.bit_length() - 1)) if 1 << i not in (SIDE, NEXT)]
    dests = [0]
    for m in reversed(reduce_bits):
        dests = [d | m for d in dests] + dests
    shards = (0, NEXT, SIDE, NEXT | SIDE)

    def table_ids(lists):
        flat = lists.reshape(-1)
        apart = (flat // blk_count) ^ me
        place = flat % blk_count
        for i, shard in enumerate(shards):
            place = jnp.where(apart == shard, i * blk_count + flat % blk_count, place)
        return jnp.where((apart & ~(NEXT | SIDE)) == 0, place, len(shards) * blk_count)

    qrow = quality[None, :]
    shard_shape = (blk_count, group, width)
    shard_out = jax.ShapeDtypeStruct(shard_shape, jnp.bfloat16)
    vec_out = jax.ShapeDtypeStruct((nprobe, docs), jnp.float32)

    def first_sums():
        return pl.pallas_call(
            first_sums_kernel,
            in_specs=[SMEM] + [HBM] * 3,
            out_specs=[VMEM] * (CORES * GROUPS),
            out_shape=[shard_out] * (CORES * GROUPS),
            scratch_shapes=[
                pltpu.VMEM((nprobe, docs), jnp.float32),
                pltpu.VMEM((1, docs), jnp.float32),
                pltpu.VMEM((tiles, docs // tiles, width), jnp.bfloat16),
                pltpu.SemaphoreType.DMA((tiles + 1 + CORES * GROUPS,)),
            ],
            compiler_params=params(),
        )(core, *(pltpu.with_memory_space_constraint(v, pltpu.HBM) for v in (probes, qrow, embeddings)))

    def hold(value):
        return pl.pallas_call(
            hold_kernel,
            in_specs=[ANY],
            out_specs=VMEM,
            out_shape=jax.ShapeDtypeStruct(value.shape, value.dtype),
            scratch_shapes=[pltpu.SemaphoreType.DMA],
            compiler_params=params(),
        )(value)

    def next_sums(c, p, pair):
        return pl.pallas_call(
            functools.partial(next_sums_kernel, c),
            in_specs=[SMEM] + [VMEM] * 5,
            out_specs=VMEM,
            out_shape=shard_out,
            compiler_params=params(),
        )(core, *pair, probes, qrow, embs[p])

    def fill(c, held, pairs, before=()):
        held = [] if held is None else [held]
        values = [v for pair in (*pairs, *before) for v in pair]
        return pl.pallas_call(
            functools.partial(fill_kernel, c, bool(before)),
            in_specs=[SMEM] + [VMEM] * (2 + len(values)) + [ANY] * len(held),
            out_specs=HBM,
            out_shape=vec_out,
            input_output_aliases={3 + len(values): 0} if held else {},
            scratch_shapes=[pltpu.VMEM((CORES, group, docs), jnp.float32), pltpu.SemaphoreType.DMA((CORES, 4))],
            compiler_params=params(),
        )(core, probes, qrow, *values, *held)

    def combine_far(ids, shards):
        rows_held = len(shards) * blk_count + 1
        return pl.pallas_call(
            table_kernel,
            in_specs=[SMEM] + [VMEM] * len(shards),
            out_specs=[VMEM] * 2,
            out_shape=[shard_out, jax.ShapeDtypeStruct((rows_held, group, width), jnp.bfloat16)],
            scratch_shapes=[pltpu.SemaphoreType.DMA((len(shards),))],
            compiler_params=params(),
        )(ids, *shards)

    def combine(ids, tables, dtype):
        return pl.pallas_call(
            lookup_kernel,
            in_specs=[SMEM] + [VMEM] * len(tables),
            out_specs=[VMEM] * len(tables),
            out_shape=[jax.ShapeDtypeStruct(shard_shape, dtype)] * len(tables),
            compiler_params=params(),
        )(ids, *tables)

    def expand(p, own, arrived, held):
        values = [own, *arrived] + ([held] if p else [])
        return pl.pallas_call(
            expand_kernel,
            in_specs=[VMEM] * (len(values) + 1),
            out_specs=VMEM,
            out_shape=jax.ShapeDtypeStruct((group, docs), jnp.bfloat16 if p + 1 == PARTS else jnp.float32),
            compiler_params=params(),
        )(*values, embs[p])

    def reduce(outgoing):
        arrived = []
        for m in reduce_bits:
            taken = {d ^ m: swap(outgoing.pop(d), "row", nrow, m) for d in list(outgoing) if d & m}
            for d, value in taken.items():
                if d:
                    outgoing[d] = add_bf16(outgoing[d], value)
                else:
                    arrived.append(value)
        return arrived

    token = []

    def take(*values):
        if token:
            values = lax.optimization_barrier(values + (token.pop(),))[:-1]
        return values

    lists = {d: swap(neighbors, "row", nrow, d) if d else neighbors for d in dests}
    first = second = None
    embs = [embeddings, swap(embeddings, "col", ncol, 1)]
    gathered = [[None] * PARTS for _ in range(GROUPS)]
    tables = [[None] * PARTS for _ in range(GROUPS)]
    own = [[None] * PARTS for _ in range(GROUPS)]
    arrived = [[None] * PARTS for _ in range(GROUPS)]
    products = [None] * GROUPS
    pairs = [None] * GROUPS
    before = [None] * GROUPS

    def start_swaps(c, p, value):
        gathered[c][p] = {0: value}
        for m in (NEXT, SIDE):
            gathered[c][p][m] = swap(value, "row", nrow, m)

    def share(c):
        (mine, other), theirs = pairs[c]
        pairs[c] = (take(mine, other), (theirs[0], swap(other, "col", ncol, 1)))

    for word in (word for line in ORDER for word in line.split()):
        c, step, p = ord(word[0]) - ord("A"), word[1], int(word[2:] or 0) - 1
        if step == "l":
            taken = take(*(lists[d] for d in dests))
            ids = dict(zip(dests, lax.optimization_barrier(tuple(table_ids(v) for v in taken))))
            token.append(ids[0])
        elif step == "s":
            if pairs[c] is None:
                *sums, tied = lax.optimization_barrier((*first_sums(), tuple(lists.values())))
                lists = dict(zip(lists, tied))
                token.append(sums[0])
                for i in range(GROUPS):
                    start_swaps(i, 0, sums[i])
                late = [swap(v, "col", ncol, 1) for v in sums[GROUPS:]]
            else:
                if p == 0:
                    share(c)
                    before[c] = pairs[c]
                    pair = pairs[c][0]
                else:
                    pair = take(*pairs[c][0])
                value = next_sums(c, p, pair)
                token.append(value)
                start_swaps(c, p, value)
        elif step == "m":
            (value,) = take(late[c])
            token.append(value)
            start_swaps(c, 1, value)
        elif step == "k":
            embs[1] = hold(*take(embs[1]))
            token.append(embs[1])
        elif step in "fg":
            held = gathered[c][p]
            if step == "g":
                held[NEXT], held[SIDE] = take(held[NEXT], held[SIDE])
            else:
                (held[NEXT],) = take(held[NEXT])
            held[NEXT | SIDE] = swap(held[NEXT], "row", nrow, SIDE)
            token.append(held[NEXT])
        elif step == "o":
            held = take(*(gathered[c][p][m] for m in shards))
            outgoing = {}
            for d in dests[:-1]:
                if outgoing:
                    outgoing[d] = combine(ids[d], [tables[c][p]], jnp.bfloat16)[0]
                else:
                    outgoing[d], tables[c][p] = combine_far(ids[d], held)
            token.append(outgoing[dests[-2]])
            arrived[c][p] = reduce(outgoing)
        elif step == "w":
            tables[c] = list(take(*tables[c]))
            own[c] = combine(ids[0], tables[c], jnp.float32)
            token.append(own[c][0])
        elif step == "z":
            arrived[c][p] = take(*arrived[c][p])
            token.append(arrived[c][p][-1])
        elif step == "e":
            here, *later = take(own[c][p], *arrived[c][p])
            value = expand(p, here, later, products[c])
            products[c] = value
            token.append(value)
            if p + 1 == PARTS:
                other = swap(value, "col", ncol, CORES)
                for i in range(2, ncol.bit_length() - 1):
                    value = add_bf16(value, other)
                    other = swap(value, "col", ncol, 1 << i)
                pairs[c] = ((value, other), (swap(value, "col", ncol, 1),))
        elif step == "p":
            theirs = take(*before[c][1])
            before[c] = (before[c][0], theirs)
            first = fill(c, first, before[c])
            token.append(first)
        elif step == "r":
            share(c)
            token.append(pairs[c][0][0])
        else:
            theirs = take(*pairs[c][1])
            second = fill(c, second, (pairs[c][0], theirs), before[c])
            token.append(second)
    return first, second


def solution(mesh):
    placed = (P("row", "col"), P("row"), P(None, "row"), P("row", None))
    return jax.shard_map(
        body,
        mesh=mesh,
        in_specs=placed,
        out_specs=(P(None, "row"), P(None, "row")),
        check_vma=False,
    )
```

```python
import functools

import jax
import jax.numpy as jnp
from jax import lax
from jax.experimental import pallas as pl
from jax.experimental.pallas import tpu as pltpu
from jax.sharding import PartitionSpec as P

CORES = 2
GROUPS = 2
PARTS = CORES
TILE_DOCS = 1024
UNROLL = 32
VMEM_LIMIT = 8 * 1024 * 1024
SIDE, NEXT = 1, 2

ORDER = (
    "As Am Bm Af1",
    "Al Af2 Ao1 Ak",
    "Ao2 Aw Ae1 Bg1",
    "Az2 Bg2 Ae2 Bo1",
    "As1 As2 Bo2 Bw",
    "Be1 Af1 Be2 Ag2",
    "Ao1 Bs1 Ap Bs2",
    "Ao2 Aw Ae1 Bf1",
    "Ae2 Bf2 Bo1 Bo2",
    "Bw Ar Bp Be1",
    "Au Be2 Br Bu",
)

VMEM = pl.BlockSpec(memory_space=pltpu.VMEM)
SMEM = pl.BlockSpec(memory_space=pltpu.SMEM)
ANY = pl.BlockSpec(memory_space=pl.ANY)
HBM = pl.BlockSpec(memory_space=pltpu.HBM)


def params():
    return pltpu.CompilerParams(vmem_limit_bytes=VMEM_LIMIT)


def swap(value, axis, size, mask):
    return lax.ppermute(value, axis, [(i, i ^ mask) for i in range(size)])


def add_bf16(a, b):
    return (a.astype(jnp.float32) + b.astype(jnp.float32)).astype(jnp.bfloat16)


def add_f32(a, b):
    return a.astype(jnp.float32) + b.astype(jnp.float32)


def block_sum(scaled, emb):
    return jnp.dot(scaled, emb, preferred_element_type=jnp.float32).astype(jnp.bfloat16)


def probe_rows(core, group, size):
    return pl.ds(pl.multiple_of((core * GROUPS + group) * size, size), size)


def first_sums_kernel(core_ref, vec_ref, quality_ref, emb_ref, *refs):
    *sums_refs, emb, vec, quality, sems = refs
    tiles = emb_ref.shape[0] // TILE_DOCS
    tile_docs = TILE_DOCS
    blocks, group, _ = sums_refs[0].shape
    block_len = tiles * tile_docs // blocks
    core = core_ref[0]
    here = [pltpu.make_async_copy(quality_ref, quality, sems.at[tiles])]
    for i in range(CORES * GROUPS):
        rows = probe_rows(core if i < GROUPS else 1 - core, i % GROUPS, group)
        here.append(pltpu.make_async_copy(vec_ref.at[rows], vec.at[pl.ds(i * group, group)], sems.at[tiles + 1 + i]))

    def tile_copy(j):
        docs = pl.ds(pl.multiple_of(j * tile_docs, tile_docs), tile_docs)
        return pltpu.make_async_copy(emb_ref.at[docs], emb.at[docs], sems.at[j])

    for copy in here:
        copy.start()
    for j in range(tiles):
        tile_copy(j).start()
    for copy in here:
        copy.wait()

    def step(j, carry):
        tile_copy(j).wait()
        for b in range(blocks // tiles):
            docs = pl.ds(pl.multiple_of(j * tile_docs + b * block_len, block_len), block_len)
            scaled = (vec[:, docs] * quality[:, docs]).astype(jnp.bfloat16)
            sums = block_sum(scaled, emb[docs])
            for i, ref in enumerate(sums_refs):
                ref[j * (blocks // tiles) + b] = sums[i * group:(i + 1) * group]
        return carry

    lax.fori_loop(0, tiles, step, 0)


def hold_kernel(src_ref, out_ref, sem):
    copy = pltpu.make_async_copy(src_ref, out_ref, sem)
    copy.start()
    copy.wait()


def next_sums_kernel(c, core_ref, mine_ref, other_ref, vec_ref, quality_ref, emb_ref, sums_ref):
    blocks, group, _ = sums_ref.shape
    block_len = emb_ref.shape[0] // blocks
    rows = probe_rows(core_ref[0], c, group)

    def step(b, carry):
        docs = pl.ds(pl.multiple_of(b * block_len, block_len), block_len)
        quality = quality_ref[:, docs]
        value = add_f32(mine_ref[:, docs], other_ref[:, docs]) * quality - vec_ref[rows, docs]
        sums_ref[b] = block_sum((value * quality).astype(jnp.bfloat16), emb_ref[docs])
        return carry

    lax.fori_loop(0, blocks, step, 0, unroll=UNROLL)


def fill_kernel(c, second, core_ref, vec_ref, quality_ref, *refs):
    out_ref, out, sems = refs[-3:]
    tiles = sems.shape[1]
    _, group, docs_all = out.shape
    tile_docs = docs_all // tiles
    copies = []
    for i in range(CORES):
        rows = probe_rows(core_ref[0] if i == 0 else 1 - core_ref[0], c, group)
        pair, before = refs[2 * i:2 * i + 2], refs[2 * (CORES + i):2 * (CORES + i) + 2]
        for j in range(tiles):
            docs = pl.ds(j * tile_docs, tile_docs)
            vec, quality = vec_ref[rows, docs], quality_ref[:, docs]
            value = add_f32(pair[0][:, docs], pair[1][:, docs]) * quality
            if second:
                first = add_f32(before[0][:, docs], before[1][:, docs]) * quality - vec
                value = 2.0 * (value - first) - vec
            else:
                value = value - vec
            out[i, :, docs] = value
            copies.append(pltpu.make_async_copy(out.at[i, :, docs], out_ref.at[rows, docs], sems.at[i, j]))
            copies[-1].start()
    for copy in copies:
        copy.wait()


def lookup(ids_ref, tables, outs, entries):
    def step(b, carry):
        places = [ids_ref[b * entries + k] for k in range(entries)]
        for table, ref in zip(tables, outs):
            total = table[places[0]].astype(jnp.float32)
            for place in places[1:]:
                total = total + table[place].astype(jnp.float32)
            ref[b] = total.astype(ref.dtype)
        return carry

    lax.fori_loop(0, outs[0].shape[0], step, 0, unroll=UNROLL)


def table_kernel(ids_ref, *refs):
    *shards, out_ref, table, sems = refs
    blocks = shards[0].shape[0]
    copies = [
        pltpu.make_async_copy(ref, table.at[pl.ds(i * blocks, blocks)], sems.at[i])
        for i, ref in enumerate(shards)
    ]
    for copy in copies:
        copy.start()
    table[len(shards) * blocks] = jnp.zeros(table.shape[1:], table.dtype)
    for copy in copies:
        copy.wait()
    lookup(ids_ref, [table], [out_ref], ids_ref.shape[0] // blocks)


def lookup_kernel(ids_ref, *refs):
    count = len(refs) // 2
    lookup(ids_ref, refs[:count], refs[count:], ids_ref.shape[0] // refs[count].shape[0])


def expand_kernel(*refs):
    own_ref, *arrived_refs, emb_ref, out_ref = refs
    held = arrived_refs.pop() if len(arrived_refs[-1].shape) == 2 else None
    blocks = own_ref.shape[0]
    block_len = emb_ref.shape[0] // blocks

    def step(b, carry):
        docs = pl.ds(pl.multiple_of(b * block_len, block_len), block_len)
        total = own_ref[b]
        for ref in arrived_refs:
            total = total + ref[b].astype(jnp.float32)
        products = lax.dot_general(
            total.astype(jnp.bfloat16), emb_ref[docs], (((1,), (1,)), ((), ())),
            preferred_element_type=jnp.float32,
        )
        if held is not None:
            products = products + held[:, docs]
        out_ref[:, docs] = products.astype(out_ref.dtype)
        return carry

    lax.fori_loop(0, blocks, step, 0, unroll=UNROLL)


def body(embeddings, quality, probes, neighbors):
    nrow, ncol = lax.axis_size("row"), lax.axis_size("col")
    me = lax.axis_index("row")
    blk_count, list_len = neighbors.shape
    docs, width = embeddings.shape
    nprobe = probes.shape[0]
    group = nprobe // (CORES * GROUPS)
    core = (lax.axis_index("col") % CORES).astype(jnp.int32).reshape(1)
    tiles = docs // TILE_DOCS
    reduce_bits = [1 << i for i in reversed(range(nrow.bit_length() - 1)) if 1 << i not in (SIDE, NEXT)]
    dests = [0]
    for m in reversed(reduce_bits):
        dests = [d | m for d in dests] + dests
    shards = (0, NEXT, SIDE, NEXT | SIDE)

    def table_ids(lists):
        flat = lists.reshape(-1)
        apart = (flat // blk_count) ^ me
        place = flat % blk_count
        for i, shard in enumerate(shards):
            place = jnp.where(apart == shard, i * blk_count + flat % blk_count, place)
        return jnp.where((apart & ~(NEXT | SIDE)) == 0, place, len(shards) * blk_count)

    qrow = quality[None, :]
    shard_shape = (blk_count, group, width)
    shard_out = jax.ShapeDtypeStruct(shard_shape, jnp.bfloat16)
    vec_out = jax.ShapeDtypeStruct((nprobe, docs), jnp.float32)

    def first_sums():
        return pl.pallas_call(
            first_sums_kernel,
            in_specs=[SMEM] + [HBM] * 3,
            out_specs=[VMEM] * (CORES * GROUPS + 1),
            out_shape=[shard_out] * (CORES * GROUPS) + [jax.ShapeDtypeStruct((docs, width), jnp.bfloat16)],
            scratch_shapes=[
                pltpu.VMEM((nprobe, docs), jnp.float32),
                pltpu.VMEM((1, docs), jnp.float32),
                pltpu.SemaphoreType.DMA((tiles + 1 + CORES * GROUPS,)),
            ],
            compiler_params=params(),
        )(core, *(pltpu.with_memory_space_constraint(v, pltpu.HBM) for v in (probes, qrow, embeddings)))

    def hold(value):
        return pl.pallas_call(
            hold_kernel,
            in_specs=[ANY],
            out_specs=VMEM,
            out_shape=jax.ShapeDtypeStruct(value.shape, value.dtype),
            scratch_shapes=[pltpu.SemaphoreType.DMA],
            compiler_params=params(),
        )(value)

    def next_sums(c, p, pair):
        return pl.pallas_call(
            functools.partial(next_sums_kernel, c),
            in_specs=[SMEM] + [VMEM] * 5,
            out_specs=VMEM,
            out_shape=shard_out,
            compiler_params=params(),
        )(core, *pair, probes, qrow, embs[p])

    def fill(c, held, pairs, before=()):
        held = [] if held is None else [held]
        values = [v for pair in (*pairs, *before) for v in pair]
        return pl.pallas_call(
            functools.partial(fill_kernel, c, bool(before)),
            in_specs=[SMEM] + [VMEM] * (2 + len(values)) + [ANY] * len(held),
            out_specs=HBM,
            out_shape=vec_out,
            input_output_aliases={3 + len(values): 0} if held else {},
            scratch_shapes=[pltpu.VMEM((CORES, group, docs), jnp.float32), pltpu.SemaphoreType.DMA((CORES, 4))],
            compiler_params=params(),
        )(core, probes, qrow, *values, *held)

    def combine_far(ids, shards):
        rows_held = len(shards) * blk_count + 1
        return pl.pallas_call(
            table_kernel,
            in_specs=[SMEM] + [VMEM] * len(shards),
            out_specs=[VMEM] * 2,
            out_shape=[shard_out, jax.ShapeDtypeStruct((rows_held, group, width), jnp.bfloat16)],
            scratch_shapes=[pltpu.SemaphoreType.DMA((len(shards),))],
            compiler_params=params(),
        )(ids, *shards)

    def combine(ids, tables, dtype):
        return pl.pallas_call(
            lookup_kernel,
            in_specs=[SMEM] + [VMEM] * len(tables),
            out_specs=[VMEM] * len(tables),
            out_shape=[jax.ShapeDtypeStruct(shard_shape, dtype)] * len(tables),
            compiler_params=params(),
        )(ids, *tables)

    def expand(p, own, arrived, held):
        values = [own, *arrived] + ([held] if p else [])
        return pl.pallas_call(
            expand_kernel,
            in_specs=[VMEM] * (len(values) + 1),
            out_specs=VMEM,
            out_shape=jax.ShapeDtypeStruct((group, docs), jnp.bfloat16 if p + 1 == PARTS else jnp.float32),
            compiler_params=params(),
        )(*values, embs[p])

    def reduce(outgoing):
        arrived = []
        for m in reduce_bits:
            taken = {d ^ m: swap(outgoing.pop(d), "row", nrow, m) for d in list(outgoing) if d & m}
            for d, value in taken.items():
                if d:
                    outgoing[d] = add_bf16(outgoing[d], value)
                else:
                    arrived.append(value)
        return arrived

    token = []

    def take(*values):
        if token:
            values = lax.optimization_barrier(values + (token.pop(),))[:-1]
        return values

    lists = {d: swap(neighbors, "row", nrow, d) if d else neighbors for d in dests}
    first = second = None
    embs = None
    gathered = [[None] * PARTS for _ in range(GROUPS)]
    tables = [[None] * PARTS for _ in range(GROUPS)]
    own = [[None] * PARTS for _ in range(GROUPS)]
    arrived = [[None] * PARTS for _ in range(GROUPS)]
    products = [None] * GROUPS
    pairs = [None] * GROUPS
    before = [None] * GROUPS

    def start_swaps(c, p, value):
        gathered[c][p] = {0: value}
        for m in (NEXT, SIDE):
            gathered[c][p][m] = swap(value, "row", nrow, m)

    def share(c):
        (mine, other), theirs = pairs[c]
        pairs[c] = (take(mine, other), (theirs[0], swap(other, "col", ncol, 1)))

    for word in (word for line in ORDER for word in line.split()):
        c, step, p = ord(word[0]) - ord("A"), word[1], int(word[2:] or 0) - 1
        if step == "l":
            taken = take(*(lists[d] for d in dests))
            ids = dict(zip(dests, lax.optimization_barrier(tuple(table_ids(v) for v in taken))))
            token.append(ids[0])
        elif step == "s":
            if pairs[c] is None:
                *sums, emb = first_sums()
                embs = [emb, swap(emb, "col", ncol, 1)]
                token.append(sums[0])
                for i in range(GROUPS):
                    start_swaps(i, 0, sums[i])
                late = [swap(v, "col", ncol, 1) for v in sums[GROUPS:]]
            else:
                if p == 0:
                    share(c)
                    before[c] = pairs[c]
                    pair = pairs[c][0]
                else:
                    pair = take(*pairs[c][0])
                value = next_sums(c, p, pair)
                token.append(value)
                start_swaps(c, p, value)
        elif step == "m":
            (value,) = take(late[c])
            token.append(value)
            start_swaps(c, 1, value)
        elif step == "k":
            embs[1] = hold(*take(embs[1]))
            token.append(embs[1])
        elif step in "fg":
            held = gathered[c][p]
            if step == "g":
                held[NEXT], held[SIDE] = take(held[NEXT], held[SIDE])
            else:
                (held[NEXT],) = take(held[NEXT])
            held[NEXT | SIDE] = swap(held[NEXT], "row", nrow, SIDE)
            token.append(held[NEXT])
        elif step == "o":
            held = take(*(gathered[c][p][m] for m in shards))
            outgoing = {}
            for d in dests[:-1]:
                if outgoing:
                    outgoing[d] = combine(ids[d], [tables[c][p]], jnp.bfloat16)[0]
                else:
                    outgoing[d], tables[c][p] = combine_far(ids[d], held)
            token.append(outgoing[dests[-2]])
            arrived[c][p] = reduce(outgoing)
        elif step == "w":
            tables[c] = list(take(*tables[c]))
            own[c] = combine(ids[0], tables[c], jnp.float32)
            token.append(own[c][0])
        elif step == "z":
            arrived[c][p] = take(*arrived[c][p])
            token.append(arrived[c][p][-1])
        elif step == "e":
            here, *later = take(own[c][p], *arrived[c][p])
            value = expand(p, here, later, products[c])
            products[c] = value
            token.append(value)
            if p + 1 == PARTS:
                other = swap(value, "col", ncol, CORES)
                for i in range(2, ncol.bit_length() - 1):
                    value = add_bf16(value, other)
                    other = swap(value, "col", ncol, 1 << i)
                pairs[c] = ((value, other), (swap(value, "col", ncol, 1),))
        elif step == "p":
            theirs = take(*before[c][1])
            before[c] = (before[c][0], theirs)
            first = fill(c, first, before[c])
            token.append(first)
        elif step == "r":
            share(c)
            token.append(pairs[c][0][0])
        else:
            theirs = take(*pairs[c][1])
            second = fill(c, second, (pairs[c][0], theirs), before[c])
            token.append(second)
    return first, second


def solution(mesh):
    placed = (P("row", "col"), P("row"), P(None, "row"), P("row", None))
    return jax.shard_map(
        body,
        mesh=mesh,
        in_specs=placed,
        out_specs=(P(None, "row"), P(None, "row")),
        check_vma=False,
    )
```

```python
import functools

import jax
import jax.numpy as jnp
from jax import lax
from jax.experimental import pallas as pl
from jax.experimental.pallas import tpu as pltpu
from jax.sharding import PartitionSpec as P

CORES = 2
GROUPS = 2
PARTS = CORES
TILE_BLOCKS = 8
UNROLL = 32
VMEM_LIMIT = 8 * 1024 * 1024
SIDE, NEXT = 1, 2

ORDER = (
    "As Am Bm Af1",
    "Al Af2 Ao1 Ak",
    "Ao2 Aw Ae1 Bg1",
    "Az2 Bg2 Ae2 Bo1",
    "As1 As2 Bo2 Bw",
    "Be1 Af1 Be2 Ag2",
    "Ao1 Bs1 Ap Bs2",
    "Ao2 Aw Ae1 Bf1",
    "Ae2 Bf2 Bo1 Bo2",
    "Bw Ar Bp Be1",
    "Au Be2 Br Bu",
)

VMEM = pl.BlockSpec(memory_space=pltpu.VMEM)
SMEM = pl.BlockSpec(memory_space=pltpu.SMEM)
ANY = pl.BlockSpec(memory_space=pl.ANY)
HBM = pl.BlockSpec(memory_space=pltpu.HBM)


def params():
    return pltpu.CompilerParams(vmem_limit_bytes=VMEM_LIMIT)


def swap(value, axis, size, mask):
    return lax.ppermute(value, axis, [(i, i ^ mask) for i in range(size)])


def add_bf16(a, b):
    return (a.astype(jnp.float32) + b.astype(jnp.float32)).astype(jnp.bfloat16)


def add_f32(a, b):
    return a.astype(jnp.float32) + b.astype(jnp.float32)


def block_sum(scaled, emb):
    return jnp.dot(scaled, emb, preferred_element_type=jnp.float32).astype(jnp.bfloat16)


def probe_rows(core, group, size):
    return pl.ds(pl.multiple_of((core * GROUPS + group) * size, size), size)


def first_sums_kernel(core_ref, vec_ref, quality_ref, emb_ref, *refs):
    *sums_refs, vec, quality, emb, sems = refs
    tiles, tile_docs = emb.shape[:2]
    blocks, group, _ = sums_refs[0].shape
    block_len = tiles * tile_docs // blocks
    core = core_ref[0]
    here = [pltpu.make_async_copy(quality_ref, quality, sems.at[tiles])]
    for i in range(CORES * GROUPS):
        rows = probe_rows(core if i < GROUPS else 1 - core, i % GROUPS, group)
        here.append(pltpu.make_async_copy(vec_ref.at[rows], vec.at[pl.ds(i * group, group)], sems.at[tiles + 1 + i]))

    def tile_copy(j):
        docs = pl.ds(pl.multiple_of(j * tile_docs, tile_docs), tile_docs)
        return pltpu.make_async_copy(emb_ref.at[docs], emb.at[j], sems.at[j])

    for copy in here:
        copy.start()
    for j in range(tiles):
        tile_copy(j).start()
    for copy in here:
        copy.wait()

    def step(j, carry):
        tile_copy(j).wait()
        for b in range(blocks // tiles):
            docs = pl.ds(pl.multiple_of(j * tile_docs + b * block_len, block_len), block_len)
            scaled = (vec[:, docs] * quality[:, docs]).astype(jnp.bfloat16)
            sums = block_sum(scaled, emb[j, b * block_len:(b + 1) * block_len])
            for i, ref in enumerate(sums_refs):
                ref[j * (blocks // tiles) + b] = sums[i * group:(i + 1) * group]
        return carry

    lax.fori_loop(0, tiles, step, 0)


def hold_kernel(src_ref, out_ref, sem):
    copy = pltpu.make_async_copy(src_ref, out_ref, sem)
    copy.start()
    copy.wait()


def next_sums_kernel(c, core_ref, mine_ref, other_ref, vec_ref, quality_ref, emb_ref, sums_ref):
    blocks, group, _ = sums_ref.shape
    block_len = emb_ref.shape[0] // blocks
    rows = probe_rows(core_ref[0], c, group)

    def step(b, carry):
        docs = pl.ds(pl.multiple_of(b * block_len, block_len), block_len)
        quality = quality_ref[:, docs]
        value = add_f32(mine_ref[:, docs], other_ref[:, docs]) * quality - vec_ref[rows, docs]
        sums_ref[b] = block_sum((value * quality).astype(jnp.bfloat16), emb_ref[docs])
        return carry

    lax.fori_loop(0, blocks, step, 0, unroll=UNROLL)


def fill_kernel(c, second, core_ref, vec_ref, quality_ref, *refs):
    out_ref, out, sems = refs[-3:]
    tiles = sems.shape[1]
    _, group, docs_all = out.shape
    tile_docs = docs_all // tiles
    copies = []
    for i in range(CORES):
        rows = probe_rows(core_ref[0] if i == 0 else 1 - core_ref[0], c, group)
        pair, before = refs[2 * i:2 * i + 2], refs[2 * (CORES + i):2 * (CORES + i) + 2]
        for j in range(tiles):
            docs = pl.ds(j * tile_docs, tile_docs)
            vec, quality = vec_ref[rows, docs], quality_ref[:, docs]
            value = add_f32(pair[0][:, docs], pair[1][:, docs]) * quality
            if second:
                first = add_f32(before[0][:, docs], before[1][:, docs]) * quality - vec
                value = 2.0 * (value - first) - vec
            else:
                value = value - vec
            out[i, :, docs] = value
            copies.append(pltpu.make_async_copy(out.at[i, :, docs], out_ref.at[rows, docs], sems.at[i, j]))
            copies[-1].start()
    for copy in copies:
        copy.wait()


def lookup(ids_ref, tables, outs, entries):
    def step(b, carry):
        places = [ids_ref[b * entries + k] for k in range(entries)]
        for table, ref in zip(tables, outs):
            total = table[places[0]].astype(jnp.float32)
            for place in places[1:]:
                total = total + table[place].astype(jnp.float32)
            ref[b] = total.astype(ref.dtype)
        return carry

    lax.fori_loop(0, outs[0].shape[0], step, 0, unroll=UNROLL)


def table_kernel(ids_ref, *refs):
    *shards, out_ref, table, sems = refs
    blocks = shards[0].shape[0]
    copies = [
        pltpu.make_async_copy(ref, table.at[pl.ds(i * blocks, blocks)], sems.at[i])
        for i, ref in enumerate(shards)
    ]
    for copy in copies:
        copy.start()
    table[len(shards) * blocks] = jnp.zeros(table.shape[1:], table.dtype)
    for copy in copies:
        copy.wait()
    lookup(ids_ref, [table], [out_ref], ids_ref.shape[0] // blocks)


def lookup_kernel(ids_ref, *refs):
    count = len(refs) // 2
    lookup(ids_ref, refs[:count], refs[count:], ids_ref.shape[0] // refs[count].shape[0])


def expand_kernel(*refs):
    own_ref, *arrived_refs, emb_ref, out_ref = refs
    held = arrived_refs.pop() if len(arrived_refs[-1].shape) == 2 else None
    blocks = own_ref.shape[0]
    block_len = emb_ref.shape[0] // blocks

    def step(b, carry):
        docs = pl.ds(pl.multiple_of(b * block_len, block_len), block_len)
        total = own_ref[b]
        for ref in arrived_refs:
            total = total + ref[b].astype(jnp.float32)
        products = lax.dot_general(
            total.astype(jnp.bfloat16), emb_ref[docs], (((1,), (1,)), ((), ())),
            preferred_element_type=jnp.float32,
        )
        if held is not None:
            products = products + held[:, docs]
        out_ref[:, docs] = products.astype(out_ref.dtype)
        return carry

    lax.fori_loop(0, blocks, step, 0, unroll=UNROLL)


def body(embeddings, quality, probes, neighbors):
    nrow, ncol = lax.axis_size("row"), lax.axis_size("col")
    me = lax.axis_index("row")
    blk_count, list_len = neighbors.shape
    docs, width = embeddings.shape
    nprobe = probes.shape[0]
    group = nprobe // (CORES * GROUPS)
    core = (lax.axis_index("col") % CORES).astype(jnp.int32).reshape(1)
    tiles = blk_count // TILE_BLOCKS
    reduce_bits = [1 << i for i in reversed(range(nrow.bit_length() - 1)) if 1 << i not in (SIDE, NEXT)]
    dests = [0]
    for m in reversed(reduce_bits):
        dests = [d | m for d in dests] + dests
    shards = (0, NEXT, SIDE, NEXT | SIDE)

    def table_ids(lists):
        flat = lists.reshape(-1)
        apart = (flat // blk_count) ^ me
        place = flat % blk_count
        for i, shard in enumerate(shards):
            place = jnp.where(apart == shard, i * blk_count + flat % blk_count, place)
        return jnp.where((apart & ~(NEXT | SIDE)) == 0, place, len(shards) * blk_count)

    qrow = quality[None, :]
    shard_shape = (blk_count, group, width)
    shard_out = jax.ShapeDtypeStruct(shard_shape, jnp.bfloat16)
    vec_out = jax.ShapeDtypeStruct((nprobe, docs), jnp.float32)

    def first_sums():
        return pl.pallas_call(
            first_sums_kernel,
            in_specs=[SMEM] + [HBM] * 3,
            out_specs=[VMEM] * (CORES * GROUPS),
            out_shape=[shard_out] * (CORES * GROUPS),
            scratch_shapes=[
                pltpu.VMEM((nprobe, docs), jnp.float32),
                pltpu.VMEM((1, docs), jnp.float32),
                pltpu.VMEM((tiles, docs // tiles, width), jnp.bfloat16),
                pltpu.SemaphoreType.DMA((tiles + 1 + CORES * GROUPS,)),
            ],
            compiler_params=params(),
        )(core, *(pltpu.with_memory_space_constraint(v, pltpu.HBM) for v in (probes, qrow, embeddings)))

    def hold(value):
        return pl.pallas_call(
            hold_kernel,
            in_specs=[ANY],
            out_specs=VMEM,
            out_shape=jax.ShapeDtypeStruct(value.shape, value.dtype),
            scratch_shapes=[pltpu.SemaphoreType.DMA],
            compiler_params=params(),
        )(value)

    def next_sums(c, p, pair):
        return pl.pallas_call(
            functools.partial(next_sums_kernel, c),
            in_specs=[SMEM] + [VMEM] * 5,
            out_specs=VMEM,
            out_shape=shard_out,
            compiler_params=params(),
        )(core, *pair, probes, qrow, embs[p])

    def fill(c, held, pairs, before=()):
        held = [] if held is None else [held]
        values = [v for pair in (*pairs, *before) for v in pair]
        return pl.pallas_call(
            functools.partial(fill_kernel, c, bool(before)),
            in_specs=[SMEM] + [VMEM] * (2 + len(values)) + [ANY] * len(held),
            out_specs=HBM,
            out_shape=vec_out,
            input_output_aliases={3 + len(values): 0} if held else {},
            scratch_shapes=[pltpu.VMEM((CORES, group, docs), jnp.float32), pltpu.SemaphoreType.DMA((CORES, 4))],
            compiler_params=params(),
        )(core, probes, qrow, *values, *held)

    def combine_far(ids, shards):
        rows_held = len(shards) * blk_count + 1
        return pl.pallas_call(
            table_kernel,
            in_specs=[SMEM] + [VMEM] * len(shards),
            out_specs=[VMEM] * 2,
            out_shape=[shard_out, jax.ShapeDtypeStruct((rows_held, group, width), jnp.bfloat16)],
            scratch_shapes=[pltpu.SemaphoreType.DMA((len(shards),))],
            compiler_params=params(),
        )(ids, *shards)

    def combine(ids, tables, dtype):
        return pl.pallas_call(
            lookup_kernel,
            in_specs=[SMEM] + [VMEM] * len(tables),
            out_specs=[VMEM] * len(tables),
            out_shape=[jax.ShapeDtypeStruct(shard_shape, dtype)] * len(tables),
            compiler_params=params(),
        )(ids, *tables)

    def expand(p, own, arrived, held):
        values = [own, *arrived] + ([held] if p else [])
        return pl.pallas_call(
            expand_kernel,
            in_specs=[VMEM] * (len(values) + 1),
            out_specs=VMEM,
            out_shape=jax.ShapeDtypeStruct((group, docs), jnp.bfloat16 if p + 1 == PARTS else jnp.float32),
            compiler_params=params(),
        )(*values, embs[p])

    def reduce(outgoing):
        arrived = []
        for m in reduce_bits:
            taken = {d ^ m: swap(outgoing.pop(d), "row", nrow, m) for d in list(outgoing) if d & m}
            for d, value in taken.items():
                if d:
                    outgoing[d] = add_bf16(outgoing[d], value)
                else:
                    arrived.append(value)
        return arrived

    token = []

    def take(*values):
        if token:
            values = lax.optimization_barrier(values + (token.pop(),))[:-1]
        return values

    lists = {d: swap(neighbors, "row", nrow, d) if d else neighbors for d in dests}
    first = second = None
    embs = [embeddings, swap(embeddings, "col", ncol, 1)]
    gathered = [[None] * PARTS for _ in range(GROUPS)]
    tables = [[None] * PARTS for _ in range(GROUPS)]
    own = [[None] * PARTS for _ in range(GROUPS)]
    arrived = [[None] * PARTS for _ in range(GROUPS)]
    products = [None] * GROUPS
    pairs = [None] * GROUPS
    before = [None] * GROUPS

    def start_swaps(c, p, value):
        gathered[c][p] = {0: value}
        for m in (NEXT, SIDE):
            gathered[c][p][m] = swap(value, "row", nrow, m)

    def share(c):
        (mine, other), theirs = pairs[c]
        pairs[c] = (take(mine, other), (theirs[0], swap(other, "col", ncol, 1)))

    for word in (word for line in ORDER for word in line.split()):
        c, step, p = ord(word[0]) - ord("A"), word[1], int(word[2:] or 0) - 1
        if step == "l":
            taken = take(*(lists[d] for d in dests))
            ids = dict(zip(dests, lax.optimization_barrier(tuple(table_ids(v) for v in taken))))
            token.append(ids[0])
        elif step == "s":
            if pairs[c] is None:
                sums = first_sums()
                token.append(sums[0])
                for i in range(GROUPS):
                    start_swaps(i, 0, sums[i])
                late = [swap(v, "col", ncol, 1) for v in sums[GROUPS:]]
            else:
                if p == 0:
                    share(c)
                    before[c] = pairs[c]
                    pair = pairs[c][0]
                else:
                    pair = take(*pairs[c][0])
                value = next_sums(c, p, pair)
                token.append(value)
                start_swaps(c, p, value)
        elif step == "m":
            (value,) = take(late[c])
            token.append(value)
            start_swaps(c, 1, value)
        elif step == "k":
            embs[1] = hold(*take(embs[1]))
            token.append(embs[1])
        elif step in "fg":
            held = gathered[c][p]
            if step == "g":
                held[NEXT], held[SIDE] = take(held[NEXT], held[SIDE])
            else:
                (held[NEXT],) = take(held[NEXT])
            held[NEXT | SIDE] = swap(held[NEXT], "row", nrow, SIDE)
            token.append(held[NEXT])
        elif step == "o":
            held = take(*(gathered[c][p][m] for m in shards))
            outgoing = {}
            for d in dests[:-1]:
                if outgoing:
                    outgoing[d] = combine(ids[d], [tables[c][p]], jnp.bfloat16)[0]
                else:
                    outgoing[d], tables[c][p] = combine_far(ids[d], held)
            token.append(outgoing[dests[-2]])
            arrived[c][p] = reduce(outgoing)
        elif step == "w":
            tables[c] = list(take(*tables[c]))
            own[c] = combine(ids[0], tables[c], jnp.float32)
            token.append(own[c][0])
        elif step == "z":
            arrived[c][p] = take(*arrived[c][p])
            token.append(arrived[c][p][-1])
        elif step == "e":
            here, *later = take(own[c][p], *arrived[c][p])
            value = expand(p, here, later, products[c])
            products[c] = value
            token.append(value)
            if p + 1 == PARTS:
                other = swap(value, "col", ncol, CORES)
                for i in range(2, ncol.bit_length() - 1):
                    value = add_bf16(value, other)
                    other = swap(value, "col", ncol, 1 << i)
                pairs[c] = ((value, other), (swap(value, "col", ncol, 1),))
        elif step == "p":
            theirs = take(*before[c][1])
            before[c] = (before[c][0], theirs)
            first = fill(c, first, before[c])
            token.append(first)
        elif step == "r":
            share(c)
            token.append(pairs[c][0][0])
        else:
            theirs = take(*pairs[c][1])
            second = fill(c, second, (pairs[c][0], theirs), before[c])
            token.append(second)
    return first, second


def solution(mesh):
    placed = (P("row", "col"), P("row"), P(None, "row"), P("row", None))
    return jax.shard_map(
        body,
        mesh=mesh,
        in_specs=placed,
        out_specs=(P(None, "row"), P(None, "row")),
        check_vma=False,
    )
```

```python
import functools

import jax
import jax.numpy as jnp
from jax import lax
from jax.experimental import pallas as pl
from jax.experimental.pallas import tpu as pltpu
from jax.sharding import PartitionSpec as P

CORES = 2
GROUPS = 2
PARTS = CORES
TILE_BLOCKS = 8
UNROLL = 64
VMEM_LIMIT = 8 * 1024 * 1024
SIDE, NEXT = 1, 2

ORDER = (
    "As Al Am Bm",
    "Af1 Af2 Ao1 Ak",
    "Ao2 Aw Ae1 Bg1",
    "Az2 Bg2 Ae2 Bo1",
    "As1 As2 Bo2 Bw",
    "Be1 Af1 Be2 Ag2",
    "Ao1 Bs1 Ap Bs2",
    "Ao2 Aw Ae1 Bf1",
    "Ae2 Bf2 Bo1 Bo2",
    "Bw Ar Bp Be1",
    "Au Be2 Br Bu",
)

VMEM = pl.BlockSpec(memory_space=pltpu.VMEM)
SMEM = pl.BlockSpec(memory_space=pltpu.SMEM)
ANY = pl.BlockSpec(memory_space=pl.ANY)
HBM = pl.BlockSpec(memory_space=pltpu.HBM)


def params():
    return pltpu.CompilerParams(vmem_limit_bytes=VMEM_LIMIT)


def swap(value, axis, size, mask):
    return lax.ppermute(value, axis, [(i, i ^ mask) for i in range(size)])


def add_bf16(a, b):
    return (a.astype(jnp.float32) + b.astype(jnp.float32)).astype(jnp.bfloat16)


def add_f32(a, b):
    return a.astype(jnp.float32) + b.astype(jnp.float32)


def block_sum(scaled, emb):
    return jnp.dot(scaled, emb, preferred_element_type=jnp.float32).astype(jnp.bfloat16)


def probe_rows(core, group, size):
    return pl.ds(pl.multiple_of((core * GROUPS + group) * size, size), size)


def first_sums_kernel(core_ref, vec_ref, quality_ref, emb_ref, *refs):
    *sums_refs, vec, quality, emb, sems = refs
    tiles, tile_docs = emb.shape[:2]
    blocks, group, _ = sums_refs[0].shape
    block_len = tiles * tile_docs // blocks
    core = core_ref[0]
    here = [pltpu.make_async_copy(quality_ref, quality, sems.at[tiles])]
    for i in range(CORES * GROUPS):
        rows = probe_rows(core if i < GROUPS else 1 - core, i % GROUPS, group)
        here.append(pltpu.make_async_copy(vec_ref.at[rows], vec.at[pl.ds(i * group, group)], sems.at[tiles + 1 + i]))

    def tile_copy(j):
        docs = pl.ds(pl.multiple_of(j * tile_docs, tile_docs), tile_docs)
        return pltpu.make_async_copy(emb_ref.at[docs], emb.at[j], sems.at[j])

    for copy in here:
        copy.start()
    for j in range(tiles):
        tile_copy(j).start()
    for copy in here:
        copy.wait()

    def step(j, carry):
        tile_copy(j).wait()
        for b in range(blocks // tiles):
            docs = pl.ds(pl.multiple_of(j * tile_docs + b * block_len, block_len), block_len)
            scaled = (vec[:, docs] * quality[:, docs]).astype(jnp.bfloat16)
            sums = block_sum(scaled, emb[j, b * block_len:(b + 1) * block_len])
            for i, ref in enumerate(sums_refs):
                ref[j * (blocks // tiles) + b] = sums[i * group:(i + 1) * group]
        return carry

    lax.fori_loop(0, tiles, step, 0)


def hold_kernel(src_ref, out_ref, sem):
    copy = pltpu.make_async_copy(src_ref, out_ref, sem)
    copy.start()
    copy.wait()


def next_sums_kernel(c, core_ref, mine_ref, other_ref, vec_ref, quality_ref, emb_ref, sums_ref):
    blocks, group, _ = sums_ref.shape
    block_len = emb_ref.shape[0] // blocks
    rows = probe_rows(core_ref[0], c, group)

    def step(b, carry):
        docs = pl.ds(pl.multiple_of(b * block_len, block_len), block_len)
        quality = quality_ref[:, docs]
        value = add_f32(mine_ref[:, docs], other_ref[:, docs]) * quality - vec_ref[rows, docs]
        sums_ref[b] = block_sum((value * quality).astype(jnp.bfloat16), emb_ref[docs])
        return carry

    lax.fori_loop(0, blocks, step, 0, unroll=UNROLL)


def fill_kernel(c, second, core_ref, vec_ref, quality_ref, *refs):
    out_ref, out, sems = refs[-3:]
    tiles = sems.shape[1]
    _, group, docs_all = out.shape
    tile_docs = docs_all // tiles
    copies = []
    for i in range(CORES):
        rows = probe_rows(core_ref[0] if i == 0 else 1 - core_ref[0], c, group)
        pair, before = refs[2 * i:2 * i + 2], refs[2 * (CORES + i):2 * (CORES + i) + 2]
        for j in range(tiles):
            docs = pl.ds(j * tile_docs, tile_docs)
            vec, quality = vec_ref[rows, docs], quality_ref[:, docs]
            value = add_f32(pair[0][:, docs], pair[1][:, docs]) * quality
            if second:
                first = add_f32(before[0][:, docs], before[1][:, docs]) * quality - vec
                value = 2.0 * (value - first) - vec
            else:
                value = value - vec
            out[i, :, docs] = value
            copies.append(pltpu.make_async_copy(out.at[i, :, docs], out_ref.at[rows, docs], sems.at[i, j]))
            copies[-1].start()
    for copy in copies:
        copy.wait()


def lookup(ids_ref, tables, outs, entries):
    def step(b, carry):
        places = [ids_ref[b * entries + k] for k in range(entries)]
        for table, ref in zip(tables, outs):
            total = table[places[0]].astype(jnp.float32)
            for place in places[1:]:
                total = total + table[place].astype(jnp.float32)
            ref[b] = total.astype(ref.dtype)
        return carry

    lax.fori_loop(0, outs[0].shape[0], step, 0, unroll=UNROLL)


def table_kernel(ids_ref, *refs):
    *shards, out_ref, table, sems = refs
    blocks = shards[0].shape[0]
    copies = [
        pltpu.make_async_copy(ref, table.at[pl.ds(i * blocks, blocks)], sems.at[i])
        for i, ref in enumerate(shards)
    ]
    for copy in copies:
        copy.start()
    table[len(shards) * blocks] = jnp.zeros(table.shape[1:], table.dtype)
    for copy in copies:
        copy.wait()
    lookup(ids_ref, [table], [out_ref], ids_ref.shape[0] // blocks)


def lookup_kernel(ids_ref, *refs):
    count = len(refs) // 2
    lookup(ids_ref, refs[:count], refs[count:], ids_ref.shape[0] // refs[count].shape[0])


def expand_kernel(*refs):
    own_ref, *arrived_refs, emb_ref, out_ref = refs
    held = arrived_refs.pop() if len(arrived_refs[-1].shape) == 2 else None
    blocks = own_ref.shape[0]
    block_len = emb_ref.shape[0] // blocks

    def step(b, carry):
        docs = pl.ds(pl.multiple_of(b * block_len, block_len), block_len)
        total = own_ref[b]
        for ref in arrived_refs:
            total = total + ref[b].astype(jnp.float32)
        products = lax.dot_general(
            total.astype(jnp.bfloat16), emb_ref[docs], (((1,), (1,)), ((), ())),
            preferred_element_type=jnp.float32,
        )
        if held is not None:
            products = products + held[:, docs]
        out_ref[:, docs] = products.astype(out_ref.dtype)
        return carry

    lax.fori_loop(0, blocks, step, 0, unroll=UNROLL)


def body(embeddings, quality, probes, neighbors):
    nrow, ncol = lax.axis_size("row"), lax.axis_size("col")
    me = lax.axis_index("row")
    blk_count, list_len = neighbors.shape
    docs, width = embeddings.shape
    nprobe = probes.shape[0]
    group = nprobe // (CORES * GROUPS)
    core = (lax.axis_index("col") % CORES).astype(jnp.int32).reshape(1)
    tiles = blk_count // TILE_BLOCKS
    reduce_bits = [1 << i for i in reversed(range(nrow.bit_length() - 1)) if 1 << i not in (SIDE, NEXT)]
    dests = [0]
    for m in reversed(reduce_bits):
        dests = [d | m for d in dests] + dests
    shards = (0, NEXT, SIDE, NEXT | SIDE)

    def table_ids(lists):
        flat = lists.reshape(-1)
        apart = (flat // blk_count) ^ me
        place = flat % blk_count
        for i, shard in enumerate(shards):
            place = jnp.where(apart == shard, i * blk_count + flat % blk_count, place)
        return jnp.where((apart & ~(NEXT | SIDE)) == 0, place, len(shards) * blk_count)

    qrow = quality[None, :]
    shard_shape = (blk_count, group, width)
    shard_out = jax.ShapeDtypeStruct(shard_shape, jnp.bfloat16)
    vec_out = jax.ShapeDtypeStruct((nprobe, docs), jnp.float32)

    def first_sums():
        return pl.pallas_call(
            first_sums_kernel,
            in_specs=[SMEM] + [HBM] * 3,
            out_specs=[VMEM] * (CORES * GROUPS),
            out_shape=[shard_out] * (CORES * GROUPS),
            scratch_shapes=[
                pltpu.VMEM((nprobe, docs), jnp.float32),
                pltpu.VMEM((1, docs), jnp.float32),
                pltpu.VMEM((tiles, docs // tiles, width), jnp.bfloat16),
                pltpu.SemaphoreType.DMA((tiles + 1 + CORES * GROUPS,)),
            ],
            compiler_params=params(),
        )(core, *(pltpu.with_memory_space_constraint(v, pltpu.HBM) for v in (probes, qrow, embeddings)))

    def hold(value):
        return pl.pallas_call(
            hold_kernel,
            in_specs=[ANY],
            out_specs=VMEM,
            out_shape=jax.ShapeDtypeStruct(value.shape, value.dtype),
            scratch_shapes=[pltpu.SemaphoreType.DMA],
            compiler_params=params(),
        )(value)

    def next_sums(c, p, pair):
        return pl.pallas_call(
            functools.partial(next_sums_kernel, c),
            in_specs=[SMEM] + [VMEM] * 5,
            out_specs=VMEM,
            out_shape=shard_out,
            compiler_params=params(),
        )(core, *pair, probes, qrow, embs[p])

    def fill(c, held, pairs, before=()):
        held = [] if held is None else [held]
        values = [v for pair in (*pairs, *before) for v in pair]
        return pl.pallas_call(
            functools.partial(fill_kernel, c, bool(before)),
            in_specs=[SMEM] + [VMEM] * (2 + len(values)) + [ANY] * len(held),
            out_specs=HBM,
            out_shape=vec_out,
            input_output_aliases={3 + len(values): 0} if held else {},
            scratch_shapes=[pltpu.VMEM((CORES, group, docs), jnp.float32), pltpu.SemaphoreType.DMA((CORES, 4))],
            compiler_params=params(),
        )(core, probes, qrow, *values, *held)

    def combine_far(ids, shards):
        rows_held = len(shards) * blk_count + 1
        return pl.pallas_call(
            table_kernel,
            in_specs=[SMEM] + [VMEM] * len(shards),
            out_specs=[VMEM] * 2,
            out_shape=[shard_out, jax.ShapeDtypeStruct((rows_held, group, width), jnp.bfloat16)],
            scratch_shapes=[pltpu.SemaphoreType.DMA((len(shards),))],
            compiler_params=params(),
        )(ids, *shards)

    def combine(ids, tables, dtype):
        return pl.pallas_call(
            lookup_kernel,
            in_specs=[SMEM] + [VMEM] * len(tables),
            out_specs=[VMEM] * len(tables),
            out_shape=[jax.ShapeDtypeStruct(shard_shape, dtype)] * len(tables),
            compiler_params=params(),
        )(ids, *tables)

    def expand(p, own, arrived, held):
        values = [own, *arrived] + ([held] if p else [])
        return pl.pallas_call(
            expand_kernel,
            in_specs=[VMEM] * (len(values) + 1),
            out_specs=VMEM,
            out_shape=jax.ShapeDtypeStruct((group, docs), jnp.bfloat16 if p + 1 == PARTS else jnp.float32),
            compiler_params=params(),
        )(*values, embs[p])

    def reduce(outgoing):
        arrived = []
        for m in reduce_bits:
            taken = {d ^ m: swap(outgoing.pop(d), "row", nrow, m) for d in list(outgoing) if d & m}
            for d, value in taken.items():
                if d:
                    outgoing[d] = add_bf16(outgoing[d], value)
                else:
                    arrived.append(value)
        return arrived

    token = []

    def take(*values):
        if token:
            values = lax.optimization_barrier(values + (token.pop(),))[:-1]
        return values

    lists = {d: swap(neighbors, "row", nrow, d) if d else neighbors for d in dests}
    first = second = None
    embs = [embeddings, swap(embeddings, "col", ncol, 1)]
    gathered = [[None] * PARTS for _ in range(GROUPS)]
    tables = [[None] * PARTS for _ in range(GROUPS)]
    own = [[None] * PARTS for _ in range(GROUPS)]
    arrived = [[None] * PARTS for _ in range(GROUPS)]
    products = [None] * GROUPS
    pairs = [None] * GROUPS
    before = [None] * GROUPS

    def start_swaps(c, p, value):
        gathered[c][p] = {0: value}
        for m in (NEXT, SIDE):
            gathered[c][p][m] = swap(value, "row", nrow, m)

    def share(c):
        (mine, other), theirs = pairs[c]
        pairs[c] = (take(mine, other), (theirs[0], swap(other, "col", ncol, 1)))

    for word in (word for line in ORDER for word in line.split()):
        c, step, p = ord(word[0]) - ord("A"), word[1], int(word[2:] or 0) - 1
        if step == "l":
            taken = take(*(lists[d] for d in dests))
            ids = dict(zip(dests, lax.optimization_barrier(tuple(table_ids(v) for v in taken))))
            token.append(ids[0])
        elif step == "s":
            if pairs[c] is None:
                *sums, tied = lax.optimization_barrier((*first_sums(), tuple(lists.values())))
                lists = dict(zip(lists, tied))
                token.append(sums[0])
                for i in range(GROUPS):
                    start_swaps(i, 0, sums[i])
                late = [swap(v, "col", ncol, 1) for v in sums[GROUPS:]]
            else:
                if p == 0:
                    share(c)
                    before[c] = pairs[c]
                    pair = pairs[c][0]
                else:
                    pair = take(*pairs[c][0])
                value = next_sums(c, p, pair)
                token.append(value)
                start_swaps(c, p, value)
        elif step == "m":
            (value,) = take(late[c])
            token.append(value)
            start_swaps(c, 1, value)
        elif step == "k":
            embs[1] = hold(*take(embs[1]))
            token.append(embs[1])
        elif step in "fg":
            held = gathered[c][p]
            if step == "g":
                held[NEXT], held[SIDE] = take(held[NEXT], held[SIDE])
            else:
                (held[NEXT],) = take(held[NEXT])
            held[NEXT | SIDE] = swap(held[NEXT], "row", nrow, SIDE)
            token.append(held[NEXT])
        elif step == "o":
            held = take(*(gathered[c][p][m] for m in shards))
            outgoing = {}
            for d in dests[:-1]:
                if outgoing:
                    outgoing[d] = combine(ids[d], [tables[c][p]], jnp.bfloat16)[0]
                else:
                    outgoing[d], tables[c][p] = combine_far(ids[d], held)
            token.append(outgoing[dests[-2]])
            arrived[c][p] = reduce(outgoing)
        elif step == "w":
            tables[c] = list(take(*tables[c]))
            own[c] = combine(ids[0], tables[c], jnp.float32)
            token.append(own[c][0])
        elif step == "z":
            arrived[c][p] = take(*arrived[c][p])
            token.append(arrived[c][p][-1])
        elif step == "e":
            here, *later = take(own[c][p], *arrived[c][p])
            value = expand(p, here, later, products[c])
            products[c] = value
            token.append(value)
            if p + 1 == PARTS:
                other = swap(value, "col", ncol, CORES)
                for i in range(2, ncol.bit_length() - 1):
                    value = add_bf16(value, other)
                    other = swap(value, "col", ncol, 1 << i)
                pairs[c] = ((value, other), (swap(value, "col", ncol, 1),))
        elif step == "p":
            theirs = take(*before[c][1])
            before[c] = (before[c][0], theirs)
            first = fill(c, first, before[c])
            token.append(first)
        elif step == "r":
            share(c)
            token.append(pairs[c][0][0])
        else:
            theirs = take(*pairs[c][1])
            second = fill(c, second, (pairs[c][0], theirs), before[c])
            token.append(second)
    return first, second


def solution(mesh):
    placed = (P("row", "col"), P("row"), P(None, "row"), P("row", None))
    return jax.shard_map(
        body,
        mesh=mesh,
        in_specs=placed,
        out_specs=(P(None, "row"), P(None, "row")),
        check_vma=False,
    )
```

```python
import functools

import jax
import jax.numpy as jnp
from jax import lax
from jax.experimental import pallas as pl
from jax.experimental.pallas import tpu as pltpu
from jax.sharding import PartitionSpec as P

CORES = 2
GROUPS = 2
PARTS = CORES
TILE_BLOCKS = 8
UNROLL = 64
VMEM_LIMIT = 8 * 1024 * 1024
SIDE, NEXT = 1, 2

ORDER = (
    "As Am Al Bm",
    "Af1 Af2 Ao1 Ak",
    "Ao2 Aw Ae1 Bg1",
    "Ae2 Bg2 Bo1 As1",
    "As2 Bo2 Bw Be1",
    "Af1 Be2 Ag2 Ao1",
    "Bs1 Ap Bs2 Ao2",
    "Aw Ae1 Bf1 Ae2",
    "Bf2 Bo1 Bo2 Bw",
    "Ar Bp Be1 Au",
    "Be2 Br Bu",
)

VMEM = pl.BlockSpec(memory_space=pltpu.VMEM)
SMEM = pl.BlockSpec(memory_space=pltpu.SMEM)
ANY = pl.BlockSpec(memory_space=pl.ANY)
HBM = pl.BlockSpec(memory_space=pltpu.HBM)


def params():
    return pltpu.CompilerParams(vmem_limit_bytes=VMEM_LIMIT)


def swap(value, axis, size, mask):
    return lax.ppermute(value, axis, [(i, i ^ mask) for i in range(size)])


def add_bf16(a, b):
    return (a.astype(jnp.float32) + b.astype(jnp.float32)).astype(jnp.bfloat16)


def add_f32(a, b):
    return a.astype(jnp.float32) + b.astype(jnp.float32)


def block_sum(scaled, emb):
    return jnp.dot(scaled, emb, preferred_element_type=jnp.float32).astype(jnp.bfloat16)


def probe_rows(core, group, size):
    return pl.ds(pl.multiple_of((core * GROUPS + group) * size, size), size)


def first_sums_kernel(core_ref, vec_ref, quality_ref, emb_ref, *refs):
    *sums_refs, vec, quality, emb, sems = refs
    tiles, tile_docs = emb.shape[:2]
    blocks, group, _ = sums_refs[0].shape
    block_len = tiles * tile_docs // blocks
    core = core_ref[0]
    here = [pltpu.make_async_copy(quality_ref, quality, sems.at[tiles])]
    for i in range(CORES * GROUPS):
        rows = probe_rows(core if i < GROUPS else 1 - core, i % GROUPS, group)
        here.append(pltpu.make_async_copy(vec_ref.at[rows], vec.at[pl.ds(i * group, group)], sems.at[tiles + 1 + i]))

    def tile_copy(j):
        docs = pl.ds(pl.multiple_of(j * tile_docs, tile_docs), tile_docs)
        return pltpu.make_async_copy(emb_ref.at[docs], emb.at[j], sems.at[j])

    for copy in here:
        copy.start()
    for j in range(tiles):
        tile_copy(j).start()
    for copy in here:
        copy.wait()

    def step(j, carry):
        tile_copy(j).wait()
        for b in range(blocks // tiles):
            docs = pl.ds(pl.multiple_of(j * tile_docs + b * block_len, block_len), block_len)
            scaled = (vec[:, docs] * quality[:, docs]).astype(jnp.bfloat16)
            sums = block_sum(scaled, emb[j, b * block_len:(b + 1) * block_len])
            for i, ref in enumerate(sums_refs):
                ref[j * (blocks // tiles) + b] = sums[i * group:(i + 1) * group]
        return carry

    lax.fori_loop(0, tiles, step, 0)


def hold_kernel(src_ref, out_ref, sem):
    copy = pltpu.make_async_copy(src_ref, out_ref, sem)
    copy.start()
    copy.wait()


def next_sums_kernel(c, core_ref, mine_ref, other_ref, vec_ref, quality_ref, emb_ref, sums_ref):
    blocks, group, _ = sums_ref.shape
    block_len = emb_ref.shape[0] // blocks
    rows = probe_rows(core_ref[0], c, group)

    def step(b, carry):
        docs = pl.ds(pl.multiple_of(b * block_len, block_len), block_len)
        quality = quality_ref[:, docs]
        value = add_f32(mine_ref[:, docs], other_ref[:, docs]) * quality - vec_ref[rows, docs]
        sums_ref[b] = block_sum((value * quality).astype(jnp.bfloat16), emb_ref[docs])
        return carry

    lax.fori_loop(0, blocks, step, 0, unroll=UNROLL)


def fill_kernel(c, second, core_ref, vec_ref, quality_ref, *refs):
    out_ref, out, sems = refs[-3:]
    tiles = sems.shape[1]
    _, group, docs_all = out.shape
    tile_docs = docs_all // tiles
    copies = []
    for i in range(CORES):
        rows = probe_rows(core_ref[0] if i == 0 else 1 - core_ref[0], c, group)
        pair, before = refs[2 * i:2 * i + 2], refs[2 * (CORES + i):2 * (CORES + i) + 2]
        for j in range(tiles):
            docs = pl.ds(j * tile_docs, tile_docs)
            vec, quality = vec_ref[rows, docs], quality_ref[:, docs]
            value = add_f32(pair[0][:, docs], pair[1][:, docs]) * quality
            if second:
                first = add_f32(before[0][:, docs], before[1][:, docs]) * quality - vec
                value = 2.0 * (value - first) - vec
            else:
                value = value - vec
            out[i, :, docs] = value
            copies.append(pltpu.make_async_copy(out.at[i, :, docs], out_ref.at[rows, docs], sems.at[i, j]))
            copies[-1].start()
    for copy in copies:
        copy.wait()


def lookup(ids_ref, tables, outs, entries):
    def step(b, carry):
        places = [ids_ref[b * entries + k] for k in range(entries)]
        for table, ref in zip(tables, outs):
            total = table[places[0]].astype(jnp.float32)
            for place in places[1:]:
                total = total + table[place].astype(jnp.float32)
            ref[b] = total.astype(ref.dtype)
        return carry

    lax.fori_loop(0, outs[0].shape[0], step, 0, unroll=UNROLL)


def table_kernel(ids_ref, *refs):
    *shards, out_ref, table, sems = refs
    blocks = shards[0].shape[0]
    copies = [
        pltpu.make_async_copy(ref, table.at[pl.ds(i * blocks, blocks)], sems.at[i])
        for i, ref in enumerate(shards)
    ]
    for copy in copies:
        copy.start()
    table[len(shards) * blocks] = jnp.zeros(table.shape[1:], table.dtype)
    for copy in copies:
        copy.wait()
    lookup(ids_ref, [table], [out_ref], ids_ref.shape[0] // blocks)


def lookup_kernel(ids_ref, *refs):
    count = len(refs) // 2
    lookup(ids_ref, refs[:count], refs[count:], ids_ref.shape[0] // refs[count].shape[0])


def expand_kernel(*refs):
    own_ref, *arrived_refs, emb_ref, out_ref = refs
    held = arrived_refs.pop() if len(arrived_refs[-1].shape) == 2 else None
    blocks = own_ref.shape[0]
    block_len = emb_ref.shape[0] // blocks

    def step(b, carry):
        docs = pl.ds(pl.multiple_of(b * block_len, block_len), block_len)
        total = own_ref[b]
        for ref in arrived_refs:
            total = total + ref[b].astype(jnp.float32)
        products = lax.dot_general(
            total.astype(jnp.bfloat16), emb_ref[docs], (((1,), (1,)), ((), ())),
            preferred_element_type=jnp.float32,
        )
        if held is not None:
            products = products + held[:, docs]
        out_ref[:, docs] = products.astype(out_ref.dtype)
        return carry

    lax.fori_loop(0, blocks, step, 0, unroll=UNROLL)


def body(embeddings, quality, probes, neighbors):
    nrow, ncol = lax.axis_size("row"), lax.axis_size("col")
    me = lax.axis_index("row")
    blk_count, list_len = neighbors.shape
    docs, width = embeddings.shape
    nprobe = probes.shape[0]
    group = nprobe // (CORES * GROUPS)
    core = (lax.axis_index("col") % CORES).astype(jnp.int32).reshape(1)
    tiles = blk_count // TILE_BLOCKS
    reduce_bits = [1 << i for i in reversed(range(nrow.bit_length() - 1)) if 1 << i not in (SIDE, NEXT)]
    dests = [0]
    for m in reversed(reduce_bits):
        dests = [d | m for d in dests] + dests
    shards = (0, NEXT, SIDE, NEXT | SIDE)

    def table_ids(lists):
        flat = lists.reshape(-1)
        apart = (flat // blk_count) ^ me
        place = flat % blk_count
        for i, shard in enumerate(shards):
            place = jnp.where(apart == shard, i * blk_count + flat % blk_count, place)
        return jnp.where((apart & ~(NEXT | SIDE)) == 0, place, len(shards) * blk_count)

    qrow = quality[None, :]
    shard_shape = (blk_count, group, width)
    shard_out = jax.ShapeDtypeStruct(shard_shape, jnp.bfloat16)
    vec_out = jax.ShapeDtypeStruct((nprobe, docs), jnp.float32)

    def first_sums():
        return pl.pallas_call(
            first_sums_kernel,
            in_specs=[SMEM] + [HBM] * 3,
            out_specs=[VMEM] * (CORES * GROUPS),
            out_shape=[shard_out] * (CORES * GROUPS),
            scratch_shapes=[
                pltpu.VMEM((nprobe, docs), jnp.float32),
                pltpu.VMEM((1, docs), jnp.float32),
                pltpu.VMEM((tiles, docs // tiles, width), jnp.bfloat16),
                pltpu.SemaphoreType.DMA((tiles + 1 + CORES * GROUPS,)),
            ],
            compiler_params=params(),
        )(core, *(pltpu.with_memory_space_constraint(v, pltpu.HBM) for v in (probes, qrow, embeddings)))

    def hold(value):
        return pl.pallas_call(
            hold_kernel,
            in_specs=[ANY],
            out_specs=VMEM,
            out_shape=jax.ShapeDtypeStruct(value.shape, value.dtype),
            scratch_shapes=[pltpu.SemaphoreType.DMA],
            compiler_params=params(),
        )(value)

    def next_sums(c, p, pair):
        return pl.pallas_call(
            functools.partial(next_sums_kernel, c),
            in_specs=[SMEM] + [VMEM] * 5,
            out_specs=VMEM,
            out_shape=shard_out,
            compiler_params=params(),
        )(core, *pair, probes, qrow, embs[p])

    def fill(c, held, pairs, before=()):
        held = [] if held is None else [held]
        values = [v for pair in (*pairs, *before) for v in pair]
        return pl.pallas_call(
            functools.partial(fill_kernel, c, bool(before)),
            in_specs=[SMEM] + [VMEM] * (2 + len(values)) + [ANY] * len(held),
            out_specs=HBM,
            out_shape=vec_out,
            input_output_aliases={3 + len(values): 0} if held else {},
            scratch_shapes=[pltpu.VMEM((CORES, group, docs), jnp.float32), pltpu.SemaphoreType.DMA((CORES, 4))],
            compiler_params=params(),
        )(core, probes, qrow, *values, *held)

    def combine_far(ids, shards):
        rows_held = len(shards) * blk_count + 1
        return pl.pallas_call(
            table_kernel,
            in_specs=[SMEM] + [VMEM] * len(shards),
            out_specs=[VMEM] * 2,
            out_shape=[shard_out, jax.ShapeDtypeStruct((rows_held, group, width), jnp.bfloat16)],
            scratch_shapes=[pltpu.SemaphoreType.DMA((len(shards),))],
            compiler_params=params(),
        )(ids, *shards)

    def combine(ids, tables, dtype):
        return pl.pallas_call(
            lookup_kernel,
            in_specs=[SMEM] + [VMEM] * len(tables),
            out_specs=[VMEM] * len(tables),
            out_shape=[jax.ShapeDtypeStruct(shard_shape, dtype)] * len(tables),
            compiler_params=params(),
        )(ids, *tables)

    def expand(p, own, arrived, held):
        values = [own, *arrived] + ([held] if p else [])
        return pl.pallas_call(
            expand_kernel,
            in_specs=[VMEM] * (len(values) + 1),
            out_specs=VMEM,
            out_shape=jax.ShapeDtypeStruct((group, docs), jnp.bfloat16 if p + 1 == PARTS else jnp.float32),
            compiler_params=params(),
        )(*values, embs[p])

    def reduce(outgoing):
        arrived = []
        for m in reduce_bits:
            taken = {d ^ m: swap(outgoing.pop(d), "row", nrow, m) for d in list(outgoing) if d & m}
            for d, value in taken.items():
                if d:
                    outgoing[d] = add_bf16(outgoing[d], value)
                else:
                    arrived.append(value)
        return arrived

    token = []

    def take(*values):
        if token:
            values = lax.optimization_barrier(values + (token.pop(),))[:-1]
        return values

    lists = {d: swap(neighbors, "row", nrow, d) if d else neighbors for d in dests}
    first = second = None
    embs = [embeddings, swap(embeddings, "col", ncol, 1)]
    gathered = [[None] * PARTS for _ in range(GROUPS)]
    tables = [[None] * PARTS for _ in range(GROUPS)]
    own = [[None] * PARTS for _ in range(GROUPS)]
    arrived = [[None] * PARTS for _ in range(GROUPS)]
    products = [None] * GROUPS
    pairs = [None] * GROUPS
    before = [None] * GROUPS

    def start_swaps(c, p, value):
        gathered[c][p] = {0: value}
        for m in (NEXT, SIDE):
            gathered[c][p][m] = swap(value, "row", nrow, m)

    def share(c):
        (mine, other), theirs = pairs[c]
        pairs[c] = (take(mine, other), (theirs[0], swap(other, "col", ncol, 1)))

    for word in (word for line in ORDER for word in line.split()):
        c, step, p = ord(word[0]) - ord("A"), word[1], int(word[2:] or 0) - 1
        if step == "l":
            taken = take(*(lists[d] for d in dests))
            ids = dict(zip(dests, lax.optimization_barrier(tuple(table_ids(v) for v in taken))))
            token.append(ids[0])
        elif step == "s":
            if pairs[c] is None:
                *sums, tied = lax.optimization_barrier((*first_sums(), tuple(lists.values())))
                lists = dict(zip(lists, tied))
                token.append(sums[0])
                for i in range(GROUPS):
                    start_swaps(i, 0, sums[i])
                late = [swap(v, "col", ncol, 1) for v in sums[GROUPS:]]
            else:
                if p == 0:
                    share(c)
                    before[c] = pairs[c]
                    pair = pairs[c][0]
                else:
                    pair = take(*pairs[c][0])
                value = next_sums(c, p, pair)
                token.append(value)
                start_swaps(c, p, value)
        elif step == "m":
            (value,) = take(late[c])
            token.append(value)
            start_swaps(c, 1, value)
        elif step == "k":
            embs[1] = hold(*take(embs[1]))
            token.append(embs[1])
        elif step in "fg":
            held = gathered[c][p]
            if step == "g":
                held[NEXT], held[SIDE] = take(held[NEXT], held[SIDE])
            else:
                (held[NEXT],) = take(held[NEXT])
            held[NEXT | SIDE] = swap(held[NEXT], "row", nrow, SIDE)
            token.append(held[NEXT])
        elif step == "o":
            held = take(*(gathered[c][p][m] for m in shards))
            outgoing = {}
            for d in dests[:-1]:
                if outgoing:
                    outgoing[d] = combine(ids[d], [tables[c][p]], jnp.bfloat16)[0]
                else:
                    outgoing[d], tables[c][p] = combine_far(ids[d], held)
            token.append(outgoing[dests[-2]])
            arrived[c][p] = reduce(outgoing)
        elif step == "w":
            tables[c] = list(take(*tables[c]))
            own[c] = combine(ids[0], tables[c], jnp.float32)
            token.append(own[c][0])
        elif step == "z":
            arrived[c][p] = take(*arrived[c][p])
            token.append(arrived[c][p][-1])
        elif step == "e":
            here, *later = take(own[c][p], *arrived[c][p])
            value = expand(p, here, later, products[c])
            products[c] = value
            token.append(value)
            if p + 1 == PARTS:
                other = swap(value, "col", ncol, CORES)
                for i in range(2, ncol.bit_length() - 1):
                    value = add_bf16(value, other)
                    other = swap(value, "col", ncol, 1 << i)
                pairs[c] = ((value, other), (swap(value, "col", ncol, 1),))
        elif step == "p":
            theirs = take(*before[c][1])
            before[c] = (before[c][0], theirs)
            first = fill(c, first, before[c])
            token.append(first)
        elif step == "r":
            share(c)
            token.append(pairs[c][0][0])
        else:
            theirs = take(*pairs[c][1])
            second = fill(c, second, (pairs[c][0], theirs), before[c])
            token.append(second)
    return first, second


def solution(mesh):
    placed = (P("row", "col"), P("row"), P(None, "row"), P("row", None))
    return jax.shard_map(
        body,
        mesh=mesh,
        in_specs=placed,
        out_specs=(P(None, "row"), P(None, "row")),
        check_vma=False,
    )
```

```python
import functools

import jax
import jax.numpy as jnp
from jax import lax
from jax.experimental import pallas as pl
from jax.experimental.pallas import tpu as pltpu
from jax.sharding import PartitionSpec as P

CORES = 2
GROUPS = 2
PARTS = CORES
TILE_BLOCKS = 8
UNROLL = 64
VMEM_LIMIT = 8 * 1024 * 1024
SIDE, NEXT = 1, 2

ORDER = (
    "As Am Bm Af1",
    "Al Af2 Ao1 Ak",
    "Ao2 Aw Ae1 Bg1",
    "Az2 Bg2 Ae2 Bo1",
    "As1 As2 Bo2 Bw",
    "Be1 Af1 Be2 Ag2",
    "Ao1 Bs1 Ap Bs2",
    "Ao2 Aw Ae1 Bf1",
    "Ae2 Bf2 Bo1 Bo2",
    "Bw Ar Bp Be1",
    "Au Be2 Br Bu",
)

VMEM = pl.BlockSpec(memory_space=pltpu.VMEM)
SMEM = pl.BlockSpec(memory_space=pltpu.SMEM)
ANY = pl.BlockSpec(memory_space=pl.ANY)
HBM = pl.BlockSpec(memory_space=pltpu.HBM)


def params():
    return pltpu.CompilerParams(vmem_limit_bytes=VMEM_LIMIT)


def swap(value, axis, size, mask):
    return lax.ppermute(value, axis, [(i, i ^ mask) for i in range(size)])


def add_bf16(a, b):
    return (a.astype(jnp.float32) + b.astype(jnp.float32)).astype(jnp.bfloat16)


def add_f32(a, b):
    return a.astype(jnp.float32) + b.astype(jnp.float32)


def block_sum(scaled, emb):
    return jnp.dot(scaled, emb, preferred_element_type=jnp.float32).astype(jnp.bfloat16)


def probe_rows(core, group, size):
    return pl.ds(pl.multiple_of((core * GROUPS + group) * size, size), size)


def first_sums_kernel(core_ref, vec_ref, quality_ref, emb_ref, *refs):
    *sums_refs, vec, quality, emb, sems = refs
    tiles, tile_docs = emb.shape[:2]
    blocks, group, _ = sums_refs[0].shape
    block_len = tiles * tile_docs // blocks
    core = core_ref[0]
    here = [pltpu.make_async_copy(quality_ref, quality, sems.at[tiles])]
    for i in range(CORES * GROUPS):
        rows = probe_rows(core if i < GROUPS else 1 - core, i % GROUPS, group)
        here.append(pltpu.make_async_copy(vec_ref.at[rows], vec.at[pl.ds(i * group, group)], sems.at[tiles + 1 + i]))

    def tile_copy(j):
        docs = pl.ds(pl.multiple_of(j * tile_docs, tile_docs), tile_docs)
        return pltpu.make_async_copy(emb_ref.at[docs], emb.at[j], sems.at[j])

    for copy in here:
        copy.start()
    for j in range(tiles):
        tile_copy(j).start()
    for copy in here:
        copy.wait()

    def step(j, carry):
        tile_copy(j).wait()
        for b in range(blocks // tiles):
            docs = pl.ds(pl.multiple_of(j * tile_docs + b * block_len, block_len), block_len)
            scaled = (vec[:, docs] * quality[:, docs]).astype(jnp.bfloat16)
            sums = block_sum(scaled, emb[j, b * block_len:(b + 1) * block_len])
            for i, ref in enumerate(sums_refs):
                ref[j * (blocks // tiles) + b] = sums[i * group:(i + 1) * group]
        return carry

    lax.fori_loop(0, tiles, step, 0)


def hold_kernel(src_ref, out_ref, sem):
    copy = pltpu.make_async_copy(src_ref, out_ref, sem)
    copy.start()
    copy.wait()


def next_sums_kernel(c, core_ref, mine_ref, other_ref, vec_ref, quality_ref, emb_ref, sums_ref):
    blocks, group, _ = sums_ref.shape
    block_len = emb_ref.shape[0] // blocks
    rows = probe_rows(core_ref[0], c, group)

    def step(b, carry):
        docs = pl.ds(pl.multiple_of(b * block_len, block_len), block_len)
        quality = quality_ref[:, docs]
        value = add_f32(mine_ref[:, docs], other_ref[:, docs]) * quality - vec_ref[rows, docs]
        sums_ref[b] = block_sum((value * quality).astype(jnp.bfloat16), emb_ref[docs])
        return carry

    lax.fori_loop(0, blocks, step, 0, unroll=UNROLL)


def fill_kernel(c, second, core_ref, vec_ref, quality_ref, *refs):
    out_ref, out, sems = refs[-3:]
    tiles = sems.shape[1]
    _, group, docs_all = out.shape
    tile_docs = docs_all // tiles
    copies = []
    for i in range(CORES):
        rows = probe_rows(core_ref[0] if i == 0 else 1 - core_ref[0], c, group)
        pair, before = refs[2 * i:2 * i + 2], refs[2 * (CORES + i):2 * (CORES + i) + 2]
        for j in range(tiles):
            docs = pl.ds(j * tile_docs, tile_docs)
            vec, quality = vec_ref[rows, docs], quality_ref[:, docs]
            value = add_f32(pair[0][:, docs], pair[1][:, docs]) * quality
            if second:
                first = add_f32(before[0][:, docs], before[1][:, docs]) * quality - vec
                value = 2.0 * (value - first) - vec
            else:
                value = value - vec
            out[i, :, docs] = value
            copies.append(pltpu.make_async_copy(out.at[i, :, docs], out_ref.at[rows, docs], sems.at[i, j]))
            copies[-1].start()
    for copy in copies:
        copy.wait()


def lookup(ids_ref, tables, outs, entries):
    def step(b, carry):
        places = [ids_ref[b * entries + k] for k in range(entries)]
        for table, ref in zip(tables, outs):
            total = table[places[0]].astype(jnp.float32)
            for place in places[1:]:
                total = total + table[place].astype(jnp.float32)
            ref[b] = total.astype(ref.dtype)
        return carry

    lax.fori_loop(0, outs[0].shape[0], step, 0, unroll=UNROLL)


def table_kernel(ids_ref, *refs):
    *shards, out_ref, table, sems = refs
    blocks = shards[0].shape[0]
    copies = [
        pltpu.make_async_copy(ref, table.at[pl.ds(i * blocks, blocks)], sems.at[i])
        for i, ref in enumerate(shards)
    ]
    for copy in copies:
        copy.start()
    table[len(shards) * blocks] = jnp.zeros(table.shape[1:], table.dtype)
    for copy in copies:
        copy.wait()
    lookup(ids_ref, [table], [out_ref], ids_ref.shape[0] // blocks)


def lookup_kernel(ids_ref, *refs):
    count = len(refs) // 2
    lookup(ids_ref, refs[:count], refs[count:], ids_ref.shape[0] // refs[count].shape[0])


def expand_kernel(*refs):
    own_ref, *arrived_refs, emb_ref, out_ref = refs
    held = arrived_refs.pop() if len(arrived_refs[-1].shape) == 2 else None
    blocks = own_ref.shape[0]
    block_len = emb_ref.shape[0] // blocks

    def step(b, carry):
        docs = pl.ds(pl.multiple_of(b * block_len, block_len), block_len)
        total = own_ref[b]
        for ref in arrived_refs:
            total = total + ref[b].astype(jnp.float32)
        products = lax.dot_general(
            total.astype(jnp.bfloat16), emb_ref[docs], (((1,), (1,)), ((), ())),
            preferred_element_type=jnp.float32,
        )
        if held is not None:
            products = products + held[:, docs]
        out_ref[:, docs] = products.astype(out_ref.dtype)
        return carry

    lax.fori_loop(0, blocks, step, 0, unroll=UNROLL)


def body(embeddings, quality, probes, neighbors):
    nrow, ncol = lax.axis_size("row"), lax.axis_size("col")
    me = lax.axis_index("row")
    blk_count, list_len = neighbors.shape
    docs, width = embeddings.shape
    nprobe = probes.shape[0]
    group = nprobe // (CORES * GROUPS)
    core = (lax.axis_index("col") % CORES).astype(jnp.int32).reshape(1)
    tiles = blk_count // TILE_BLOCKS
    reduce_bits = [1 << i for i in reversed(range(nrow.bit_length() - 1)) if 1 << i not in (SIDE, NEXT)]
    dests = [0]
    for m in reversed(reduce_bits):
        dests = [d | m for d in dests] + dests
    shards = (0, NEXT, SIDE, NEXT | SIDE)

    def table_ids(lists):
        flat = lists.reshape(-1)
        apart = (flat // blk_count) ^ me
        place = flat % blk_count
        for i, shard in enumerate(shards):
            place = jnp.where(apart == shard, i * blk_count + flat % blk_count, place)
        return jnp.where((apart & ~(NEXT | SIDE)) == 0, place, len(shards) * blk_count)

    qrow = quality[None, :]
    shard_shape = (blk_count, group, width)
    shard_out = jax.ShapeDtypeStruct(shard_shape, jnp.bfloat16)
    vec_out = jax.ShapeDtypeStruct((nprobe, docs), jnp.float32)

    def first_sums():
        return pl.pallas_call(
            first_sums_kernel,
            in_specs=[SMEM] + [HBM] * 3,
            out_specs=[VMEM] * (CORES * GROUPS),
            out_shape=[shard_out] * (CORES * GROUPS),
            scratch_shapes=[
                pltpu.VMEM((nprobe, docs), jnp.float32),
                pltpu.VMEM((1, docs), jnp.float32),
                pltpu.VMEM((tiles, docs // tiles, width), jnp.bfloat16),
                pltpu.SemaphoreType.DMA((tiles + 1 + CORES * GROUPS,)),
            ],
            compiler_params=params(),
        )(core, *(pltpu.with_memory_space_constraint(v, pltpu.HBM) for v in (probes, qrow, embeddings)))

    def hold(value):
        return pl.pallas_call(
            hold_kernel,
            in_specs=[ANY],
            out_specs=VMEM,
            out_shape=jax.ShapeDtypeStruct(value.shape, value.dtype),
            scratch_shapes=[pltpu.SemaphoreType.DMA],
            compiler_params=params(),
        )(value)

    def next_sums(c, p, pair):
        return pl.pallas_call(
            functools.partial(next_sums_kernel, c),
            in_specs=[SMEM] + [VMEM] * 5,
            out_specs=VMEM,
            out_shape=shard_out,
            compiler_params=params(),
        )(core, *pair, probes, qrow, embs[p])

    def fill(c, held, pairs, before=()):
        held = [] if held is None else [held]
        values = [v for pair in (*pairs, *before) for v in pair]
        return pl.pallas_call(
            functools.partial(fill_kernel, c, bool(before)),
            in_specs=[SMEM] + [VMEM] * (2 + len(values)) + [ANY] * len(held),
            out_specs=HBM,
            out_shape=vec_out,
            input_output_aliases={3 + len(values): 0} if held else {},
            scratch_shapes=[pltpu.VMEM((CORES, group, docs), jnp.float32), pltpu.SemaphoreType.DMA((CORES, 4))],
            compiler_params=params(),
        )(core, probes, qrow, *values, *held)

    def combine_far(ids, shards):
        rows_held = len(shards) * blk_count + 1
        return pl.pallas_call(
            table_kernel,
            in_specs=[SMEM] + [VMEM] * len(shards),
            out_specs=[VMEM] * 2,
            out_shape=[shard_out, jax.ShapeDtypeStruct((rows_held, group, width), jnp.bfloat16)],
            scratch_shapes=[pltpu.SemaphoreType.DMA((len(shards),))],
            compiler_params=params(),
        )(ids, *shards)

    def combine(ids, tables, dtype):
        return pl.pallas_call(
            lookup_kernel,
            in_specs=[SMEM] + [VMEM] * len(tables),
            out_specs=[VMEM] * len(tables),
            out_shape=[jax.ShapeDtypeStruct(shard_shape, dtype)] * len(tables),
            compiler_params=params(),
        )(ids, *tables)

    def expand(p, own, arrived, held):
        values = [own, *arrived] + ([held] if p else [])
        return pl.pallas_call(
            expand_kernel,
            in_specs=[VMEM] * (len(values) + 1),
            out_specs=VMEM,
            out_shape=jax.ShapeDtypeStruct((group, docs), jnp.bfloat16 if p + 1 == PARTS else jnp.float32),
            compiler_params=params(),
        )(*values, embs[p])

    def reduce(outgoing):
        arrived = []
        for m in reduce_bits:
            taken = {d ^ m: swap(outgoing.pop(d), "row", nrow, m) for d in list(outgoing) if d & m}
            for d, value in taken.items():
                if d:
                    outgoing[d] = add_bf16(outgoing[d], value)
                else:
                    arrived.append(value)
        return arrived

    token = []

    def take(*values):
        if token:
            values = lax.optimization_barrier(values + (token.pop(),))[:-1]
        return values

    lists = {d: swap(neighbors, "row", nrow, d) if d else neighbors for d in dests}
    first = second = None
    embs = [embeddings, swap(embeddings, "col", ncol, 1)]
    gathered = [[None] * PARTS for _ in range(GROUPS)]
    tables = [[None] * PARTS for _ in range(GROUPS)]
    own = [[None] * PARTS for _ in range(GROUPS)]
    arrived = [[None] * PARTS for _ in range(GROUPS)]
    products = [None] * GROUPS
    pairs = [None] * GROUPS
    before = [None] * GROUPS

    def start_swaps(c, p, value):
        gathered[c][p] = {0: value}
        for m in (NEXT, SIDE):
            gathered[c][p][m] = swap(value, "row", nrow, m)

    def share(c):
        (mine, other), theirs = pairs[c]
        pairs[c] = (take(mine, other), (theirs[0], swap(other, "col", ncol, 1)))

    for word in (word for line in ORDER for word in line.split()):
        c, step, p = ord(word[0]) - ord("A"), word[1], int(word[2:] or 0) - 1
        if step == "l":
            taken = take(*(lists[d] for d in dests))
            ids = dict(zip(dests, lax.optimization_barrier(tuple(table_ids(v) for v in taken))))
            token.append(ids[0])
        elif step == "s":
            if pairs[c] is None:
                sums = first_sums()
                token.append(sums[0])
                for i in range(GROUPS):
                    start_swaps(i, 0, sums[i])
                late = [swap(v, "col", ncol, 1) for v in sums[GROUPS:]]
            else:
                if p == 0:
                    share(c)
                    before[c] = pairs[c]
                    pair = pairs[c][0]
                else:
                    pair = take(*pairs[c][0])
                value = next_sums(c, p, pair)
                token.append(value)
                start_swaps(c, p, value)
        elif step == "m":
            (value,) = take(late[c])
            token.append(value)
            start_swaps(c, 1, value)
        elif step == "k":
            embs[1] = hold(*take(embs[1]))
            token.append(embs[1])
        elif step in "fg":
            held = gathered[c][p]
            if step == "g":
                held[NEXT], held[SIDE] = take(held[NEXT], held[SIDE])
            else:
                (held[NEXT],) = take(held[NEXT])
            held[NEXT | SIDE] = swap(held[NEXT], "row", nrow, SIDE)
            token.append(held[NEXT])
        elif step == "o":
            held = take(*(gathered[c][p][m] for m in shards))
            outgoing = {}
            for d in dests[:-1]:
                if outgoing:
                    outgoing[d] = combine(ids[d], [tables[c][p]], jnp.bfloat16)[0]
                else:
                    outgoing[d], tables[c][p] = combine_far(ids[d], held)
            token.append(outgoing[dests[-2]])
            arrived[c][p] = reduce(outgoing)
        elif step == "w":
            tables[c] = list(take(*tables[c]))
            own[c] = combine(ids[0], tables[c], jnp.float32)
            token.append(own[c][0])
        elif step == "z":
            arrived[c][p] = take(*arrived[c][p])
            token.append(arrived[c][p][-1])
        elif step == "e":
            here, *later = take(own[c][p], *arrived[c][p])
            value = expand(p, here, later, products[c])
            products[c] = value
            token.append(value)
            if p + 1 == PARTS:
                other = swap(value, "col", ncol, CORES)
                for i in range(2, ncol.bit_length() - 1):
                    value = add_bf16(value, other)
                    other = swap(value, "col", ncol, 1 << i)
                pairs[c] = ((value, other), (swap(value, "col", ncol, 1),))
        elif step == "p":
            theirs = take(*before[c][1])
            before[c] = (before[c][0], theirs)
            first = fill(c, first, before[c])
            token.append(first)
        elif step == "r":
            share(c)
            token.append(pairs[c][0][0])
        else:
            theirs = take(*pairs[c][1])
            second = fill(c, second, (pairs[c][0], theirs), before[c])
            token.append(second)
    return first, second


def solution(mesh):
    placed = (P("row", "col"), P("row"), P(None, "row"), P("row", None))
    return jax.shard_map(
        body,
        mesh=mesh,
        in_specs=placed,
        out_specs=(P(None, "row"), P(None, "row")),
        check_vma=False,
    )
```
